128 devices in a mesh: gy: 8 (over z, core), gz: 16 (over y, x).
Axes of the slice: x: 4, y: 4, z: 4, core: 2. Of those that a mesh axis runs over, the one named last changes fastest.
Arguments:
- populations: float32 [19, 4, 256, 2048], P(None, None, 'gy', 'gz'), may hold values from 0.5 to 1.5
- solid_mask: int32 [4, 256, 2048], P(None, 'gy', 'gz'), may hold values from 0 to 1, as said below
- centers: int32 [3, 512], P(None, ('gy', 'gz')), may hold values from 0 to 2047, as said below
- tile_lists: int32 [2048, 4], P(('gy', 'gz')), may hold values from -15 to 126, as said below
- sphere_state: float32 [8, 512], P(None, ('gy', 'gz')), may hold values from -0.2 to 2.5, as said below
- destination: int32 [512], P(('gy', 'gz')), may hold values from 0 to 511, as said below
- relax_rates: float32 [19], replicated, may hold values from 0.6 to 1.9
Outputs:
- populations_next: float32 [19, 4, 256, 2048], P(None, None, 'gy', 'gz')
- forces: float32 [6, 512], P(None, ('gy', 'gz'))
- state_next: float32 [8, 512], P(None, ('gy', 'gz'))
The draws below stay inside these ranges and needn't reach their ends.
Inputs may be any that keep to these rules, and one draw needn't show every extreme that they name: `solid_mask`: 1 marks a solid cell, 0 a fluid one; every cell within distance 6 of a sphere's center (wrapping in y and z) is solid. `centers`: row 0 is x, rows 1 and 2 are global y and z. Sphere g belongs to device g // 4 (devices numbered with gz fastest), whose 32 rows and 128 columns contain its y and z; x lies from 0 to 3. Of one device's spheres at most 2 have local y below 7, at most 2 have local y at least 25, and likewise in z with 128; each of these four counts is exactly 2 on some device. `tile_lists`: A device's 8 * 2 rows form 8 blocks of 2 rows, one for each offset (dy, dz) in the order (-1,-1), (-1,0), (-1,1), (0,-1), (0,1), (1,-1), (1,0), (1,1), offsets wrapping. Block (dy, dz) names, in rising slot order, exactly those spheres of the device at that offset whose local y is below 7 if dy = 1 or at least 25 if dy = -1, and likewise in z for dz; columns: the sphere's slot on its device, the tile's first row and column in this device's local coordinates (center minus 16 / 2 plus dy * 32 and dz * 128), the center's x. Unused rows are -1, 0, 0, 0 and come last in a block. `sphere_state`: rows 0 to 2 a sphere's velocity and rows 3 to 5 its angular velocity, each from -0.2 to 0.2; row 6 the fluid density over the sphere's density, from 0.125 to 0.67; row 7 the reciprocal of the sphere's gyration factor k (moment of inertia k m * 6^2), from 1.5 to 2.5. `destination`: A permutation of the sphere slots; each sphere's new slot lies on its own device or on one of the 8 devices whose gy and gz indices differ by -1, 0 or 1, with wrap.
All inputs are finite; a program needn't handle non-finite values.
Results may differ from the reference program's by a relative error of at most 0.0003.
Values sent between devices are 32-bit elements; how exact they have to be, the bound alone decides.
No kernel may reach another device: no remote copies, remote signals or barrier semaphores. Data moves between devices by JAX's collectives and lax.ppermute only.
A program may use at most 128 MiB of HBM per device.

```python
import math
import jax
import jax.numpy as jnp
import numpy as np
from jax import lax

X = 4
CY = 32
CZ = 128
SLOTS = 4
TILE = 16
RADIUS = 6
CAP = 2
NY = 256
NZ = 2048
SPH = 512
N_GY = 8
N_GZ = 16


DIRECTIONS = ((-1, -1), (-1, 0), (-1, 1), (0, -1), (0, 1), (1, -1), (1, 0), (1, 1))


NEIGHBOURHOOD = ((0, 0), (-1, -1), (-1, 0), (-1, 1), (0, -1), (0, 1), (1, -1), (1, 0), (1, 1))


def sphere_layout(key):
    grid_y = NY // CY
    grid_z = NZ // CZ
    devices = grid_y * grid_z
    subkeys = jax.random.split(jax.random.fold_in(key, 31), 17)
    reach = RADIUS + 1

    def banded(key_list, extent):
        shuffles = jax.vmap(lambda subkey: jax.random.permutation(subkey, SLOTS))(jax.random.split(key_list[0], devices))
        slot_rank = jnp.argsort(shuffles, axis=1).astype(jnp.int32)
        device_ids = jnp.arange(devices)
        low_count = jax.random.randint(key_list[1], (devices,), 0, CAP + 1)
        low_count = jnp.where(device_ids == jax.random.randint(key_list[2], (), 0, devices), CAP, low_count)
        high_count = jax.random.randint(key_list[3], (devices,), 0, CAP + 1)
        high_count = jnp.where(device_ids == jax.random.randint(key_list[4], (), 0, devices), CAP, high_count)
        low_band = slot_rank < low_count[:, None]
        high_band = (slot_rank >= low_count[:, None]) & (slot_rank < (low_count + high_count)[:, None])
        low_place = jax.random.randint(key_list[5], (devices, SLOTS), 0, reach)
        middle_place = jax.random.randint(key_list[6], (devices, SLOTS), reach, extent - reach)
        high_place = jax.random.randint(key_list[7], (devices, SLOTS), extent - reach, extent)
        placed = jnp.where(low_band, low_place, jnp.where(high_band, high_place, middle_place))
        return (placed, low_band, high_band)
    local_y, low_y, high_y = banded(subkeys[0:8], CY)
    local_z, low_z, high_z = banded(subkeys[8:16], CZ)
    center_x = jax.random.randint(subkeys[16], (devices, SLOTS), X // 2 - 2, X // 2 + 2)
    return (local_y, local_z, center_x, low_y, high_y, low_z, high_z)


def draw_centers(key, part):
    grid_z = NZ // CZ
    local_y, local_z, center_x, low_y, high_y, low_z, high_z = sphere_layout(key)
    device_ids = jnp.arange(local_y.shape[0])[:, None]
    global_y = device_ids // grid_z * CY + local_y
    global_z = device_ids % grid_z * CZ + local_z
    return jnp.stack([center_x, global_y, global_z]).reshape(3, SPH).astype(jnp.int32)


def draw_tile_lists(key, part):
    grid_y = NY // CY
    grid_z = NZ // CZ
    local_y, local_z, center_x, low_y, high_y, low_z, high_z = sphere_layout(key)
    devices = local_y.shape[0]
    device_ids = jnp.arange(devices)
    blocks = []
    for offset in DIRECTIONS:
        owner = (device_ids // grid_z + offset[0]) % grid_y * grid_z + (device_ids % grid_z + offset[1]) % grid_z
        condition = jnp.ones((devices, SLOTS), dtype=bool)
        if offset[0] == 1:
            condition = condition & low_y[owner]
        if offset[0] == -1:
            condition = condition & high_y[owner]
        if offset[1] == 1:
            condition = condition & low_z[owner]
        if offset[1] == -1:
            condition = condition & high_z[owner]
        slot_rank = jnp.cumsum(condition.astype(jnp.int32), axis=1) - 1
        chosen = condition[:, None, :] & (slot_rank[:, None, :] == jnp.arange(CAP)[None, :, None])
        present = jnp.any(chosen, axis=2)
        picked = chosen.astype(jnp.int32)
        slot_column = jnp.sum(picked * jnp.arange(SLOTS)[None, None, :], axis=2)
        anchor_y = jnp.sum(picked * local_y[owner][:, None, :], axis=2) - TILE // 2 + offset[0] * CY
        anchor_z = jnp.sum(picked * local_z[owner][:, None, :], axis=2) - TILE // 2 + offset[1] * CZ
        centre_x = jnp.sum(picked * center_x[owner][:, None, :], axis=2)
        blocks.append(jnp.stack([jnp.where(present, slot_column, -1), jnp.where(present, anchor_y, 0), jnp.where(present, anchor_z, 0), jnp.where(present, centre_x, 0)], axis=2))
    return jnp.stack(blocks, axis=1).reshape(devices * 8 * CAP, 4).astype(jnp.int32)


def draw_solid_mask(key, part):
    grid_y = NY // CY
    grid_z = NZ // CZ
    local_y, local_z, center_x, low_y, high_y, low_z, high_z = sphere_layout(key)
    devices = local_y.shape[0]
    plane_grid = lax.broadcasted_iota(jnp.int32, (X, CY, CZ), 0)
    row_grid = lax.broadcasted_iota(jnp.int32, (X, CY, CZ), 1)
    column_grid = lax.broadcasted_iota(jnp.int32, (X, CY, CZ), 2)

    def one_device(device):
        solid_cells = jnp.zeros((X, CY, CZ), dtype=bool)
        for offset in NEIGHBOURHOOD:
            owner = (device // grid_z + offset[0]) % grid_y * grid_z + (device % grid_z + offset[1]) % grid_z
            relative_y = local_y[owner] + offset[0] * CY
            relative_z = local_z[owner] + offset[1] * CZ
            relative_x = center_x[owner]
            distance = (plane_grid[None] - relative_x[:, None, None, None]) ** 2 + (row_grid[None] - relative_y[:, None, None, None]) ** 2 + (column_grid[None] - relative_z[:, None, None, None]) ** 2
            solid_cells = solid_cells | jnp.any(distance <= RADIUS * RADIUS, axis=0)
        return solid_cells
    shells = lax.map(one_device, jnp.arange(devices))
    lattice = shells.reshape(grid_y, grid_z, X, CY, CZ).transpose(2, 0, 3, 1, 4).reshape(X, NY, NZ)
    scattered = jax.random.randint(jax.random.fold_in(key, 77), (X, NY, NZ), 0, 32) == 0
    return (lattice | scattered).astype(jnp.int32)


def draw_destination(key, part):
    grid_y = NY // CY
    grid_z = NZ // CZ
    devices = grid_y * grid_z
    subkeys = jax.random.split(jax.random.fold_in(key, 47), 3)
    shift_z = jax.random.randint(subkeys[0], (SLOTS, grid_y), -1, 2)
    shift_y = jax.random.randint(subkeys[1], (SLOTS, grid_z), -1, 2)
    shuffles = jax.vmap(lambda subkey: jax.random.permutation(subkey, SLOTS))(jax.random.split(subkeys[2], devices))
    device_ids = jnp.arange(devices)[:, None]
    slot_ids = jnp.arange(SLOTS)[None, :]
    row_index = device_ids // grid_z
    column_index = device_ids % grid_z
    new_z = (column_index + shift_z[slot_ids, row_index]) % grid_z
    new_y = (row_index + shift_y[slot_ids, new_z]) % grid_y
    new_device = new_y * grid_z + new_z
    new_slot = shuffles[new_device, slot_ids]
    return (new_device * SLOTS + new_slot).reshape(SPH).astype(jnp.int32)


def draw_sphere_state(key, part):
    subkeys = jax.random.split(jax.random.fold_in(key, 53), 3)
    motion = jax.random.uniform(subkeys[0], (6, SPH), dtype=jnp.float32, minval=-0.2, maxval=0.2)
    ratio = jnp.exp(jax.random.uniform(subkeys[1], (SPH,), dtype=jnp.float32, minval=math.log(1.5), maxval=math.log(8.0)))
    density_share = 1.0 / ratio
    gyration_inverse = jax.random.uniform(subkeys[2], (SPH,), dtype=jnp.float32, minval=1.5, maxval=2.5)
    return jnp.concatenate([motion, density_share[None], gyration_inverse[None]], axis=0).astype(jnp.float32)


def steps_of(own_key, shape, shards, smallest, largest):
    level = 1.0
    for position, parts in shards:
        steps = jax.random.uniform(jax.random.fold_in(jax.random.fold_in(own_key, 6), position), (parts,), jnp.float32, smallest / len(shards), largest / len(shards))
        level = level * jnp.repeat(jnp.exp(steps), shape[position] // parts).reshape((-1,) + (1,) * (len(shape) - 1 - position))
    return level


def setup_inputs(seed: int = 0) -> dict:
    seeds = jax.random.split(jax.random.key(seed), 8)
    return {
        "populations": jnp.clip(0.5 + 1.0 * jax.random.uniform(seeds[0], (19, X, NY, NZ), jnp.float32) ** steps_of(seeds[0], (19, X, NY, NZ), ((2, 8), (3, 16)), -0.2, 0.2), 0.5, 1.5),
        "solid_mask": draw_solid_mask(jax.random.fold_in(seeds[7], 71), 0),
        "centers": draw_centers(jax.random.fold_in(seeds[7], 71), 0),
        "tile_lists": draw_tile_lists(jax.random.fold_in(seeds[7], 71), 0),
        "sphere_state": draw_sphere_state(jax.random.fold_in(seeds[7], 71), 0),
        "destination": draw_destination(jax.random.fold_in(seeds[7], 71), 0),
        "relax_rates": jnp.clip(jax.random.uniform(seeds[6], (19,), jnp.float32, 0.6, 1.9), 0.6, 1.9),
    }


VELOCITIES = ((0, 0, 0), (1, 0, 0), (-1, 0, 0), (0, 1, 0), (0, -1, 0), (0, 0, 1), (0, 0, -1), (1, 1, 0), (-1, -1, 0), (1, -1, 0), (-1, 1, 0), (1, 0, 1), (-1, 0, -1), (1, 0, -1), (-1, 0, 1), (0, 1, 1), (0, -1, -1), (0, 1, -1), (0, -1, 1))
OPPOSITE = (0, 2, 1, 4, 3, 6, 5, 8, 7, 10, 9, 12, 11, 14, 13, 16, 15, 18, 17)
WEIGHTS = (1.0 / 3.0,) + (1.0 / 18.0,) * 6 + (1.0 / 36.0,) * 12
EXPONENTS = ((0, 0, 0), (1, 0, 0), (0, 1, 0), (0, 0, 1), (2, 0, 0), (0, 2, 0), (0, 0, 2), (1, 1, 0), (1, 0, 1), (0, 1, 1), (1, 2, 0), (1, 0, 2), (2, 1, 0), (0, 1, 2), (2, 0, 1), (0, 2, 1), (2, 2, 0), (2, 0, 2), (0, 2, 2))
DIRECTIONS = ((-1, -1), (-1, 0), (-1, 1), (0, -1), (0, 1), (1, -1), (1, 0), (1, 1))

def moment_basis():
    velocity = np.array(VELOCITIES, dtype=np.float32)
    moment_rows = []
    for powers_entry in EXPONENTS:
        vector = velocity[:, 0] ** powers_entry[0] * velocity[:, 1] ** powers_entry[1] * velocity[:, 2] ** powers_entry[2]
        for earlier in moment_rows:
            vector = vector - np.dot(earlier, vector) * earlier
        length = np.sqrt(np.dot(vector, vector))
        moment_rows.append(vector / length)
    return np.array(moment_rows, dtype=np.float32)

def relax_matrix(relax_rates):
    moment_rows = jnp.asarray(moment_basis())
    return jnp.dot(moment_rows.T * relax_rates[None, :], moment_rows, precision=lax.Precision.HIGHEST, preferred_element_type=jnp.float32)

def collide(flat_pops, relax_rates):
    velocity = jnp.asarray(np.array(VELOCITIES, dtype=np.float32))
    weight = jnp.asarray(np.array(WEIGHTS, dtype=np.float32))
    density = lax.optimization_barrier(jnp.sum(flat_pops, axis=0))
    momentum = jnp.dot(velocity.T, flat_pops, precision=lax.Precision.HIGHEST, preferred_element_type=jnp.float32)
    velocity_field = momentum / density[None, :]
    projected = jnp.dot(velocity, velocity_field, precision=lax.Precision.HIGHEST, preferred_element_type=jnp.float32)
    square = lax.optimization_barrier(jnp.sum(velocity_field * velocity_field, axis=0))
    equilibrium = weight[:, None] * density[None, :] * (1.0 + 3.0 * projected + 4.5 * projected * projected - 1.5 * square[None, :])
    return flat_pops - jnp.dot(relax_matrix(relax_rates), flat_pops - equilibrium, precision=lax.Precision.HIGHEST, preferred_element_type=jnp.float32)

def momentum_sums(tile, center_x):
    cell_count = tile.shape[1]
    planes = cell_count // (TILE * TILE)
    cell_index = jnp.arange(cell_count, dtype=jnp.int32)
    plane_index = cell_index // (TILE * TILE)
    offset_x = plane_index - center_x
    offset_y = cell_index // TILE % TILE - TILE // 2
    offset_z = cell_index % TILE - TILE // 2
    limit_sq = RADIUS * RADIUS
    inside = offset_x * offset_x + offset_y * offset_y + offset_z * offset_z <= limit_sq
    link_list = []
    for velocity in VELOCITIES:
        shift_x = offset_x + velocity[0]
        shift_y = offset_y + velocity[1]
        shift_z = offset_z + velocity[2]
        target = shift_x * shift_x + shift_y * shift_y + shift_z * shift_z <= limit_sq
        within = (plane_index + velocity[0] >= 0) & (plane_index + velocity[0] < planes)
        link_list.append(target & within & jnp.logical_not(inside))
    link_mask = jnp.stack(link_list).astype(tile.dtype)
    weighted = link_mask * tile
    link_total = lax.optimization_barrier(jnp.sum(weighted, axis=1))
    lever_arm = jnp.stack([offset_x, offset_y, offset_z]).astype(tile.dtype)
    moment = jnp.stack([lax.optimization_barrier(jnp.sum(weighted * lever_arm[axis_id][None, :], axis=1)) for axis_id in range(3)], axis=1)
    velocity_table = jnp.asarray(np.array(VELOCITIES, dtype=np.float32)).astype(tile.dtype)
    force_sum = 2.0 * lax.optimization_barrier(jnp.sum(link_total[:, None] * velocity_table, axis=0))
    torque = 2.0 * lax.optimization_barrier(jnp.sum(jnp.cross(moment, velocity_table), axis=0))
    return jnp.concatenate([force_sum, torque])

def stream(collided, populations, solid_mask):
    planes = collided.shape[1]
    solid_wall = jnp.pad(solid_mask, ((1, 1), (0, 0), (0, 0)), constant_values=1)
    framed = jnp.pad(collided, ((0, 0), (1, 1), (0, 0), (0, 0)))
    read = []
    for direction in range(19):
        velocity = VELOCITIES[direction]
        start_x = 1 - velocity[0]
        pulled = jnp.roll(framed[direction], (velocity[1], velocity[2]), axis=(1, 2))[start_x:start_x + planes]
        wall_flag = jnp.roll(solid_wall, (velocity[1], velocity[2]), axis=(1, 2))[start_x:start_x + planes]
        read.append(jnp.where(wall_flag > 0, collided[OPPOSITE[direction]], pulled))
    return jnp.where(solid_mask[None] > 0, populations, jnp.stack(read))

def cut_tile(padded_blocks, device, anchor_y, anchor_z):
    zero_index = jnp.zeros((), jnp.int32)
    window = lax.dynamic_slice(padded_blocks, (device.astype(jnp.int32), zero_index, zero_index, (anchor_y + TILE).astype(jnp.int32), (anchor_z + TILE).astype(jnp.int32)), (1, 19, X, TILE, TILE))
    return window.reshape(19, X * TILE * TILE)

def reference(populations, solid_mask, centers, tile_lists, sphere_state, destination, relax_rates):
    collided = collide(populations.reshape(19, -1), relax_rates).reshape(populations.shape)
    populations_next = stream(collided, populations, solid_mask)
    device_total = N_GY * N_GZ
    blocks_view = collided.reshape(19, X, N_GY, CY, N_GZ, CZ).transpose(2, 4, 0, 1, 3, 5)
    blocks_view = blocks_view.reshape(device_total, 19, X, CY, CZ)
    padded_blocks = jnp.pad(blocks_view, ((0, 0), (0, 0), (0, 0), (TILE, TILE), (TILE, TILE)))
    sphere_ids = jnp.arange(SPH, dtype=jnp.int32)
    owners = sphere_ids // SLOTS
    local_y = centers[1] - owners // N_GZ * CY
    local_z = centers[2] - owners % N_GZ * CZ
    own_tiles = lax.map(lambda packed: cut_tile(padded_blocks, packed[0], packed[1], packed[2]), (owners, local_y - TILE // 2, local_z - TILE // 2))
    listed = tile_lists.reshape(device_total, 8, CAP, 4)
    source = jnp.broadcast_to(jnp.arange(device_total, dtype=jnp.int32)[:, None, None], (device_total, 8, CAP))
    step_y = jnp.array([offset[0] for offset in DIRECTIONS], dtype=jnp.int32)[None, :, None]
    step_z = jnp.array([offset[1] for offset in DIRECTIONS], dtype=jnp.int32)[None, :, None]
    owner_device = (source // N_GZ + step_y) % N_GY * N_GZ + (source % N_GZ + step_z) % N_GZ
    slot_column = listed[..., 0]
    target = jnp.where(slot_column >= 0, owner_device * SLOTS + slot_column, SPH).astype(jnp.int32)
    listed_tiles = lax.map(lambda packed: cut_tile(padded_blocks, packed[0], packed[1], packed[2]), (source.reshape(-1), listed[..., 1].reshape(-1), listed[..., 2].reshape(-1)))
    assembled = own_tiles.at[target.reshape(-1)].add(listed_tiles, mode='drop')
    forces = lax.map(lambda packed: momentum_sums(packed[0], packed[1]), (assembled, centers[0])).T
    mass_factor = sphere_state[6:7] * (3.0 / (4.0 * math.pi * RADIUS * RADIUS * RADIUS))
    spin_factor = mass_factor * sphere_state[7:8] * (1.0 / (RADIUS * RADIUS))
    gained = jnp.concatenate([forces[0:3] * mass_factor, forces[3:6] * spin_factor, jnp.zeros((2, SPH), sphere_state.dtype)], axis=0)
    updated = sphere_state + gained
    state_next = jnp.zeros_like(sphere_state).at[:, destination].set(updated)
    return (populations_next, forces, state_next)
```

```python
import math

import jax
import jax.numpy as jnp
import numpy as np
from jax import lax
from jax.experimental import pallas as pl
from jax.experimental.pallas import tpu as pltpu
from jax.sharding import PartitionSpec as P

TILE = 16
RADIUS = 6
PLANES = 4
ROWS = 32
COLS = 128
SLOTS = 4
GROUPS = PLANES * ROWS // 8

VELOCITIES = (
    (0, 0, 0),
    (1, 0, 0),
    (-1, 0, 0),
    (0, 1, 0),
    (0, -1, 0),
    (0, 0, 1),
    (0, 0, -1),
    (1, 1, 0),
    (-1, -1, 0),
    (1, -1, 0),
    (-1, 1, 0),
    (1, 0, 1),
    (-1, 0, -1),
    (1, 0, -1),
    (-1, 0, 1),
    (0, 1, 1),
    (0, -1, -1),
    (0, 1, -1),
    (0, -1, 1),
)
OPPOSITE = (0, 2, 1, 4, 3, 6, 5, 8, 7, 10, 9, 12, 11, 14, 13, 16, 15, 18, 17)
EXPONENTS = (
    (0, 0, 0),
    (1, 0, 0),
    (0, 1, 0),
    (0, 0, 1),
    (2, 0, 0),
    (0, 2, 0),
    (0, 0, 2),
    (1, 1, 0),
    (1, 0, 1),
    (0, 1, 1),
    (1, 2, 0),
    (1, 0, 2),
    (2, 1, 0),
    (0, 1, 2),
    (2, 0, 1),
    (0, 2, 1),
    (2, 2, 0),
    (2, 0, 2),
    (0, 2, 2),
)
DIRECTIONS = ((-1, -1), (-1, 0), (-1, 1), (0, -1), (0, 1), (1, -1), (1, 0), (1, 1))

Z_UP = (5, 11, 14, 15, 18)
Z_DOWN = (6, 12, 13, 16, 17)
Y_UP = (3, 7, 10, 15, 17)
Y_DOWN = (4, 8, 9, 16, 18)
CLASS_MEMBER = (0, 1, 3, 5, 7, 11, 15)
EVEN_MOMENTS = (0, 4, 5, 6, 16, 17, 18)
ODD_MOMENTS = ((1, 10, 11), (2, 12, 13), (3, 14, 15))
ODD_CLASSES = ((1, 4, 5), (2, 4, 6), (3, 5, 6))
CROSS_MOMENTS = (7, 8, 9)
STATE_LANE = 64
DEST_LANE = 96
EDGE_ROWS = 24


def moment_basis():
    velocity = np.array(VELOCITIES, dtype=np.float64)
    moment_rows = []
    for a, b, e in EXPONENTS:
        vector = velocity[:, 0] ** a * velocity[:, 1] ** b * velocity[:, 2] ** e
        for earlier in moment_rows:
            vector = vector - np.dot(earlier, vector) * earlier
        moment_rows.append(vector / np.sqrt(np.dot(vector, vector)))
    return np.array(moment_rows)


BASIS = moment_basis()


def store_coefficients(rates, coef):
    splat = [jnp.full((8, COLS), rates[k], jnp.float32) for k in range(19)]
    at = 0
    for a in range(7):
        for b in range(a, 7):
            total = None
            for k in EVEN_MOMENTS:
                c = float(BASIS[k, CLASS_MEMBER[a]] * BASIS[k, CLASS_MEMBER[b]])
                if abs(c) > 1e-12:
                    total = c * splat[k] if total is None else total + c * splat[k]
            coef[at] = total
            at += 1
    for axis in range(3):
        for a in range(3):
            for b in range(a, 3):
                total = None
                for k in ODD_MOMENTS[axis]:
                    c = float(
                        BASIS[k, CLASS_MEMBER[ODD_CLASSES[axis][a]]]
                        * BASIS[k, CLASS_MEMBER[ODD_CLASSES[axis][b]]]
                    )
                    if abs(c) > 1e-12:
                        total = c * splat[k] if total is None else total + c * splat[k]
                coef[at] = total
                at += 1
    for axis in range(3):
        c = float(BASIS[CROSS_MOMENTS[axis], CLASS_MEMBER[4 + axis]] ** 2)
        coef[at] = c * splat[CROSS_MOMENTS[axis]]
        at += 1


N_COEF = 28 + 18 + 3


def collide(f, coef):
    even_at = {}
    at = 0
    for a in range(7):
        for b in range(a, 7):
            even_at[a, b] = even_at[b, a] = at
            at += 1
    odd_at = []
    for _ in range(3):
        table = {}
        for a in range(3):
            for b in range(a, 3):
                table[a, b] = table[b, a] = at
                at += 1
        odd_at.append(table)
    cross_at = at

    def split(i):
        ab, amb = f[i] + f[i + 1], f[i] - f[i + 1]
        cd, cmd = f[i + 2] + f[i + 3], f[i + 2] - f[i + 3]
        return ab + cd, ab - cd, amb + cmd, amb - cmd

    s_xy, q_xy, xy_x, xy_y = split(7)
    s_xz, q_xz, xz_x, xz_z = split(11)
    s_yz, q_yz, yz_y, yz_z = split(15)
    s_x, s_y, s_z = f[1] + f[2], f[3] + f[4], f[5] + f[6]
    d_x, d_y, d_z = f[1] - f[2], f[3] - f[4], f[5] - f[6]
    rho = ((f[0] + s_x) + (s_y + s_z)) + ((s_xy + s_xz) + s_yz)
    j_x = d_x + (xy_x + xz_x)
    j_y = d_y + (xy_y + yz_y)
    j_z = d_z + (xz_z + yz_z)
    inverse = 1.0 / rho
    u_x, u_y, u_z = j_x * inverse, j_y * inverse, j_z * inverse
    e_x, e_y, e_z = j_x * u_x, j_y * u_y, j_z * u_z
    base = (rho - 1.5 * ((e_x + e_y) + e_z)) * (1.0 / 9.0)
    h_x, h_y, h_z = 0.5 * e_x, 0.5 * e_y, 0.5 * e_z
    even = (
        f[0] - 3.0 * base,
        s_x - (base + h_x),
        s_y - (base + h_y),
        s_z - (base + h_z),
        s_xy - (base + (h_x + h_y)),
        s_xz - (base + (h_x + h_z)),
        s_yz - (base + (h_y + h_z)),
    )
    third = 1.0 / 3.0
    t_x, t_y, t_z = third * j_x, third * j_y, third * j_z
    odd = (
        (d_x - t_x, xy_x - t_x, xz_x - t_x),
        (d_y - t_y, xy_y - t_y, yz_y - t_y),
        (d_z - t_z, xz_z - t_z, yz_z - t_z),
    )
    cross = (
        (q_xy - j_x * u_y) * coef[cross_at],
        (q_xz - j_x * u_z) * coef[cross_at + 1],
        (q_yz - j_y * u_z) * coef[cross_at + 2],
    )

    def apply(vector, table, n):
        out = []
        for a in range(n):
            terms = [coef[table[a, b]] * vector[b] for b in range(n)]
            while len(terms) > 1:
                terms = [
                    terms[i] + terms[i + 1] if i + 1 < len(terms) else terms[i]
                    for i in range(0, len(terms), 2)
                ]
            out.append(terms[0])
        return out

    ev = apply(even, even_at, 7)
    ox, oy, oz = (apply(odd[axis], odd_at[axis], 3) for axis in range(3))
    new = [f[0] - ev[0]]
    for axis, o in enumerate((ox, oy, oz)):
        i = 1 + 2 * axis
        new += [f[i] - (ev[1 + axis] + o[0]), f[i + 1] - (ev[1 + axis] - o[0])]
    for axis, (a, b) in enumerate(((ox[1], oy[1]), (ox[2], oz[1]), (oy[2], oz[2]))):
        i = 7 + 4 * axis
        plus, minus = ev[4 + axis] + cross[axis], ev[4 + axis] - cross[axis]
        both, differ = a + b, a - b
        new += [
            f[i] - (plus + both),
            f[i + 1] - (plus - both),
            f[i + 2] - (minus + differ),
            f[i + 3] - (minus - differ),
        ]
    return new


def sphere_partial(coll, center_x, center_y, center_z, row_f, lane_f):
    first = jnp.maximum(lax.shift_right_arithmetic(center_y - (RADIUS + 1), 3), 0)
    last = jnp.minimum(lax.shift_right_arithmetic(center_y + (RADIUS + 1), 3), ROWS // 8 - 1)
    x_f = center_x.astype(jnp.float32)
    r_z = lane_f - center_z.astype(jnp.float32)
    z_sq = r_z * r_z
    zero = jnp.zeros((8, COLS), jnp.float32)

    def row_tile(tile, carry):
        f_x, f_y, f_z, t_x, t_y, t_z = carry
        r_y = row_f + (tile * 8 - center_y).astype(jnp.float32)
        yz_sq = r_y * r_y + z_sq
        p_x, p_y, p_z, x_py, x_pz = zero, zero, zero, zero, zero
        y_plus_z, y_minus_z = r_y + r_z, r_y - r_z
        for t in range(PLANES):
            r_x = t - x_f
            dist = yz_sq + r_x * r_x
            outside = dist > float(RADIUS * RADIUS)
            half = jnp.where(outside, (RADIUS * RADIUS - 1.0) * 0.5 - 0.5 * dist, -1e9)
            half_2 = half - 0.5

            def linked(i, along, limit):
                up, down = VELOCITIES[i][0], VELOCITIES[i + 1][0]
                total = None
                if 0 <= t + up < PLANES:
                    total = jnp.where(along <= limit, coll[i, t * 4 + tile], 0.0)
                if 0 <= t + down < PLANES:
                    back = jnp.where(-along <= limit, coll[i + 1, t * 4 + tile], 0.0)
                    total = -back if total is None else total - back
                return total

            l_x = linked(1, r_x, half)
            l_y = linked(3, r_y, half)
            l_z = linked(5, r_z, half)
            l_xy = linked(7, r_y + r_x, half_2)
            l_xmy = linked(9, r_x - r_y, half_2)
            l_xz = linked(11, r_z + r_x, half_2)
            l_xmz = linked(13, r_x - r_z, half_2)
            l_yz = linked(15, y_plus_z, half_2)
            l_ymz = linked(17, y_minus_z, half_2)
            m_x = l_x + ((l_xy + l_xmy) + (l_xz + l_xmz))
            m_y = l_y + ((l_xy - l_xmy) + (l_yz + l_ymz))
            m_z = l_z + ((l_xz - l_xmz) + (l_yz - l_ymz))
            p_x, p_y, p_z = p_x + m_x, p_y + m_y, p_z + m_z
            x_py, x_pz = x_py + r_x * m_y, x_pz + r_x * m_z
        return (
            f_x + p_x,
            f_y + p_y,
            f_z + p_z,
            t_x + (r_y * p_z - r_z * p_y),
            t_y + (r_z * p_x - x_pz),
            t_z + (x_py - r_y * p_x),
        )

    sums = lax.fori_loop(first, last + 1, row_tile, (zero,) * 6)
    packed = zero
    for j in range(6):
        packed = jnp.where(row_f == float(j), jnp.sum(sums[j], axis=0, keepdims=True), packed)
    return packed


def collide_kernel(
    pops,
    mask,
    state,
    centers,
    lists,
    destination,
    rates,
    held,
    up_z,
    down_z,
    info,
    up_y,
    down_y,
    coll,
    coef,
    turn,
    partial,
):
    lane = lax.broadcasted_iota(jnp.int32, (8, COLS), 1)
    lane_f = lane.astype(jnp.float32)
    row_f = lax.broadcasted_iota(jnp.int32, (8, COLS), 0).astype(jnp.float32)
    store_coefficients(rates, coef)

    def group(g, _):
        f = [pops[i, g] for i in range(19)]
        solid = mask[g] > 0
        flag = solid.astype(jnp.float32)
        new = collide(f, coef)
        edge = jnp.zeros((8, COLS), jnp.float32)
        for i in range(19):
            coll[i, g] = new[i]
            held[i, g] = jnp.where(solid, f[i], new[i])
        for k, values in enumerate([new[i] for i in Z_UP] + [flag]):
            edge = jnp.where(lane == k, pltpu.roll(values, k + 1, 1), edge)
        for k, values in enumerate([new[i] for i in Z_DOWN] + [flag]):
            edge = jnp.where(lane == 8 + k, pltpu.roll(values, 8 + k, 1), edge)
        turn[pl.ds(pl.multiple_of(g * 8, 8), 8), :] = edge
        return 0

    lax.fori_loop(0, GROUPS, group, 0)

    turned = turn[...].T
    up_z[0:8, :] = turned[0:8, :]
    down_z[0:8, :] = turned[8:16, :]
    for t in range(PLANES):
        for d in range(5):
            up_y[d * 4 + t : d * 4 + t + 1, :] = coll[Y_UP[d], t * 4 + 3, 7:8, :]
            down_y[d * 4 + t : d * 4 + t + 1, :] = coll[Y_DOWN[d], t * 4, 0:1, :]
        up_y[20 + t : 21 + t, :] = mask[t * 4 + 3, 7:8, :].astype(jnp.float32)
        down_y[20 + t : 21 + t, :] = mask[t * 4, 0:1, :].astype(jnp.float32)

    def own(s, _):
        partial[s] = sphere_partial(
            coll, centers[0, s], centers[1, s] & (ROWS - 1), centers[2, s] & (COLS - 1), row_f, lane_f
        )
        return 0

    lax.fori_loop(0, SLOTS, own, 0)

    def listed(r, _):
        partial[SLOTS + r] = jnp.zeros((8, COLS), jnp.float32)

        @pl.when(lists[r, 0] >= 0)
        def _():
            partial[SLOTS + r] = sphere_partial(
                coll, lists[r, 3], lists[r, 1] + TILE // 2, lists[r, 2] + TILE // 2, row_f, lane_f
            )

        return 0

    lax.fori_loop(0, 16, listed, 0)

    tile = jnp.zeros((8, COLS), jnp.float32)
    for s in range(SLOTS):
        total = 2.0 * jnp.sum(partial[s], axis=1, keepdims=True)
        tile = jnp.where(lane == 4 * SLOTS + s, total, tile)
        tile = jnp.where(lane == STATE_LANE + s, state[:, s : s + 1], tile)
        tile = jnp.where(lane == DEST_LANE + s, destination[s].astype(jnp.float32), tile)
    for r in range(16):
        offset = DIRECTIONS[r // 2]
        block = (offset[0] + 1) * 3 + offset[1] + 1
        total = 2.0 * jnp.sum(partial[SLOTS + r], axis=1, keepdims=True)
        slot = lists[r, 0]
        at = jnp.where(slot >= 0, block * SLOTS + slot, -1)
        tile = jnp.where(lane == at, total, tile)
    info[...] = tile
    up_z[8:16, :] = tile
    down_z[8:16, :] = tile


def update_kernel(
    held,
    mask,
    centers,
    info,
    west,
    east,
    west_2,
    east_2,
    south,
    north,
    south_2,
    north_2,
    out,
    forces,
    state_next,
    ext,
    turn,
):
    lane = lax.broadcasted_iota(jnp.int32, (8, COLS), 1)
    sub = lax.broadcasted_iota(jnp.int32, (8, COLS), 0)
    row = lane & (ROWS - 1)
    plane = lax.shift_right_logical(lane, 5)
    wall = jnp.inf

    def walled(ref, start):
        values = ref[start : start + 8, :]
        return jnp.where(values[5:6, :] > 0.5, wall, values)

    def side(here, below, above, shifts):
        total = here
        for k, (c_x, c_y) in enumerate(shifts):
            moved = here
            if c_y == 1:
                moved = jnp.where(row == 0, pltpu.roll(below, COLS - 31, 1), pltpu.roll(here, 1, 1))
            if c_y == -1:
                moved = jnp.where(
                    row == ROWS - 1, pltpu.roll(above, 31, 1), pltpu.roll(here, COLS - 1, 1)
                )
            if c_x == 1:
                moved = jnp.where(plane == 0, wall, pltpu.roll(here, 32, 1))
            if c_x == -1:
                moved = jnp.where(plane == PLANES - 1, wall, pltpu.roll(here, COLS - 32, 1))
            total = jnp.where(sub == k, moved, total)
        return total

    turn[...] = jnp.zeros((COLS, COLS), jnp.float32)
    turn[0:8, :] = side(
        walled(west, 0),
        walled(south, EDGE_ROWS),
        walled(north, EDGE_ROWS),
        [VELOCITIES[i][:2] for i in Z_UP],
    )
    turn[8:16, :] = side(
        walled(east, 0),
        walled(south, EDGE_ROWS + 16),
        walled(north, EDGE_ROWS + 16),
        [VELOCITIES[i][:2] for i in Z_DOWN],
    )
    turned = turn[...].T
    turn[...] = turned

    column = lax.broadcasted_iota(jnp.int32, (ROWS, COLS), 1)
    for t in range(PLANES):
        solid = mask[t] > 0
        for i in range(19):
            ext[i, t, 8 : 8 + ROWS, :] = jnp.where(solid, wall, held[i, t])
        flag_low = south[20 + t : 21 + t, :] > 0.5
        flag_high = north[20 + t : 21 + t, :] > 0.5
        for d in range(5):
            r = d * 4 + t
            ext[Y_UP[d], t, 7:8, :] = jnp.where(flag_low, wall, south[r : r + 1, :])
            ext[Y_DOWN[d], t, 8 + ROWS : 9 + ROWS, :] = jnp.where(flag_high, wall, north[r : r + 1, :])
    for t in range(PLANES):
        solid = mask[t] > 0
        for i in range(19):
            c_x, c_y, c_z = VELOCITIES[i]
            source = t - c_x
            if not 0 <= source < PLANES:
                out[i, t] = jnp.where(solid, held[i, t], held[OPPOSITE[i], t])
                continue
            pulled = ext[i, source, 8 - c_y : 8 - c_y + ROWS, :]
            if c_z == 1:
                k = Z_UP.index(i)
                pulled = jnp.where(
                    column == 0, turn[t * ROWS : (t + 1) * ROWS, k : k + 1], pltpu.roll(pulled, 1, 1)
                )
            if c_z == -1:
                k = 8 + Z_DOWN.index(i)
                pulled = jnp.where(
                    column == COLS - 1,
                    turn[t * ROWS : (t + 1) * ROWS, k : k + 1],
                    pltpu.roll(pulled, COLS - 1, 1),
                )
            fluid = jnp.where(pulled == wall, held[OPPOSITE[i], t], pulled)
            out[i, t] = jnp.where(solid, held[i, t], fluid)

    tiles = {(0, 0): info[...]}
    tiles[0, -1] = west[8:16, :]
    tiles[0, 1] = east[8:16, :]
    tiles[0, -2] = west_2[...]
    tiles[0, 2] = east_2[...]
    for a, ref in ((-1, south), (1, north)):
        tiles[a, -1] = ref[EDGE_ROWS + 8 : EDGE_ROWS + 16, :]
        tiles[a, 1] = ref[EDGE_ROWS + 24 : EDGE_ROWS + 32, :]
        tiles[a, 0] = ref[EDGE_ROWS + 32 : EDGE_ROWS + 40, :]
        tiles[a, -2] = ref[EDGE_ROWS + 40 : EDGE_ROWS + 48, :]
        tiles[a, 2] = ref[EDGE_ROWS + 48 : EDGE_ROWS + 56, :]
    for a, ref in ((-2, south_2), (2, north_2)):
        for k, b in enumerate((0, -1, 1, -2, 2)):
            tiles[a, b] = ref[k * 8 : k * 8 + 8, :]
    device = lax.shift_right_logical(centers[1, 0], 5) * 16 + lax.shift_right_logical(centers[2, 0], 7)
    own_lanes = lane < SLOTS
    picked = [jnp.zeros((8, COLS), jnp.float32) for _ in range(SLOTS)]
    for a in (-1, 0, 1):
        for b in (-1, 0, 1):
            force = jnp.zeros((8, COLS), jnp.float32)
            for e in (-1, 0, 1):
                for g in (-1, 0, 1):
                    block = (1 - e) * 3 + 1 - g
                    shift = (COLS - block * SLOTS) % COLS
                    part = tiles[a + e, b + g]
                    force = force + (pltpu.roll(part, shift, 1) if shift else part)
            if a == 0 and b == 0:
                forces[...] = force[0:6, 0:SLOTS]
            record = pltpu.roll(tiles[a, b], COLS - STATE_LANE, 1)
            target = pltpu.roll(tiles[a, b], COLS - DEST_LANE, 1)[0:1, :]
            mass = record[6:7, :] * (3.0 / (4.0 * math.pi * RADIUS * RADIUS * RADIUS))
            spin = mass * record[7:8, :] * (1.0 / (RADIUS * RADIUS))
            gain = jnp.where(sub < 3, force * mass, jnp.where(sub < 6, force * spin, 0.0))
            updated = record + gain
            for j in range(SLOTS):
                wanted = (device * SLOTS + j).astype(jnp.float32)
                picked[j] = picked[j] + jnp.where(own_lanes & (target == wanted), updated, 0.0)
    result = jnp.zeros((8, COLS), jnp.float32)
    for j in range(SLOTS):
        result = jnp.where(lane == j, jnp.sum(picked[j], axis=1, keepdims=True), result)
    state_next[...] = result[:, 0:SLOTS]


VMEM = pl.BlockSpec(memory_space=pltpu.VMEM)
SMEM = pl.BlockSpec(memory_space=pltpu.SMEM)


def passed_along(block, axis, distance):
    count = lax.axis_size(axis)
    return lax.ppermute(block, axis, [((i - distance) % count, i) for i in range(count)])


def f32(*shape):
    return jax.ShapeDtypeStruct(shape, jnp.float32)


def on_device(populations, solid_mask, centers, tile_lists, sphere_state, destination, relax_rates):
    held, up_z, down_z, info, up_y, down_y = pl.pallas_call(
        collide_kernel,
        out_shape=(
            f32(19, GROUPS, 8, COLS),
            f32(16, COLS),
            f32(16, COLS),
            f32(8, COLS),
            f32(EDGE_ROWS, COLS),
            f32(EDGE_ROWS, COLS),
        ),
        in_specs=[VMEM, VMEM, VMEM, SMEM, SMEM, SMEM, SMEM],
        out_specs=(VMEM,) * 6,
        scratch_shapes=[
            pltpu.VMEM((19, GROUPS, 8, COLS), jnp.float32),
            pltpu.VMEM((N_COEF, 8, COLS), jnp.float32),
            pltpu.VMEM((COLS, COLS), jnp.float32),
            pltpu.VMEM((20, 8, COLS), jnp.float32),
        ],
        compiler_params=pltpu.CompilerParams(vmem_limit_bytes=32 * 1024 * 1024),
        name="collide",
    )(
        populations.reshape(19, GROUPS, 8, COLS),
        solid_mask.reshape(GROUPS, 8, COLS),
        sphere_state,
        centers,
        tile_lists,
        destination,
        relax_rates,
    )
    west = passed_along(up_z, "gz", 1)
    east = passed_along(down_z, "gz", -1)
    west_2 = passed_along(info, "gz", 2)
    east_2 = passed_along(info, "gz", -2)
    shared = [west, east, info, west_2, east_2]
    south = passed_along(jnp.concatenate([up_y] + shared), "gy", 1)
    north = passed_along(jnp.concatenate([down_y] + shared), "gy", -1)
    far = jnp.concatenate([info, west[8:16], east[8:16], west_2, east_2])
    south_2 = passed_along(far, "gy", 2)
    north_2 = passed_along(far, "gy", -2)
    return pl.pallas_call(
        update_kernel,
        out_shape=(f32(19, PLANES, ROWS, COLS), f32(6, SLOTS), f32(8, SLOTS)),
        in_specs=[VMEM, VMEM, SMEM] + [VMEM] * 9,
        out_specs=(VMEM,) * 3,
        scratch_shapes=[
            pltpu.VMEM((19, PLANES, ROWS + 16, COLS), jnp.float32),
            pltpu.VMEM((COLS, COLS), jnp.float32),
        ],
        compiler_params=pltpu.CompilerParams(vmem_limit_bytes=32 * 1024 * 1024),
        name="update",
    )(
        held.reshape(19, PLANES, ROWS, COLS),
        solid_mask,
        centers,
        info,
        west,
        east,
        west_2,
        east_2,
        south,
        north,
        south_2,
        north_2,
    )


def solution(mesh):
    return jax.shard_map(
        on_device,
        mesh=mesh,
        in_specs=(
            P(None, None, "gy", "gz"),
            P(None, "gy", "gz"),
            P(None, ("gy", "gz")),
            P(("gy", "gz"), None),
            P(None, ("gy", "gz")),
            P(("gy", "gz")),
            P(),
        ),
        out_specs=(P(None, None, "gy", "gz"), P(None, ("gy", "gz")), P(None, ("gy", "gz"))),
        check_vma=False,
    )
```

```python
import math

import jax
import jax.numpy as jnp
import numpy as np
from jax import lax
from jax.experimental import pallas as pl
from jax.experimental.pallas import tpu as pltpu
from jax.sharding import PartitionSpec as P

TILE = 16
RADIUS = 6
PLANES = 4
ROWS = 32
COLS = 128
SLOTS = 4
GROUPS = PLANES * ROWS // 8

VELOCITIES = (
    (0, 0, 0),
    (1, 0, 0),
    (-1, 0, 0),
    (0, 1, 0),
    (0, -1, 0),
    (0, 0, 1),
    (0, 0, -1),
    (1, 1, 0),
    (-1, -1, 0),
    (1, -1, 0),
    (-1, 1, 0),
    (1, 0, 1),
    (-1, 0, -1),
    (1, 0, -1),
    (-1, 0, 1),
    (0, 1, 1),
    (0, -1, -1),
    (0, 1, -1),
    (0, -1, 1),
)
OPPOSITE = (0, 2, 1, 4, 3, 6, 5, 8, 7, 10, 9, 12, 11, 14, 13, 16, 15, 18, 17)
EXPONENTS = (
    (0, 0, 0),
    (1, 0, 0),
    (0, 1, 0),
    (0, 0, 1),
    (2, 0, 0),
    (0, 2, 0),
    (0, 0, 2),
    (1, 1, 0),
    (1, 0, 1),
    (0, 1, 1),
    (1, 2, 0),
    (1, 0, 2),
    (2, 1, 0),
    (0, 1, 2),
    (2, 0, 1),
    (0, 2, 1),
    (2, 2, 0),
    (2, 0, 2),
    (0, 2, 2),
)
DIRECTIONS = ((-1, -1), (-1, 0), (-1, 1), (0, -1), (0, 1), (1, -1), (1, 0), (1, 1))

Z_UP = (5, 11, 14, 15, 18)
Z_DOWN = (6, 12, 13, 16, 17)
Y_UP = (3, 7, 10, 15, 17)
Y_DOWN = (4, 8, 9, 16, 18)
CLASS_MEMBER = (0, 1, 3, 5, 7, 11, 15)
EVEN_MOMENTS = (0, 4, 5, 6, 16, 17, 18)
ODD_MOMENTS = ((1, 10, 11), (2, 12, 13), (3, 14, 15))
ODD_CLASSES = ((1, 4, 5), (2, 4, 6), (3, 5, 6))
CROSS_MOMENTS = (7, 8, 9)
STATE_LANE = 40
DEST_LANE = 48
HALF = 64
EDGE_ROWS = 24


def moment_basis():
    velocity = np.array(VELOCITIES, dtype=np.float64)
    moment_rows = []
    for a, b, e in EXPONENTS:
        vector = velocity[:, 0] ** a * velocity[:, 1] ** b * velocity[:, 2] ** e
        for earlier in moment_rows:
            vector = vector - np.dot(earlier, vector) * earlier
        moment_rows.append(vector / np.sqrt(np.dot(vector, vector)))
    return np.array(moment_rows)


BASIS = moment_basis()


def store_coefficients(rates, coef):
    splat = [jnp.full((8, COLS), rates[k], jnp.float32) for k in range(19)]
    at = 0
    for a in range(7):
        for b in range(a, 7):
            total = None
            for k in EVEN_MOMENTS:
                c = float(BASIS[k, CLASS_MEMBER[a]] * BASIS[k, CLASS_MEMBER[b]])
                if abs(c) > 1e-12:
                    total = c * splat[k] if total is None else total + c * splat[k]
            coef[at] = total
            at += 1
    for axis in range(3):
        for a in range(3):
            for b in range(a, 3):
                total = None
                for k in ODD_MOMENTS[axis]:
                    c = float(
                        BASIS[k, CLASS_MEMBER[ODD_CLASSES[axis][a]]]
                        * BASIS[k, CLASS_MEMBER[ODD_CLASSES[axis][b]]]
                    )
                    if abs(c) > 1e-12:
                        total = c * splat[k] if total is None else total + c * splat[k]
                coef[at] = total
                at += 1
    for axis in range(3):
        c = float(BASIS[CROSS_MOMENTS[axis], CLASS_MEMBER[4 + axis]] ** 2)
        coef[at] = c * splat[CROSS_MOMENTS[axis]]
        at += 1


N_COEF = 28 + 18 + 3


def collide(f, coef):
    even_at = {}
    at = 0
    for a in range(7):
        for b in range(a, 7):
            even_at[a, b] = even_at[b, a] = at
            at += 1
    odd_at = []
    for _ in range(3):
        table = {}
        for a in range(3):
            for b in range(a, 3):
                table[a, b] = table[b, a] = at
                at += 1
        odd_at.append(table)
    cross_at = at

    def split(i):
        ab, amb = f[i] + f[i + 1], f[i] - f[i + 1]
        cd, cmd = f[i + 2] + f[i + 3], f[i + 2] - f[i + 3]
        return ab + cd, ab - cd, amb + cmd, amb - cmd

    s_xy, q_xy, xy_x, xy_y = split(7)
    s_xz, q_xz, xz_x, xz_z = split(11)
    s_yz, q_yz, yz_y, yz_z = split(15)
    s_x, s_y, s_z = f[1] + f[2], f[3] + f[4], f[5] + f[6]
    d_x, d_y, d_z = f[1] - f[2], f[3] - f[4], f[5] - f[6]
    rho = ((f[0] + s_x) + (s_y + s_z)) + ((s_xy + s_xz) + s_yz)
    j_x = d_x + (xy_x + xz_x)
    j_y = d_y + (xy_y + yz_y)
    j_z = d_z + (xz_z + yz_z)
    inverse = 1.0 / rho
    u_x, u_y, u_z = j_x * inverse, j_y * inverse, j_z * inverse
    e_x, e_y, e_z = j_x * u_x, j_y * u_y, j_z * u_z
    base = (rho - 1.5 * ((e_x + e_y) + e_z)) * (1.0 / 9.0)
    h_x, h_y, h_z = 0.5 * e_x, 0.5 * e_y, 0.5 * e_z
    even = (
        f[0] - 3.0 * base,
        s_x - (base + h_x),
        s_y - (base + h_y),
        s_z - (base + h_z),
        s_xy - (base + (h_x + h_y)),
        s_xz - (base + (h_x + h_z)),
        s_yz - (base + (h_y + h_z)),
    )
    third = 1.0 / 3.0
    t_x, t_y, t_z = third * j_x, third * j_y, third * j_z
    odd = (
        (d_x - t_x, xy_x - t_x, xz_x - t_x),
        (d_y - t_y, xy_y - t_y, yz_y - t_y),
        (d_z - t_z, xz_z - t_z, yz_z - t_z),
    )
    cross = (
        (q_xy - j_x * u_y) * coef[cross_at],
        (q_xz - j_x * u_z) * coef[cross_at + 1],
        (q_yz - j_y * u_z) * coef[cross_at + 2],
    )

    def apply(vector, table, n):
        out = []
        for a in range(n):
            terms = [coef[table[a, b]] * vector[b] for b in range(n)]
            while len(terms) > 1:
                terms = [
                    terms[i] + terms[i + 1] if i + 1 < len(terms) else terms[i]
                    for i in range(0, len(terms), 2)
                ]
            out.append(terms[0])
        return out

    ev = apply(even, even_at, 7)
    ox, oy, oz = (apply(odd[axis], odd_at[axis], 3) for axis in range(3))
    new = [f[0] - ev[0]]
    for axis, o in enumerate((ox, oy, oz)):
        i = 1 + 2 * axis
        new += [f[i] - (ev[1 + axis] + o[0]), f[i + 1] - (ev[1 + axis] - o[0])]
    for axis, (a, b) in enumerate(((ox[1], oy[1]), (ox[2], oz[1]), (oy[2], oz[2]))):
        i = 7 + 4 * axis
        plus, minus = ev[4 + axis] + cross[axis], ev[4 + axis] - cross[axis]
        both, differ = a + b, a - b
        new += [
            f[i] - (plus + both),
            f[i + 1] - (plus - both),
            f[i + 2] - (minus + differ),
            f[i + 3] - (minus - differ),
        ]
    return new


def sphere_partial(coll, center_x, center_y, center_z, row_f, lane_f):
    first = jnp.maximum(lax.shift_right_arithmetic(center_y - (RADIUS + 1), 3), 0)
    last = jnp.minimum(lax.shift_right_arithmetic(center_y + (RADIUS + 1), 3), ROWS // 8 - 1)
    x_f = center_x.astype(jnp.float32)
    r_z = lane_f - center_z.astype(jnp.float32)
    z_sq = r_z * r_z
    zero = jnp.zeros((8, COLS), jnp.float32)

    def row_tile(tile, carry):
        f_x, f_y, f_z, t_x, t_y, t_z = carry
        r_y = row_f + (tile * 8 - center_y).astype(jnp.float32)
        yz_sq = r_y * r_y + z_sq
        p_x, p_y, p_z, x_py, x_pz = zero, zero, zero, zero, zero
        y_plus_z, y_minus_z = r_y + r_z, r_y - r_z
        for t in range(PLANES):
            r_x = t - x_f
            dist = yz_sq + r_x * r_x
            outside = dist > float(RADIUS * RADIUS)
            half = jnp.where(outside, (RADIUS * RADIUS - 1.0) * 0.5 - 0.5 * dist, -1e9)
            half_2 = half - 0.5

            def linked(i, along, limit):
                up, down = VELOCITIES[i][0], VELOCITIES[i + 1][0]
                total = None
                if 0 <= t + up < PLANES:
                    total = jnp.where(along <= limit, coll[i, t * 4 + tile], 0.0)
                if 0 <= t + down < PLANES:
                    back = jnp.where(-along <= limit, coll[i + 1, t * 4 + tile], 0.0)
                    total = -back if total is None else total - back
                return total

            l_x = linked(1, r_x, half)
            l_y = linked(3, r_y, half)
            l_z = linked(5, r_z, half)
            l_xy = linked(7, r_y + r_x, half_2)
            l_xmy = linked(9, r_x - r_y, half_2)
            l_xz = linked(11, r_z + r_x, half_2)
            l_xmz = linked(13, r_x - r_z, half_2)
            l_yz = linked(15, y_plus_z, half_2)
            l_ymz = linked(17, y_minus_z, half_2)
            m_x = l_x + ((l_xy + l_xmy) + (l_xz + l_xmz))
            m_y = l_y + ((l_xy - l_xmy) + (l_yz + l_ymz))
            m_z = l_z + ((l_xz - l_xmz) + (l_yz - l_ymz))
            p_x, p_y, p_z = p_x + m_x, p_y + m_y, p_z + m_z
            x_py, x_pz = x_py + r_x * m_y, x_pz + r_x * m_z
        return (
            f_x + p_x,
            f_y + p_y,
            f_z + p_z,
            t_x + (r_y * p_z - r_z * p_y),
            t_y + (r_z * p_x - x_pz),
            t_z + (x_py - r_y * p_x),
        )

    sums = lax.fori_loop(first, last + 1, row_tile, (zero,) * 6)
    packed = zero
    for j in range(6):
        packed = jnp.where(row_f == float(j), jnp.sum(sums[j], axis=0, keepdims=True), packed)
    return packed


def collide_kernel(
    pops_in,
    mask_in,
    state_in,
    centers_in,
    lists_in,
    destination_in,
    rates_in,
    held,
    walls,
    keep,
    give,
    info,
    inner,
    outer,
    meta,
    pops,
    mask,
    state,
    centers,
    lists,
    destination,
    rates,
    coll,
    coef,
    turn,
    partial,
    sems,
):
    small = [
        pltpu.make_async_copy(source, target, sems.at[4 + k])
        for k, (source, target) in enumerate(
            (
                (rates_in, rates),
                (mask_in, mask),
                (centers_in, centers),
                (lists_in, lists),
                (destination_in, destination),
                (state_in, state),
            )
        )
    ]
    large = [
        pltpu.make_async_copy(
            pops_in.at[:, pl.ds(t * 4, 4)], pops.at[:, pl.ds(t * 4, 4)], sems.at[t]
        )
        for t in range(PLANES)
    ]
    small[0].start()
    small[1].start()
    for copy in large:
        copy.start()
    for copy in small[2:]:
        copy.start()
    lane = lax.broadcasted_iota(jnp.int32, (8, COLS), 1)
    lane_f = lane.astype(jnp.float32)
    row_f = lax.broadcasted_iota(jnp.int32, (8, COLS), 0).astype(jnp.float32)
    small[0].wait()
    store_coefficients(rates, coef)
    small[1].wait()

    def group(g, _):
        f = [pops[i, g] for i in range(19)]
        solid = mask[g] > 0
        flag = solid.astype(jnp.float32)
        walls[g] = flag
        new = collide(f, coef)
        edge = jnp.zeros((8, COLS), jnp.float32)
        for i in range(19):
            coll[i, g] = new[i]
            held[i, g] = jnp.where(solid, f[i], new[i])
        for k, values in enumerate([new[i] for i in Z_UP] + [flag]):
            edge = jnp.where(lane == k, pltpu.roll(values, k + 1, 1), edge)
        for k, values in enumerate([new[i] for i in Z_DOWN] + [flag]):
            edge = jnp.where(lane == 8 + k, pltpu.roll(values, 8 + k, 1), edge)
        turn[pl.ds(pl.multiple_of(g * 8, 8), 8), :] = edge
        return 0

    for t in range(PLANES):
        large[t].wait()
        lax.fori_loop(t * 4, t * 4 + 4, group, 0)
    for copy in small[2:]:
        copy.wait()

    device_y = lax.shift_right_logical(centers[1, 0], 5)
    device_z = lax.shift_right_logical(centers[2, 0], 7)
    core = device_y & 1
    first = core == 0
    meta[0:1, :] = jnp.full((1, COLS), (device_y * 16 + device_z) * SLOTS, jnp.int32).astype(
        jnp.float32
    )
    meta[1:2, :] = jnp.full((1, COLS), core, jnp.int32).astype(jnp.float32)
    meta[2:8, :] = jnp.zeros((6, COLS), jnp.float32)

    turned = turn[...].T
    up_z, down_z = turned[0:8, :], turned[8:16, :]
    keep[...] = jnp.where(first, up_z, down_z)
    give[...] = jnp.where(first, down_z, up_z)
    for t in range(PLANES):
        for d in range(5):
            up = coll[Y_UP[d], t * 4 + 3, 7:8, :]
            down = coll[Y_DOWN[d], t * 4, 0:1, :]
            inner[d * 4 + t : d * 4 + t + 1, :] = jnp.where(first, up, down)
            outer[d * 4 + t : d * 4 + t + 1, :] = jnp.where(first, down, up)
        up = walls[t * 4 + 3, 7:8, :]
        down = walls[t * 4, 0:1, :]
        inner[20 + t : 21 + t, :] = jnp.where(first, up, down)
        outer[20 + t : 21 + t, :] = jnp.where(first, down, up)

    def own(s, _):
        partial[s] = sphere_partial(
            coll, centers[0, s], centers[1, s] & (ROWS - 1), centers[2, s] & (COLS - 1), row_f, lane_f
        )
        return 0

    lax.fori_loop(0, SLOTS, own, 0)

    def listed(r, _):
        partial[SLOTS + r] = jnp.zeros((8, COLS), jnp.float32)

        @pl.when(lists[0, r] >= 0)
        def _():
            partial[SLOTS + r] = sphere_partial(
                coll, lists[3, r], lists[1, r] + TILE // 2, lists[2, r] + TILE // 2, row_f, lane_f
            )

        return 0

    lax.fori_loop(0, 16, listed, 0)

    base = core * HALF
    tile = jnp.zeros((8, COLS), jnp.float32)
    records = state[...].T
    for s in range(SLOTS):
        total = 2.0 * jnp.sum(partial[s], axis=1, keepdims=True)
        tile = jnp.where(lane == base + 4 * SLOTS + s, total, tile)
        tile = jnp.where(lane == base + STATE_LANE + s, records[:, s : s + 1], tile)
        tile = jnp.where(lane == base + DEST_LANE + s, destination[s].astype(jnp.float32), tile)
    for r in range(16):
        offset = DIRECTIONS[r // 2]
        block = (offset[0] + 1) * 3 + offset[1] + 1
        total = 2.0 * jnp.sum(partial[SLOTS + r], axis=1, keepdims=True)
        slot = lists[0, r]
        at = jnp.where(slot >= 0, base + block * SLOTS + slot, -1)
        tile = jnp.where(lane == at, total, tile)
    info[...] = tile


def update_kernel(
    held,
    walls,
    meta,
    chip,
    partner_edge,
    near_in,
    near_2,
    far_in,
    outer_in,
    inner_in,
    out_hbm,
    forces,
    state_next,
    ext,
    turn,
    out,
    sems,
):
    lane = lax.broadcasted_iota(jnp.int32, (8, COLS), 1)
    sub = lax.broadcasted_iota(jnp.int32, (8, COLS), 0)
    row = lane & (ROWS - 1)
    plane = lax.shift_right_logical(lane, 5)
    wall = jnp.inf
    second = jnp.broadcast_to(meta[1:2, :], (8, COLS)) > 0.5

    def swap_if(a, b):
        return jnp.where(second, b, a), jnp.where(second, a, b)

    def walled(values):
        return jnp.where(values[5:6, :] > 0.5, wall, values)

    def side(here, below, above, shifts):
        total = here
        for k, (c_x, c_y) in enumerate(shifts):
            moved = here
            if c_y == 1:
                moved = jnp.where(row == 0, pltpu.roll(below, COLS - 31, 1), pltpu.roll(here, 1, 1))
            if c_y == -1:
                moved = jnp.where(
                    row == ROWS - 1, pltpu.roll(above, 31, 1), pltpu.roll(here, COLS - 1, 1)
                )
            if c_x == 1:
                moved = jnp.where(plane == 0, wall, pltpu.roll(here, 32, 1))
            if c_x == -1:
                moved = jnp.where(plane == PLANES - 1, wall, pltpu.roll(here, COLS - 32, 1))
            total = jnp.where(sub == k, moved, total)
        return total

    west, east = swap_if(walled(near_in[0:8, :]), walled(far_in[8:16, :]))
    west_partner, east_partner = swap_if(walled(near_in[8:16, :]), walled(far_in[0:8, :]))
    west_outer, east_outer = swap_if(
        walled(outer_in[EDGE_ROWS + 8 : EDGE_ROWS + 16, :]), walled(outer_in[EDGE_ROWS : EDGE_ROWS + 8, :])
    )
    west_south, west_north = swap_if(west_outer, west_partner)
    east_south, east_north = swap_if(east_outer, east_partner)
    turn[...] = jnp.zeros((COLS, COLS), jnp.float32)
    turn[0:8, :] = side(west, west_south, west_north, [VELOCITIES[i][:2] for i in Z_UP])
    turn[8:16, :] = side(east, east_south, east_north, [VELOCITIES[i][:2] for i in Z_DOWN])
    turned = turn[...].T
    turn[...] = turned
    pairs = [
        swap_if(outer_in[k : k + 8, :], partner_edge[k : k + 8, :]) for k in range(0, EDGE_ROWS, 8)
    ]
    south = [p[0] for p in pairs]
    north = [p[1] for p in pairs]

    def edge_row(edge, r):
        return edge[r // 8][r % 8 : r % 8 + 1, :]

    column = lax.broadcasted_iota(jnp.int32, (ROWS, COLS), 1)
    for t in range(PLANES):
        solid = walls[t] > 0.5
        for i in range(19):
            ext[i, t, 8 : 8 + ROWS, :] = jnp.where(solid, wall, held[i, t])
        flag_low = edge_row(south, 20 + t) > 0.5
        flag_high = edge_row(north, 20 + t) > 0.5
        for d in range(5):
            r = d * 4 + t
            ext[Y_UP[d], t, 7:8, :] = jnp.where(flag_low, wall, edge_row(south, r))
            ext[Y_DOWN[d], t, 8 + ROWS : 9 + ROWS, :] = jnp.where(
                flag_high, wall, edge_row(north, r)
            )
    copies = []
    for t in range(PLANES):
        solid = walls[t] > 0.5
        for i in range(19):
            c_x, c_y, c_z = VELOCITIES[i]
            source = t - c_x
            if not 0 <= source < PLANES:
                out[i, t] = jnp.where(solid, held[i, t], held[OPPOSITE[i], t])
                continue
            pulled = ext[i, source, 8 - c_y : 8 - c_y + ROWS, :]
            if c_z == 1:
                k = Z_UP.index(i)
                pulled = jnp.where(
                    column == 0, turn[t * ROWS : (t + 1) * ROWS, k : k + 1], pltpu.roll(pulled, 1, 1)
                )
            if c_z == -1:
                k = 8 + Z_DOWN.index(i)
                pulled = jnp.where(
                    column == COLS - 1,
                    turn[t * ROWS : (t + 1) * ROWS, k : k + 1],
                    pltpu.roll(pulled, COLS - 1, 1),
                )
            fluid = jnp.where(pulled == wall, held[OPPOSITE[i], t], pulled)
            out[i, t] = jnp.where(solid, held[i, t], fluid)
        copies.append(pltpu.make_async_copy(out.at[:, t], out_hbm.at[:, t], sems.at[t]))
        copies[t].start()

    middle = {0: chip[...]}
    middle[-1], middle[1] = swap_if(near_in[16:24, :], far_in[16:24, :])
    middle[-2], middle[2] = swap_if(near_2[...], far_in[24:32, :])
    arrived = []
    for ref, start in ((outer_in, EDGE_ROWS + 16), (inner_in, 0)):
        group = [ref[start + 8 * k : start + 8 * k + 8, :] for k in range(5)]
        columns = {0: group[0]}
        columns[-1], columns[1] = swap_if(group[3], group[1])
        columns[-2], columns[2] = swap_if(group[4], group[2])
        arrived.append(columns)
    tiles = {}
    low = lane < HALF
    for b in range(-2, 3):
        before, after = swap_if(arrived[0][b], arrived[1][b])
        turned_before, turned_own, turned_after = (
            pltpu.roll(part, HALF, 1) for part in (before, middle[b], after)
        )
        tiles[0, b] = jnp.where(second, jnp.where(low, turned_before, turned_own), before)
        tiles[1, b] = jnp.where(second, jnp.where(low, turned_own, turned_after), middle[b])
        tiles[2, b] = jnp.where(second, turned_after, after)

    def device_lanes(a, b, at):
        shift = (COLS - (at + HALF * (a % 2))) % COLS
        part = tiles[(a + 2) // 2, b]
        return pltpu.roll(part, shift, 1) if shift else part

    own_lanes = lane < SLOTS
    picked = [jnp.zeros((8, COLS), jnp.float32) for _ in range(SLOTS)]
    for a in (-1, 0, 1):
        for b in (-1, 0, 1):
            force = jnp.zeros((8, COLS), jnp.float32)
            for e in (-1, 0, 1):
                for g in (-1, 0, 1):
                    block = (1 - e) * 3 + 1 - g
                    force = force + device_lanes(a + e, b + g, block * SLOTS)
            if a == 0 and b == 0:
                own_force = force
            record = device_lanes(a, b, STATE_LANE)
            target = device_lanes(a, b, DEST_LANE)[0:1, :]
            mass = record[6:7, :] * (3.0 / (4.0 * math.pi * RADIUS * RADIUS * RADIUS))
            spin = mass * record[7:8, :] * (1.0 / (RADIUS * RADIUS))
            gain = jnp.where(sub < 3, force * mass, jnp.where(sub < 6, force * spin, 0.0))
            updated = record + gain
            for j in range(SLOTS):
                wanted = meta[0:1, :] + float(j)
                picked[j] = picked[j] + jnp.where(own_lanes & (target == wanted), updated, 0.0)
    result = jnp.zeros((8, COLS), jnp.float32)
    for j in range(SLOTS):
        result = jnp.where(lane == j, jnp.sum(picked[j], axis=1, keepdims=True), result)
    turn[0:8, :] = result
    turn[8:16, :] = own_force
    turned = turn[...].T
    state_next[...] = turned[0:SLOTS, 0:8]
    forces[...] = turned[0:SLOTS, 8:14]
    for copy in copies:
        copy.wait()


VMEM = pl.BlockSpec(memory_space=pltpu.VMEM)
HBM = pl.BlockSpec(memory_space=pltpu.HBM)


def f32(*shape):
    return jax.ShapeDtypeStruct(shape, jnp.float32)


def swapped(block, distance):
    count = lax.axis_size("gy")
    route = [(p, (p + (distance if p % 2 == 0 else -distance)) % count) for p in range(count)]
    return lax.ppermute(block, "gy", route)


def spread(block, distance):
    count_y, count_z = lax.axis_size("gy"), lax.axis_size("gz")
    route = []
    for p in range(count_y):
        step = distance if p % 2 == 0 else -distance
        route += [(p * count_z + q, p * count_z + (q + step) % count_z) for q in range(count_z)]
    return lax.ppermute(block, ("gy", "gz"), route)


def on_device(populations, solid_mask, centers, tile_lists, sphere_state, destination, relax_rates):
    held, walls, keep, give, info, inner, outer, meta = pl.pallas_call(
        collide_kernel,
        out_shape=(
            f32(19, GROUPS, 8, COLS),
            f32(GROUPS, 8, COLS),
            f32(8, COLS),
            f32(8, COLS),
            f32(8, COLS),
            f32(EDGE_ROWS, COLS),
            f32(EDGE_ROWS, COLS),
            f32(8, COLS),
        ),
        in_specs=[HBM] * 7,
        out_specs=(VMEM,) * 8,
        scratch_shapes=[
            pltpu.VMEM((19, GROUPS, 8, COLS), jnp.float32),
            pltpu.VMEM((GROUPS, 8, COLS), jnp.int32),
            pltpu.VMEM((SLOTS, 8), jnp.float32),
            pltpu.SMEM((3, SLOTS), jnp.int32),
            pltpu.SMEM((4, 16), jnp.int32),
            pltpu.SMEM((SLOTS,), jnp.int32),
            pltpu.SMEM((19,), jnp.float32),
            pltpu.VMEM((19, GROUPS, 8, COLS), jnp.float32),
            pltpu.VMEM((N_COEF, 8, COLS), jnp.float32),
            pltpu.VMEM((COLS, COLS), jnp.float32),
            pltpu.VMEM((20, 8, COLS), jnp.float32),
            pltpu.SemaphoreType.DMA((10,)),
        ],
        compiler_params=pltpu.CompilerParams(vmem_limit_bytes=32 * 1024 * 1024),
        name="collide",
    )(
        populations.reshape(19, GROUPS, 8, COLS),
        solid_mask.reshape(GROUPS, 8, COLS),
        sphere_state.T,
        centers,
        tile_lists.T,
        destination,
        relax_rates,
    )
    partner = swapped(jnp.concatenate([give, info, inner]), 1)
    chip = info + partner[8:16]
    near_2 = spread(chip, 2)
    near = spread(jnp.concatenate([keep, partner[0:8], chip]), 1)
    far = swapped(jnp.concatenate([near, near_2]), 1)
    spheres = [chip, near[16:24], near_2, far[16:32]]
    from_outer = swapped(jnp.concatenate([outer, near[0:8], far[8:16]] + spheres), -1)
    from_inner = swapped(jnp.concatenate(spheres), 3)
    populations_next, forces, state_next = pl.pallas_call(
        update_kernel,
        out_shape=(f32(19, PLANES, ROWS, COLS), f32(SLOTS, 6), f32(SLOTS, 8)),
        in_specs=[VMEM] * 10,
        out_specs=(HBM, VMEM, VMEM),
        scratch_shapes=[
            pltpu.VMEM((19, PLANES, ROWS + 16, COLS), jnp.float32),
            pltpu.VMEM((COLS, COLS), jnp.float32),
            pltpu.VMEM((19, PLANES, ROWS, COLS), jnp.float32),
            pltpu.SemaphoreType.DMA((PLANES,)),
        ],
        compiler_params=pltpu.CompilerParams(vmem_limit_bytes=32 * 1024 * 1024),
        name="update",
    )(
        held.reshape(19, PLANES, ROWS, COLS),
        walls.reshape(PLANES, ROWS, COLS),
        meta,
        chip,
        partner[16:40],
        near,
        near_2,
        far,
        from_outer,
        from_inner,
    )
    return populations_next, forces.T, state_next.T


def solution(mesh):
    return jax.shard_map(
        on_device,
        mesh=mesh,
        in_specs=(
            P(None, None, "gy", "gz"),
            P(None, "gy", "gz"),
            P(None, ("gy", "gz")),
            P(("gy", "gz"), None),
            P(None, ("gy", "gz")),
            P(("gy", "gz")),
            P(),
        ),
        out_specs=(P(None, None, "gy", "gz"), P(None, ("gy", "gz")), P(None, ("gy", "gz"))),
        check_vma=False,
    )
```

```python
import math

import jax
import jax.numpy as jnp
import numpy as np
from jax import lax
from jax.experimental import pallas as pl
from jax.experimental.pallas import tpu as pltpu
from jax.sharding import PartitionSpec as P

TILE = 16
RADIUS = 6
PLANES = 4
ROWS = 32
COLS = 128
SLOTS = 4
GROUPS = PLANES * ROWS // 8

VELOCITIES = (
    (0, 0, 0),
    (1, 0, 0),
    (-1, 0, 0),
    (0, 1, 0),
    (0, -1, 0),
    (0, 0, 1),
    (0, 0, -1),
    (1, 1, 0),
    (-1, -1, 0),
    (1, -1, 0),
    (-1, 1, 0),
    (1, 0, 1),
    (-1, 0, -1),
    (1, 0, -1),
    (-1, 0, 1),
    (0, 1, 1),
    (0, -1, -1),
    (0, 1, -1),
    (0, -1, 1),
)
OPPOSITE = (0, 2, 1, 4, 3, 6, 5, 8, 7, 10, 9, 12, 11, 14, 13, 16, 15, 18, 17)
EXPONENTS = (
    (0, 0, 0),
    (1, 0, 0),
    (0, 1, 0),
    (0, 0, 1),
    (2, 0, 0),
    (0, 2, 0),
    (0, 0, 2),
    (1, 1, 0),
    (1, 0, 1),
    (0, 1, 1),
    (1, 2, 0),
    (1, 0, 2),
    (2, 1, 0),
    (0, 1, 2),
    (2, 0, 1),
    (0, 2, 1),
    (2, 2, 0),
    (2, 0, 2),
    (0, 2, 2),
)
DIRECTIONS = ((-1, -1), (-1, 0), (-1, 1), (0, -1), (0, 1), (1, -1), (1, 0), (1, 1))

Z_UP = (5, 11, 14, 15, 18)
Z_DOWN = (6, 12, 13, 16, 17)
Y_UP = (3, 7, 10, 15, 17)
Y_DOWN = (4, 8, 9, 16, 18)
CLASS_MEMBER = (0, 1, 3, 5, 7, 11, 15)
EVEN_MOMENTS = (0, 4, 5, 6, 16, 17, 18)
ODD_MOMENTS = ((1, 10, 11), (2, 12, 13), (3, 14, 15))
ODD_CLASSES = ((1, 4, 5), (2, 4, 6), (3, 5, 6))
CROSS_MOMENTS = (7, 8, 9)
STATE_LANE = 40
DEST_LANE = 48
HALF = 64
EDGE_ROWS = 24


def moment_basis():
    velocity = np.array(VELOCITIES, dtype=np.float64)
    moment_rows = []
    for a, b, e in EXPONENTS:
        vector = velocity[:, 0] ** a * velocity[:, 1] ** b * velocity[:, 2] ** e
        for earlier in moment_rows:
            vector = vector - np.dot(earlier, vector) * earlier
        moment_rows.append(vector / np.sqrt(np.dot(vector, vector)))
    return np.array(moment_rows)


BASIS = moment_basis()


def store_coefficients(rates, coef):
    splat = [jnp.full((8, COLS), rates[k], jnp.float32) for k in range(19)]
    at = 0
    for a in range(7):
        for b in range(a, 7):
            total = None
            for k in EVEN_MOMENTS:
                c = float(BASIS[k, CLASS_MEMBER[a]] * BASIS[k, CLASS_MEMBER[b]])
                if abs(c) > 1e-12:
                    total = c * splat[k] if total is None else total + c * splat[k]
            coef[at] = total
            at += 1
    for axis in range(3):
        for a in range(3):
            for b in range(a, 3):
                total = None
                for k in ODD_MOMENTS[axis]:
                    c = float(
                        BASIS[k, CLASS_MEMBER[ODD_CLASSES[axis][a]]]
                        * BASIS[k, CLASS_MEMBER[ODD_CLASSES[axis][b]]]
                    )
                    if abs(c) > 1e-12:
                        total = c * splat[k] if total is None else total + c * splat[k]
                coef[at] = total
                at += 1
    for axis in range(3):
        c = float(BASIS[CROSS_MOMENTS[axis], CLASS_MEMBER[4 + axis]] ** 2)
        coef[at] = c * splat[CROSS_MOMENTS[axis]]
        at += 1


N_COEF = 28 + 18 + 3


def collide(f, coef):
    even_at = {}
    at = 0
    for a in range(7):
        for b in range(a, 7):
            even_at[a, b] = even_at[b, a] = at
            at += 1
    odd_at = []
    for _ in range(3):
        table = {}
        for a in range(3):
            for b in range(a, 3):
                table[a, b] = table[b, a] = at
                at += 1
        odd_at.append(table)
    cross_at = at

    def split(i):
        ab, amb = f[i] + f[i + 1], f[i] - f[i + 1]
        cd, cmd = f[i + 2] + f[i + 3], f[i + 2] - f[i + 3]
        return ab + cd, ab - cd, amb + cmd, amb - cmd

    s_xy, q_xy, xy_x, xy_y = split(7)
    s_xz, q_xz, xz_x, xz_z = split(11)
    s_yz, q_yz, yz_y, yz_z = split(15)
    s_x, s_y, s_z = f[1] + f[2], f[3] + f[4], f[5] + f[6]
    d_x, d_y, d_z = f[1] - f[2], f[3] - f[4], f[5] - f[6]
    rho = ((f[0] + s_x) + (s_y + s_z)) + ((s_xy + s_xz) + s_yz)
    j_x = d_x + (xy_x + xz_x)
    j_y = d_y + (xy_y + yz_y)
    j_z = d_z + (xz_z + yz_z)
    inverse = 1.0 / rho
    u_x, u_y, u_z = j_x * inverse, j_y * inverse, j_z * inverse
    e_x, e_y, e_z = j_x * u_x, j_y * u_y, j_z * u_z
    base = (rho - 1.5 * ((e_x + e_y) + e_z)) * (1.0 / 9.0)
    h_x, h_y, h_z = 0.5 * e_x, 0.5 * e_y, 0.5 * e_z
    even = (
        f[0] - 3.0 * base,
        s_x - (base + h_x),
        s_y - (base + h_y),
        s_z - (base + h_z),
        s_xy - (base + (h_x + h_y)),
        s_xz - (base + (h_x + h_z)),
        s_yz - (base + (h_y + h_z)),
    )
    third = 1.0 / 3.0
    t_x, t_y, t_z = third * j_x, third * j_y, third * j_z
    odd = (
        (d_x - t_x, xy_x - t_x, xz_x - t_x),
        (d_y - t_y, xy_y - t_y, yz_y - t_y),
        (d_z - t_z, xz_z - t_z, yz_z - t_z),
    )
    cross = (
        (q_xy - j_x * u_y) * coef[cross_at],
        (q_xz - j_x * u_z) * coef[cross_at + 1],
        (q_yz - j_y * u_z) * coef[cross_at + 2],
    )

    def apply(vector, table, n):
        out = []
        for a in range(n):
            terms = [coef[table[a, b]] * vector[b] for b in range(n)]
            while len(terms) > 1:
                terms = [
                    terms[i] + terms[i + 1] if i + 1 < len(terms) else terms[i]
                    for i in range(0, len(terms), 2)
                ]
            out.append(terms[0])
        return out

    ev = apply(even, even_at, 7)
    ox, oy, oz = (apply(odd[axis], odd_at[axis], 3) for axis in range(3))
    new = [f[0] - ev[0]]
    for axis, o in enumerate((ox, oy, oz)):
        i = 1 + 2 * axis
        new += [f[i] - (ev[1 + axis] + o[0]), f[i + 1] - (ev[1 + axis] - o[0])]
    for axis, (a, b) in enumerate(((ox[1], oy[1]), (ox[2], oz[1]), (oy[2], oz[2]))):
        i = 7 + 4 * axis
        plus, minus = ev[4 + axis] + cross[axis], ev[4 + axis] - cross[axis]
        both, differ = a + b, a - b
        new += [
            f[i] - (plus + both),
            f[i + 1] - (plus - both),
            f[i + 2] - (minus + differ),
            f[i + 3] - (minus - differ),
        ]
    return new


def sphere_partial(coll, center_x, center_y, center_z, row_f, lane_f):
    first = jnp.maximum(lax.shift_right_arithmetic(center_y - (RADIUS + 1), 3), 0)
    last = jnp.minimum(lax.shift_right_arithmetic(center_y + (RADIUS + 1), 3), ROWS // 8 - 1)
    x_f = center_x.astype(jnp.float32)
    r_z = lane_f - center_z.astype(jnp.float32)
    z_sq = r_z * r_z
    zero = jnp.zeros((8, COLS), jnp.float32)

    def row_tile(tile, carry):
        f_x, f_y, f_z, t_x, t_y, t_z = carry
        r_y = row_f + (tile * 8 - center_y).astype(jnp.float32)
        yz_sq = r_y * r_y + z_sq
        p_x, p_y, p_z, x_py, x_pz = zero, zero, zero, zero, zero
        y_plus_z, y_minus_z = r_y + r_z, r_y - r_z
        for t in range(PLANES):
            r_x = t - x_f
            dist = yz_sq + r_x * r_x
            outside = dist > float(RADIUS * RADIUS)
            half = jnp.where(outside, (RADIUS * RADIUS - 1.0) * 0.5 - 0.5 * dist, -1e9)
            half_2 = half - 0.5

            def linked(i, along, limit):
                up, down = VELOCITIES[i][0], VELOCITIES[i + 1][0]
                total = None
                if 0 <= t + up < PLANES:
                    total = jnp.where(along <= limit, coll[i, t * 4 + tile], 0.0)
                if 0 <= t + down < PLANES:
                    back = jnp.where(-along <= limit, coll[i + 1, t * 4 + tile], 0.0)
                    total = -back if total is None else total - back
                return total

            l_x = linked(1, r_x, half)
            l_y = linked(3, r_y, half)
            l_z = linked(5, r_z, half)
            l_xy = linked(7, r_y + r_x, half_2)
            l_xmy = linked(9, r_x - r_y, half_2)
            l_xz = linked(11, r_z + r_x, half_2)
            l_xmz = linked(13, r_x - r_z, half_2)
            l_yz = linked(15, y_plus_z, half_2)
            l_ymz = linked(17, y_minus_z, half_2)
            m_x = l_x + ((l_xy + l_xmy) + (l_xz + l_xmz))
            m_y = l_y + ((l_xy - l_xmy) + (l_yz + l_ymz))
            m_z = l_z + ((l_xz - l_xmz) + (l_yz - l_ymz))
            p_x, p_y, p_z = p_x + m_x, p_y + m_y, p_z + m_z
            x_py, x_pz = x_py + r_x * m_y, x_pz + r_x * m_z
        return (
            f_x + p_x,
            f_y + p_y,
            f_z + p_z,
            t_x + (r_y * p_z - r_z * p_y),
            t_y + (r_z * p_x - x_pz),
            t_z + (x_py - r_y * p_x),
        )

    sums = lax.fori_loop(first, last + 1, row_tile, (zero,) * 6)
    packed = zero
    for j in range(6):
        packed = jnp.where(row_f == float(j), jnp.sum(sums[j], axis=0, keepdims=True), packed)
    return packed


def collide_kernel(
    pops_in,
    mask_in,
    state_in,
    centers_in,
    lists_in,
    destination_in,
    rates_in,
    held,
    walls,
    keep,
    give,
    info,
    inner,
    outer,
    meta,
    pops,
    mask,
    state,
    centers,
    lists,
    destination,
    rates,
    coll,
    coef,
    turn,
    partial,
    sems,
):
    small = [
        pltpu.make_async_copy(source, target, sems.at[4 + k])
        for k, (source, target) in enumerate(
            (
                (rates_in, rates),
                (mask_in, mask),
                (centers_in, centers),
                (lists_in, lists),
                (destination_in, destination),
                (state_in, state),
            )
        )
    ]
    large = [
        pltpu.make_async_copy(
            pops_in.at[:, pl.ds(t * 4, 4)], pops.at[:, pl.ds(t * 4, 4)], sems.at[t]
        )
        for t in range(PLANES)
    ]
    small[0].start()
    small[1].start()
    for copy in large:
        copy.start()
    for copy in small[2:]:
        copy.start()
    lane = lax.broadcasted_iota(jnp.int32, (8, COLS), 1)
    lane_f = lane.astype(jnp.float32)
    row_f = lax.broadcasted_iota(jnp.int32, (8, COLS), 0).astype(jnp.float32)
    small[0].wait()
    store_coefficients(rates, coef)
    small[1].wait()

    def group(g, _):
        f = [pops[i, g] for i in range(19)]
        solid = mask[g] > 0
        flag = solid.astype(jnp.float32)
        walls[g] = flag
        new = collide(f, coef)
        edge = jnp.zeros((8, COLS), jnp.float32)
        for i in range(19):
            coll[i, g] = new[i]
            held[i, g] = jnp.where(solid, f[i], new[i])
        for k, values in enumerate([new[i] for i in Z_UP] + [flag]):
            edge = jnp.where(lane == k, pltpu.roll(values, k + 1, 1), edge)
        for k, values in enumerate([new[i] for i in Z_DOWN] + [flag]):
            edge = jnp.where(lane == 8 + k, pltpu.roll(values, 8 + k, 1), edge)
        turn[pl.ds(pl.multiple_of(g * 8, 8), 8), :] = edge
        return 0

    for t in range(PLANES):
        large[t].wait()
        lax.fori_loop(t * 4, t * 4 + 4, group, 0)
    for copy in small[2:]:
        copy.wait()

    device_y = lax.shift_right_logical(centers[1, 0], 5)
    device_z = lax.shift_right_logical(centers[2, 0], 7)
    core = device_y & 1
    first = core == 0
    meta[0:1, :] = jnp.full((1, COLS), (device_y * 16 + device_z) * SLOTS, jnp.int32).astype(
        jnp.float32
    )
    meta[1:2, :] = jnp.full((1, COLS), core, jnp.int32).astype(jnp.float32)
    meta[2:8, :] = jnp.zeros((6, COLS), jnp.float32)

    turned = turn[...].T
    up_z, down_z = turned[0:8, :], turned[8:16, :]
    keep[...] = jnp.where(first, up_z, down_z)
    give[...] = jnp.where(first, down_z, up_z)
    for t in range(PLANES):
        for d in range(5):
            up = coll[Y_UP[d], t * 4 + 3, 7:8, :]
            down = coll[Y_DOWN[d], t * 4, 0:1, :]
            inner[d * 4 + t : d * 4 + t + 1, :] = jnp.where(first, up, down)
            outer[d * 4 + t : d * 4 + t + 1, :] = jnp.where(first, down, up)
        up = walls[t * 4 + 3, 7:8, :]
        down = walls[t * 4, 0:1, :]
        inner[20 + t : 21 + t, :] = jnp.where(first, up, down)
        outer[20 + t : 21 + t, :] = jnp.where(first, down, up)

    def own(s, _):
        partial[s] = sphere_partial(
            coll, centers[0, s], centers[1, s] & (ROWS - 1), centers[2, s] & (COLS - 1), row_f, lane_f
        )
        return 0

    lax.fori_loop(0, SLOTS, own, 0)

    def listed(r, _):
        partial[SLOTS + r] = jnp.zeros((8, COLS), jnp.float32)

        @pl.when(lists[0, r] >= 0)
        def _():
            partial[SLOTS + r] = sphere_partial(
                coll, lists[3, r], lists[1, r] + TILE // 2, lists[2, r] + TILE // 2, row_f, lane_f
            )

        return 0

    lax.fori_loop(0, 16, listed, 0)

    base = core * HALF
    tile = jnp.zeros((8, COLS), jnp.float32)
    records = state[...].T
    for s in range(SLOTS):
        total = 2.0 * jnp.sum(partial[s], axis=1, keepdims=True)
        tile = jnp.where(lane == base + 4 * SLOTS + s, total, tile)
        tile = jnp.where(lane == base + STATE_LANE + s, records[:, s : s + 1], tile)
        tile = jnp.where(lane == base + DEST_LANE + s, destination[s].astype(jnp.float32), tile)
    for r in range(16):
        offset = DIRECTIONS[r // 2]
        block = (offset[0] + 1) * 3 + offset[1] + 1
        total = 2.0 * jnp.sum(partial[SLOTS + r], axis=1, keepdims=True)
        slot = lists[0, r]
        at = jnp.where(slot >= 0, base + block * SLOTS + slot, -1)
        tile = jnp.where(lane == at, total, tile)
    info[...] = tile


def update_kernel(
    held,
    walls,
    meta,
    chip,
    partner_edge,
    near_in,
    near_2,
    far_in,
    outer_in,
    inner_in,
    out_hbm,
    forces,
    state_next,
    ext,
    turn,
    out,
    sems,
):
    lane = lax.broadcasted_iota(jnp.int32, (8, COLS), 1)
    sub = lax.broadcasted_iota(jnp.int32, (8, COLS), 0)
    row = lane & (ROWS - 1)
    plane = lax.shift_right_logical(lane, 5)
    wall = jnp.inf
    second = jnp.broadcast_to(meta[1:2, :], (8, COLS)) > 0.5

    def swap_if(a, b):
        return jnp.where(second, b, a), jnp.where(second, a, b)

    def walled(values):
        return jnp.where(values[5:6, :] > 0.5, wall, values)

    def side(here, below, above, shifts):
        total = here
        for k, (c_x, c_y) in enumerate(shifts):
            moved = here
            if c_y == 1:
                moved = jnp.where(row == 0, pltpu.roll(below, COLS - 31, 1), pltpu.roll(here, 1, 1))
            if c_y == -1:
                moved = jnp.where(
                    row == ROWS - 1, pltpu.roll(above, 31, 1), pltpu.roll(here, COLS - 1, 1)
                )
            if c_x == 1:
                moved = jnp.where(plane == 0, wall, pltpu.roll(here, 32, 1))
            if c_x == -1:
                moved = jnp.where(plane == PLANES - 1, wall, pltpu.roll(here, COLS - 32, 1))
            total = jnp.where(sub == k, moved, total)
        return total

    west, east = swap_if(walled(near_in[0:8, :]), walled(far_in[8:16, :]))
    west_partner, east_partner = swap_if(walled(near_in[8:16, :]), walled(far_in[0:8, :]))
    west_outer, east_outer = swap_if(
        walled(outer_in[EDGE_ROWS + 8 : EDGE_ROWS + 16, :]), walled(outer_in[EDGE_ROWS : EDGE_ROWS + 8, :])
    )
    west_south, west_north = swap_if(west_outer, west_partner)
    east_south, east_north = swap_if(east_outer, east_partner)
    turn[...] = jnp.zeros((COLS, COLS), jnp.float32)
    turn[0:8, :] = side(west, west_south, west_north, [VELOCITIES[i][:2] for i in Z_UP])
    turn[8:16, :] = side(east, east_south, east_north, [VELOCITIES[i][:2] for i in Z_DOWN])
    turned = turn[...].T
    turn[...] = turned
    pairs = [
        swap_if(outer_in[k : k + 8, :], partner_edge[k : k + 8, :]) for k in range(0, EDGE_ROWS, 8)
    ]
    south = [p[0] for p in pairs]
    north = [p[1] for p in pairs]

    def edge_row(edge, r):
        return edge[r // 8][r % 8 : r % 8 + 1, :]

    column = lax.broadcasted_iota(jnp.int32, (ROWS, COLS), 1)
    for t in range(PLANES):
        solid = walls[t] > 0.5
        for i in range(19):
            ext[i, t, 8 : 8 + ROWS, :] = jnp.where(solid, wall, held[i, t])
        flag_low = edge_row(south, 20 + t) > 0.5
        flag_high = edge_row(north, 20 + t) > 0.5
        for d in range(5):
            r = d * 4 + t
            ext[Y_UP[d], t, 7:8, :] = jnp.where(flag_low, wall, edge_row(south, r))
            ext[Y_DOWN[d], t, 8 + ROWS : 9 + ROWS, :] = jnp.where(
                flag_high, wall, edge_row(north, r)
            )
    copies = []
    for t in range(PLANES):
        solid = walls[t] > 0.5
        for i in range(19):
            c_x, c_y, c_z = VELOCITIES[i]
            source = t - c_x
            if not 0 <= source < PLANES:
                out[i, t] = jnp.where(solid, held[i, t], held[OPPOSITE[i], t])
                continue
            pulled = ext[i, source, 8 - c_y : 8 - c_y + ROWS, :]
            if c_z == 1:
                k = Z_UP.index(i)
                pulled = jnp.where(
                    column == 0, turn[t * ROWS : (t + 1) * ROWS, k : k + 1], pltpu.roll(pulled, 1, 1)
                )
            if c_z == -1:
                k = 8 + Z_DOWN.index(i)
                pulled = jnp.where(
                    column == COLS - 1,
                    turn[t * ROWS : (t + 1) * ROWS, k : k + 1],
                    pltpu.roll(pulled, COLS - 1, 1),
                )
            fluid = jnp.where(pulled == wall, held[OPPOSITE[i], t], pulled)
            out[i, t] = jnp.where(solid, held[i, t], fluid)
        copies.append(pltpu.make_async_copy(out.at[:, t], out_hbm.at[:, t], sems.at[t]))
        copies[t].start()

    middle = {0: chip[...]}
    middle[-1], middle[1] = swap_if(near_in[16:24, :], far_in[16:24, :])
    middle[-2], middle[2] = swap_if(near_2[...], far_in[24:32, :])
    arrived = []
    for ref, start in ((outer_in, EDGE_ROWS + 16), (inner_in, 0)):
        group = [ref[start + 8 * k : start + 8 * k + 8, :] for k in range(5)]
        columns = {0: group[0]}
        columns[-1], columns[1] = swap_if(group[3], group[1])
        columns[-2], columns[2] = swap_if(group[4], group[2])
        arrived.append(columns)
    tiles = {}
    low = lane < HALF
    for b in range(-2, 3):
        before, after = swap_if(arrived[0][b], arrived[1][b])
        turned_before, turned_own, turned_after = (
            pltpu.roll(part, HALF, 1) for part in (before, middle[b], after)
        )
        tiles[0, b] = jnp.where(second, jnp.where(low, turned_before, turned_own), before)
        tiles[1, b] = jnp.where(second, jnp.where(low, turned_own, turned_after), middle[b])
        tiles[2, b] = jnp.where(second, turned_after, after)

    def device_lanes(a, b, at):
        shift = (COLS - (at + HALF * (a % 2))) % COLS
        part = tiles[(a + 2) // 2, b]
        return pltpu.roll(part, shift, 1) if shift else part

    own_lanes = lane < SLOTS
    picked = [jnp.zeros((8, COLS), jnp.float32) for _ in range(SLOTS)]
    for a in (-1, 0, 1):
        for b in (-1, 0, 1):
            force = jnp.zeros((8, COLS), jnp.float32)
            for e in (-1, 0, 1):
                for g in (-1, 0, 1):
                    block = (1 - e) * 3 + 1 - g
                    force = force + device_lanes(a + e, b + g, block * SLOTS)
            if a == 0 and b == 0:
                own_force = force
            record = device_lanes(a, b, STATE_LANE)
            target = device_lanes(a, b, DEST_LANE)[0:1, :]
            mass = record[6:7, :] * (3.0 / (4.0 * math.pi * RADIUS * RADIUS * RADIUS))
            spin = mass * record[7:8, :] * (1.0 / (RADIUS * RADIUS))
            gain = jnp.where(sub < 3, force * mass, jnp.where(sub < 6, force * spin, 0.0))
            updated = record + gain
            for j in range(SLOTS):
                wanted = meta[0:1, :] + float(j)
                picked[j] = picked[j] + jnp.where(own_lanes & (target == wanted), updated, 0.0)
    result = jnp.zeros((8, COLS), jnp.float32)
    for j in range(SLOTS):
        result = jnp.where(lane == j, jnp.sum(picked[j], axis=1, keepdims=True), result)
    turn[0:8, :] = result
    turn[8:16, :] = own_force
    turned = turn[...].T
    state_next[...] = turned[0:SLOTS, 0:8]
    forces[...] = turned[0:SLOTS, 8:14]
    for copy in copies:
        copy.wait()


VMEM = pl.BlockSpec(memory_space=pltpu.VMEM)
HBM = pl.BlockSpec(memory_space=pltpu.HBM)


def f32(*shape):
    return jax.ShapeDtypeStruct(shape, jnp.float32)


def in_hbm(array):
    return pltpu.with_memory_space_constraint(array, pltpu.HBM)


def swapped(block, distance):
    count = lax.axis_size("gy")
    route = [(p, (p + (distance if p % 2 == 0 else -distance)) % count) for p in range(count)]
    return lax.ppermute(block, "gy", route)


def spread(block, distance):
    count_y, count_z = lax.axis_size("gy"), lax.axis_size("gz")
    route = []
    for p in range(count_y):
        step = distance if p % 2 == 0 else -distance
        route += [(p * count_z + q, p * count_z + (q + step) % count_z) for q in range(count_z)]
    return lax.ppermute(block, ("gy", "gz"), route)


def on_device(populations, solid_mask, centers, tile_lists, sphere_state, destination, relax_rates):
    held, walls, keep, give, info, inner, outer, meta = pl.pallas_call(
        collide_kernel,
        out_shape=(
            f32(19, GROUPS, 8, COLS),
            f32(GROUPS, 8, COLS),
            f32(8, COLS),
            f32(8, COLS),
            f32(8, COLS),
            f32(EDGE_ROWS, COLS),
            f32(EDGE_ROWS, COLS),
            f32(8, COLS),
        ),
        in_specs=[HBM] * 7,
        out_specs=(VMEM,) * 8,
        scratch_shapes=[
            pltpu.VMEM((19, GROUPS, 8, COLS), jnp.float32),
            pltpu.VMEM((GROUPS, 8, COLS), jnp.int32),
            pltpu.VMEM((SLOTS, 8), jnp.float32),
            pltpu.SMEM((3, SLOTS), jnp.int32),
            pltpu.SMEM((4, 16), jnp.int32),
            pltpu.SMEM((SLOTS,), jnp.int32),
            pltpu.SMEM((19,), jnp.float32),
            pltpu.VMEM((19, GROUPS, 8, COLS), jnp.float32),
            pltpu.VMEM((N_COEF, 8, COLS), jnp.float32),
            pltpu.VMEM((COLS, COLS), jnp.float32),
            pltpu.VMEM((20, 8, COLS), jnp.float32),
            pltpu.SemaphoreType.DMA((10,)),
        ],
        compiler_params=pltpu.CompilerParams(vmem_limit_bytes=32 * 1024 * 1024),
        name="collide",
    )(
        in_hbm(populations.reshape(19, GROUPS, 8, COLS)),
        in_hbm(solid_mask.reshape(GROUPS, 8, COLS)),
        in_hbm(sphere_state.T),
        in_hbm(centers),
        in_hbm(tile_lists.T),
        in_hbm(destination),
        in_hbm(relax_rates),
    )
    partner = swapped(jnp.concatenate([give, info, inner]), 1)
    chip = info + partner[8:16]
    near_2 = spread(chip, 2)
    near = spread(jnp.concatenate([keep, partner[0:8], chip]), 1)
    far = swapped(jnp.concatenate([near, near_2]), 1)
    spheres = [chip, near[16:24], near_2, far[16:32]]
    from_outer = swapped(jnp.concatenate([outer, near[0:8], far[8:16]] + spheres), -1)
    from_inner = swapped(jnp.concatenate(spheres), 3)
    populations_next, forces, state_next = pl.pallas_call(
        update_kernel,
        out_shape=(f32(19, PLANES, ROWS, COLS), f32(SLOTS, 6), f32(SLOTS, 8)),
        in_specs=[VMEM] * 10,
        out_specs=(HBM, VMEM, VMEM),
        scratch_shapes=[
            pltpu.VMEM((19, PLANES, ROWS + 16, COLS), jnp.float32),
            pltpu.VMEM((COLS, COLS), jnp.float32),
            pltpu.VMEM((19, PLANES, ROWS, COLS), jnp.float32),
            pltpu.SemaphoreType.DMA((PLANES,)),
        ],
        compiler_params=pltpu.CompilerParams(vmem_limit_bytes=32 * 1024 * 1024),
        name="update",
    )(
        held.reshape(19, PLANES, ROWS, COLS),
        walls.reshape(PLANES, ROWS, COLS),
        meta,
        chip,
        partner[16:40],
        near,
        near_2,
        far,
        from_outer,
        from_inner,
    )
    return populations_next, forces.T, state_next.T


def solution(mesh):
    return jax.shard_map(
        on_device,
        mesh=mesh,
        in_specs=(
            P(None, None, "gy", "gz"),
            P(None, "gy", "gz"),
            P(None, ("gy", "gz")),
            P(("gy", "gz"), None),
            P(None, ("gy", "gz")),
            P(("gy", "gz")),
            P(),
        ),
        out_specs=(P(None, None, "gy", "gz"), P(None, ("gy", "gz")), P(None, ("gy", "gz"))),
        check_vma=False,
    )
```

```python
import math

import jax
import jax.numpy as jnp
import numpy as np
from jax import lax
from jax.experimental import pallas as pl
from jax.experimental.pallas import tpu as pltpu
from jax.sharding import PartitionSpec as P

TILE = 16
RADIUS = 6
PLANES = 4
ROWS = 32
COLS = 128
SLOTS = 4
GROUPS = PLANES * ROWS // 8

VELOCITIES = (
    (0, 0, 0),
    (1, 0, 0),
    (-1, 0, 0),
    (0, 1, 0),
    (0, -1, 0),
    (0, 0, 1),
    (0, 0, -1),
    (1, 1, 0),
    (-1, -1, 0),
    (1, -1, 0),
    (-1, 1, 0),
    (1, 0, 1),
    (-1, 0, -1),
    (1, 0, -1),
    (-1, 0, 1),
    (0, 1, 1),
    (0, -1, -1),
    (0, 1, -1),
    (0, -1, 1),
)
OPPOSITE = (0, 2, 1, 4, 3, 6, 5, 8, 7, 10, 9, 12, 11, 14, 13, 16, 15, 18, 17)
EXPONENTS = (
    (0, 0, 0),
    (1, 0, 0),
    (0, 1, 0),
    (0, 0, 1),
    (2, 0, 0),
    (0, 2, 0),
    (0, 0, 2),
    (1, 1, 0),
    (1, 0, 1),
    (0, 1, 1),
    (1, 2, 0),
    (1, 0, 2),
    (2, 1, 0),
    (0, 1, 2),
    (2, 0, 1),
    (0, 2, 1),
    (2, 2, 0),
    (2, 0, 2),
    (0, 2, 2),
)
DIRECTIONS = ((-1, -1), (-1, 0), (-1, 1), (0, -1), (0, 1), (1, -1), (1, 0), (1, 1))

Z_UP = (5, 11, 14, 15, 18)
Z_DOWN = (6, 12, 13, 16, 17)
Y_UP = (3, 7, 10, 15, 17)
Y_DOWN = (4, 8, 9, 16, 18)
CLASS_MEMBER = (0, 1, 3, 5, 7, 11, 15)
EVEN_MOMENTS = (0, 4, 5, 6, 16, 17, 18)
ODD_MOMENTS = ((1, 10, 11), (2, 12, 13), (3, 14, 15))
ODD_CLASSES = ((1, 4, 5), (2, 4, 6), (3, 5, 6))
CROSS_MOMENTS = (7, 8, 9)
STATE_LANE = 40
DEST_LANE = 48
HALF = 64
EDGE_ROWS = 24


def moment_basis():
    velocity = np.array(VELOCITIES, dtype=np.float64)
    moment_rows = []
    for a, b, e in EXPONENTS:
        vector = velocity[:, 0] ** a * velocity[:, 1] ** b * velocity[:, 2] ** e
        for earlier in moment_rows:
            vector = vector - np.dot(earlier, vector) * earlier
        moment_rows.append(vector / np.sqrt(np.dot(vector, vector)))
    return np.array(moment_rows)


BASIS = moment_basis()


def store_coefficients(rates, coef):
    splat = [jnp.full((8, COLS), rates[k], jnp.float32) for k in range(19)]
    at = 0
    for a in range(7):
        for b in range(a, 7):
            total = None
            for k in EVEN_MOMENTS:
                c = float(BASIS[k, CLASS_MEMBER[a]] * BASIS[k, CLASS_MEMBER[b]])
                if abs(c) > 1e-12:
                    total = c * splat[k] if total is None else total + c * splat[k]
            coef[at] = total
            at += 1
    for axis in range(3):
        for a in range(3):
            for b in range(a, 3):
                total = None
                for k in ODD_MOMENTS[axis]:
                    c = float(
                        BASIS[k, CLASS_MEMBER[ODD_CLASSES[axis][a]]]
                        * BASIS[k, CLASS_MEMBER[ODD_CLASSES[axis][b]]]
                    )
                    if abs(c) > 1e-12:
                        total = c * splat[k] if total is None else total + c * splat[k]
                coef[at] = total
                at += 1
    for axis in range(3):
        c = float(BASIS[CROSS_MOMENTS[axis], CLASS_MEMBER[4 + axis]] ** 2)
        coef[at] = c * splat[CROSS_MOMENTS[axis]]
        at += 1


N_COEF = 28 + 18 + 3


def collide(f, coef):
    even_at = {}
    at = 0
    for a in range(7):
        for b in range(a, 7):
            even_at[a, b] = even_at[b, a] = at
            at += 1
    odd_at = []
    for _ in range(3):
        table = {}
        for a in range(3):
            for b in range(a, 3):
                table[a, b] = table[b, a] = at
                at += 1
        odd_at.append(table)
    cross_at = at

    def split(i):
        ab, amb = f[i] + f[i + 1], f[i] - f[i + 1]
        cd, cmd = f[i + 2] + f[i + 3], f[i + 2] - f[i + 3]
        return ab + cd, ab - cd, amb + cmd, amb - cmd

    s_xy, q_xy, xy_x, xy_y = split(7)
    s_xz, q_xz, xz_x, xz_z = split(11)
    s_yz, q_yz, yz_y, yz_z = split(15)
    s_x, s_y, s_z = f[1] + f[2], f[3] + f[4], f[5] + f[6]
    d_x, d_y, d_z = f[1] - f[2], f[3] - f[4], f[5] - f[6]
    rho = ((f[0] + s_x) + (s_y + s_z)) + ((s_xy + s_xz) + s_yz)
    j_x = d_x + (xy_x + xz_x)
    j_y = d_y + (xy_y + yz_y)
    j_z = d_z + (xz_z + yz_z)
    inverse = 1.0 / rho
    u_x, u_y, u_z = j_x * inverse, j_y * inverse, j_z * inverse
    e_x, e_y, e_z = j_x * u_x, j_y * u_y, j_z * u_z
    base = (rho - 1.5 * ((e_x + e_y) + e_z)) * (1.0 / 9.0)
    h_x, h_y, h_z = 0.5 * e_x, 0.5 * e_y, 0.5 * e_z
    even = (
        f[0] - 3.0 * base,
        s_x - (base + h_x),
        s_y - (base + h_y),
        s_z - (base + h_z),
        s_xy - (base + (h_x + h_y)),
        s_xz - (base + (h_x + h_z)),
        s_yz - (base + (h_y + h_z)),
    )
    third = 1.0 / 3.0
    t_x, t_y, t_z = third * j_x, third * j_y, third * j_z
    odd = (
        (d_x - t_x, xy_x - t_x, xz_x - t_x),
        (d_y - t_y, xy_y - t_y, yz_y - t_y),
        (d_z - t_z, xz_z - t_z, yz_z - t_z),
    )
    cross = (
        (q_xy - j_x * u_y) * coef[cross_at],
        (q_xz - j_x * u_z) * coef[cross_at + 1],
        (q_yz - j_y * u_z) * coef[cross_at + 2],
    )

    def apply(vector, table, n):
        out = []
        for a in range(n):
            terms = [coef[table[a, b]] * vector[b] for b in range(n)]
            while len(terms) > 1:
                terms = [
                    terms[i] + terms[i + 1] if i + 1 < len(terms) else terms[i]
                    for i in range(0, len(terms), 2)
                ]
            out.append(terms[0])
        return out

    ev = apply(even, even_at, 7)
    ox, oy, oz = (apply(odd[axis], odd_at[axis], 3) for axis in range(3))
    new = [f[0] - ev[0]]
    for axis, o in enumerate((ox, oy, oz)):
        i = 1 + 2 * axis
        new += [f[i] - (ev[1 + axis] + o[0]), f[i + 1] - (ev[1 + axis] - o[0])]
    for axis, (a, b) in enumerate(((ox[1], oy[1]), (ox[2], oz[1]), (oy[2], oz[2]))):
        i = 7 + 4 * axis
        plus, minus = ev[4 + axis] + cross[axis], ev[4 + axis] - cross[axis]
        both, differ = a + b, a - b
        new += [
            f[i] - (plus + both),
            f[i + 1] - (plus - both),
            f[i + 2] - (minus + differ),
            f[i + 3] - (minus - differ),
        ]
    return new


def sphere_partial(coll, center_x, center_y, center_z, row_f, lane_f):
    first = jnp.maximum(lax.shift_right_arithmetic(center_y - (RADIUS + 1), 3), 0)
    last = jnp.minimum(lax.shift_right_arithmetic(center_y + (RADIUS + 1), 3), ROWS // 8 - 1)
    x_f = center_x.astype(jnp.float32)
    r_z = lane_f - center_z.astype(jnp.float32)
    z_sq = r_z * r_z
    zero = jnp.zeros((8, COLS), jnp.float32)

    def row_tile(tile, carry):
        f_x, f_y, f_z, t_x, t_y, t_z = carry
        r_y = row_f + (tile * 8 - center_y).astype(jnp.float32)
        yz_sq = r_y * r_y + z_sq
        p_x, p_y, p_z, x_py, x_pz = zero, zero, zero, zero, zero
        y_plus_z, y_minus_z = r_y + r_z, r_y - r_z
        for t in range(PLANES):
            r_x = t - x_f
            dist = yz_sq + r_x * r_x
            outside = dist > float(RADIUS * RADIUS)
            half = jnp.where(outside, (RADIUS * RADIUS - 1.0) * 0.5 - 0.5 * dist, -1e9)
            half_2 = half - 0.5
            limits = {1: (half, -half), 2: (half_2, -half_2)}

            def linked(i, along, kind):
                limit, negative = limits[kind]
                up, down = VELOCITIES[i][0], VELOCITIES[i + 1][0]
                total = None
                if 0 <= t + up < PLANES:
                    total = jnp.where(along <= limit, coll[i, t * 4 + tile], 0.0)
                if 0 <= t + down < PLANES:
                    back = jnp.where(along >= negative, coll[i + 1, t * 4 + tile], 0.0)
                    total = -back if total is None else total - back
                return total

            l_x = linked(1, r_x, 1)
            l_y = linked(3, r_y, 1)
            l_z = linked(5, r_z, 1)
            l_xy = linked(7, r_y + r_x, 2)
            l_xmy = linked(9, r_x - r_y, 2)
            l_xz = linked(11, r_z + r_x, 2)
            l_xmz = linked(13, r_x - r_z, 2)
            l_yz = linked(15, y_plus_z, 2)
            l_ymz = linked(17, y_minus_z, 2)
            m_x = l_x + ((l_xy + l_xmy) + (l_xz + l_xmz))
            m_y = l_y + ((l_xy - l_xmy) + (l_yz + l_ymz))
            m_z = l_z + ((l_xz - l_xmz) + (l_yz - l_ymz))
            p_x, p_y, p_z = p_x + m_x, p_y + m_y, p_z + m_z
            x_py, x_pz = x_py + r_x * m_y, x_pz + r_x * m_z
        return (
            f_x + p_x,
            f_y + p_y,
            f_z + p_z,
            t_x + (r_y * p_z - r_z * p_y),
            t_y + (r_z * p_x - x_pz),
            t_z + (x_py - r_y * p_x),
        )

    sums = lax.fori_loop(first, last + 1, row_tile, (zero,) * 6)
    packed = zero
    for j in range(6):
        packed = jnp.where(row_f == float(j), jnp.sum(sums[j], axis=0, keepdims=True), packed)
    return packed


def collide_kernel(
    pops_in,
    mask_in,
    state_in,
    centers_in,
    lists_in,
    destination_in,
    rates_in,
    held,
    walls,
    keep,
    give,
    info,
    inner,
    outer,
    border,
    meta,
    pops,
    mask,
    state,
    centers,
    lists,
    destination,
    rates,
    coll,
    coef,
    turn,
    partial,
    sems,
):
    small = [
        pltpu.make_async_copy(source, target, sems.at[4 + k])
        for k, (source, target) in enumerate(
            (
                (rates_in, rates),
                (mask_in, mask),
                (centers_in, centers),
                (lists_in, lists),
                (destination_in, destination),
                (state_in, state),
            )
        )
    ]
    large = [
        pltpu.make_async_copy(
            pops_in.at[:, pl.ds(t * 4, 4)], pops.at[:, pl.ds(t * 4, 4)], sems.at[t]
        )
        for t in range(PLANES)
    ]
    small[0].start()
    small[1].start()
    for copy in large:
        copy.start()
    for copy in small[2:]:
        copy.start()
    lane = lax.broadcasted_iota(jnp.int32, (8, COLS), 1)
    lane_f = lane.astype(jnp.float32)
    row_f = lax.broadcasted_iota(jnp.int32, (8, COLS), 0).astype(jnp.float32)
    small[0].wait()
    store_coefficients(rates, coef)
    small[1].wait()

    def group(g, _):
        f = [pops[i, g] for i in range(19)]
        solid = mask[g] > 0
        flag = solid.astype(jnp.float32)
        walls[g] = flag
        new = collide(f, coef)
        for i in range(19):
            coll[i, g] = new[i]
            held[i, g] = jnp.where(solid, f[i], new[i])
        return 0

    for t in range(PLANES):
        large[t].wait()
        lax.fori_loop(t * 4, t * 4 + 4, group, 0)
    for copy in small[2:]:
        copy.wait()

    device_y = lax.shift_right_logical(centers[1, 0], 5)
    device_z = lax.shift_right_logical(centers[2, 0], 7)
    core = device_y & 1
    first = core == 0
    meta[0:1, :] = jnp.full((1, COLS), (device_y * 16 + device_z) * SLOTS, jnp.int32).astype(
        jnp.float32
    )
    meta[1:2, :] = jnp.full((1, COLS), core, jnp.int32).astype(jnp.float32)
    meta[2:8, :] = jnp.zeros((6, COLS), jnp.float32)

    for g in range(GROUPS):
        edge = jnp.zeros((8, COLS), jnp.float32)
        for k in range(6):
            values = coll[Z_UP[k], g] if k < 5 else walls[g]
            edge = jnp.where(lane == k, pltpu.roll(values, k + 1, 1), edge)
        for k in range(6):
            values = coll[Z_DOWN[k], g] if k < 5 else walls[g]
            edge = jnp.where(lane == 8 + k, pltpu.roll(values, 8 + k, 1), edge)
        turn[g * 8 : g * 8 + 8, :] = edge
    turned = turn[...].T
    up_z, down_z = turned[0:8, :], turned[8:16, :]
    border[...] = turned[0:16, :]
    keep[...] = jnp.where(first, up_z, down_z)
    give[...] = jnp.where(first, down_z, up_z)
    for t in range(PLANES):
        for d in range(5):
            up = coll[Y_UP[d], t * 4 + 3, 7:8, :]
            down = coll[Y_DOWN[d], t * 4, 0:1, :]
            inner[d * 4 + t : d * 4 + t + 1, :] = jnp.where(first, up, down)
            outer[d * 4 + t : d * 4 + t + 1, :] = jnp.where(first, down, up)
        up = walls[t * 4 + 3, 7:8, :]
        down = walls[t * 4, 0:1, :]
        inner[20 + t : 21 + t, :] = jnp.where(first, up, down)
        outer[20 + t : 21 + t, :] = jnp.where(first, down, up)

    def own(s, _):
        partial[s] = sphere_partial(
            coll, centers[0, s], centers[1, s] & (ROWS - 1), centers[2, s] & (COLS - 1), row_f, lane_f
        )
        return 0

    lax.fori_loop(0, SLOTS, own, 0)

    def listed(r, _):
        partial[SLOTS + r] = jnp.zeros((8, COLS), jnp.float32)

        @pl.when(lists[0, r] >= 0)
        def _():
            partial[SLOTS + r] = sphere_partial(
                coll, lists[3, r], lists[1, r] + TILE // 2, lists[2, r] + TILE // 2, row_f, lane_f
            )

        return 0

    lax.fori_loop(0, 16, listed, 0)

    base = core * HALF
    tile = jnp.zeros((8, COLS), jnp.float32)
    for s in range(SLOTS):
        total = 2.0 * jnp.sum(partial[s], axis=1, keepdims=True)
        tile = jnp.where(lane == base + 4 * SLOTS + s, total, tile)
        column = jnp.zeros((8, COLS), jnp.float32)
        for r in range(8):
            column = jnp.where(row_f == float(r), state[s, r], column)
        tile = jnp.where(lane == base + STATE_LANE + s, column, tile)
        tile = jnp.where(lane == base + DEST_LANE + s, destination[s].astype(jnp.float32), tile)
    for r in range(16):
        offset = DIRECTIONS[r // 2]
        block = (offset[0] + 1) * 3 + offset[1] + 1
        total = 2.0 * jnp.sum(partial[SLOTS + r], axis=1, keepdims=True)
        slot = lists[0, r]
        at = jnp.where(slot >= 0, base + block * SLOTS + slot, -1)
        tile = jnp.where(lane == at, total, tile)
    info[...] = tile


Z_ALL = (5, 6, 11, 12, 13, 14, 15, 16, 17, 18)
Y_ONLY = (3, 4, 7, 8, 9, 10)


def stream_kernel(held, walls, out_hbm, z_part, y_part, ext, out, sems):
    wall = jnp.inf
    column = lax.broadcasted_iota(jnp.int32, (ROWS, COLS), 1)
    for t in range(PLANES):
        solid = walls[t] > 0.5
        for i in range(19):
            ext[i, t, 8 : 8 + ROWS, :] = jnp.where(solid, wall, held[i, t])
            c_y = VELOCITIES[i][1]
            if c_y == 1:
                ext[i, t, 7:8, :] = jnp.full((1, COLS), wall, jnp.float32)
            if c_y == -1:
                ext[i, t, 8 + ROWS : 9 + ROWS, :] = jnp.full((1, COLS), wall, jnp.float32)
    for t in range(PLANES):
        solid = walls[t] > 0.5
        for i in range(19):
            c_x, c_y, c_z = VELOCITIES[i]
            source = t - c_x
            if 0 <= source < PLANES:
                pulled = ext[i, source, 8 - c_y : 8 - c_y + ROWS, :]
                if c_z == 1:
                    pulled = jnp.where(column == 0, wall, pltpu.roll(pulled, 1, 1))
                if c_z == -1:
                    pulled = jnp.where(column == COLS - 1, wall, pltpu.roll(pulled, COLS - 1, 1))
                fluid = jnp.where(pulled == wall, held[OPPOSITE[i], t], pulled)
            else:
                fluid = held[OPPOSITE[i], t]
            result = jnp.where(solid, held[i, t], fluid)
            if c_z == 0:
                out[i, t] = result
            else:
                z_part[Z_ALL.index(i), t] = result
            if i in Y_ONLY:
                y_part[Y_ONLY.index(i), t] = result[0:8] if c_y == 1 else result[ROWS - 8 : ROWS]
    copies = [
        pltpu.make_async_copy(out.at[lo:hi], out_hbm.at[lo:hi], sems.at[k])
        for k, (lo, hi) in enumerate(((0, 5), (7, 11)))
    ]
    for copy in copies:
        copy.start()
    for copy in copies:
        copy.wait()


def update_kernel(
    streamed,
    z_part,
    y_part,
    walls,
    border,
    meta,
    chip,
    partner_edge,
    near_in,
    near_2,
    far_in,
    outer_in,
    inner_in,
    out_hbm,
    forces,
    state_next,
    turn,
    z_new,
    y_new,
    sems,
):
    del streamed
    lane = lax.broadcasted_iota(jnp.int32, (8, COLS), 1)
    sub = lax.broadcasted_iota(jnp.int32, (8, COLS), 0)
    row = lane & (ROWS - 1)
    plane = lax.shift_right_logical(lane, 5)
    wall = jnp.inf
    second = jnp.broadcast_to(meta[1:2, :], (8, COLS)) > 0.5

    def swap_if(a, b):
        return jnp.where(second, b, a), jnp.where(second, a, b)

    def walled(values):
        return jnp.where(values[5:6, :] > 0.5, wall, values)

    def side(here, below, above, shifts):
        total = here
        for k, (c_x, c_y) in enumerate(shifts):
            moved = here
            if c_y == 1:
                moved = jnp.where(row == 0, pltpu.roll(below, COLS - 31, 1), pltpu.roll(here, 1, 1))
            if c_y == -1:
                moved = jnp.where(
                    row == ROWS - 1, pltpu.roll(above, 31, 1), pltpu.roll(here, COLS - 1, 1)
                )
            if c_x == 1:
                moved = jnp.where(plane == 0, wall, pltpu.roll(here, 32, 1))
            if c_x == -1:
                moved = jnp.where(plane == PLANES - 1, wall, pltpu.roll(here, COLS - 32, 1))
            total = jnp.where(sub == k, moved, total)
        return total

    west, east = swap_if(walled(near_in[0:8, :]), walled(far_in[8:16, :]))
    west_partner, east_partner = swap_if(walled(near_in[8:16, :]), walled(far_in[0:8, :]))
    west_outer, east_outer = swap_if(
        walled(outer_in[EDGE_ROWS + 8 : EDGE_ROWS + 16, :]), walled(outer_in[EDGE_ROWS : EDGE_ROWS + 8, :])
    )
    west_south, west_north = swap_if(west_outer, west_partner)
    east_south, east_north = swap_if(east_outer, east_partner)
    low_solid = border[13:14, :] > 0.5
    high_solid = border[5:6, :] > 0.5
    turn[...] = jnp.zeros((COLS, COLS), jnp.float32)
    turn[0:8, :] = jnp.where(
        low_solid, wall, side(west, west_south, west_north, [VELOCITIES[i][:2] for i in Z_UP])
    )
    turn[8:16, :] = jnp.where(
        high_solid, wall, side(east, east_south, east_north, [VELOCITIES[i][:2] for i in Z_DOWN])
    )
    turned = turn[...].T
    turn[...] = turned
    pairs = [
        swap_if(outer_in[k : k + 8, :], partner_edge[k : k + 8, :]) for k in range(0, EDGE_ROWS, 8)
    ]
    south = [p[0] for p in pairs]
    north = [p[1] for p in pairs]

    def edge_row(edge, r):
        return edge[r // 8][r % 8 : r % 8 + 1, :]

    def border_row(i, t):
        c_x, c_y, _ = VELOCITIES[i]
        edge, order, cells = (
            (south, Y_UP, walls[t, 0:1, :]) if c_y == 1 else (north, Y_DOWN, walls[t, ROWS - 1 : ROWS, :])
        )
        values = edge_row(edge, order.index(i) * 4 + t - c_x)
        return jnp.where(edge_row(edge, 20 + t - c_x) > 0.5, wall, values), cells > 0.5

    def mended(tile, i, values):
        changed = (sub == (0 if VELOCITIES[i][1] == 1 else 7)) & (values != wall)
        return jnp.where(changed, values, tile)

    column = lax.broadcasted_iota(jnp.int32, (ROWS, COLS), 1)
    first_lane = lax.broadcasted_iota(jnp.int32, (1, COLS), 1)
    copies = []

    def send(source, target):
        copies.append(pltpu.make_async_copy(source, target, sems.at[len(copies)]))
        copies[-1].start()

    for z, i in enumerate(Z_ALL):
        _, c_y, c_z = VELOCITIES[i]
        k = Z_UP.index(i) if c_z == 1 else 8 + Z_DOWN.index(i)
        edge = 0 if c_z == 1 else COLS - 1
        for t in range(PLANES):
            entering = turn[t * ROWS : (t + 1) * ROWS, k : k + 1]
            values = jnp.where((column == edge) & (entering != wall), entering, z_part[z, t])
            z_new[z, t] = values
            if c_y != 0:
                values_in, solid = border_row(i, t)
                values_in = pltpu.roll(values_in, 1 if c_z == 1 else COLS - 1, 1)
                values_in = jnp.where(solid | (first_lane == edge), wall, values_in)
                at = 0 if c_y == 1 else ROWS - 8
                z_new[z, t, at : at + 8, :] = mended(values[at : at + 8], i, values_in)
        if z == 1:
            send(z_new.at[0:2], out_hbm.at[5:7])
        if z == 5:
            send(z_new.at[2:6], out_hbm.at[11:15])
        if z == 9:
            send(z_new.at[6:10], out_hbm.at[15:19])
    for y, i in enumerate(Y_ONLY):
        c_x, c_y, _ = VELOCITIES[i]
        for t in range(PLANES):
            tile = y_part[y, t]
            if 0 <= t - c_x < PLANES:
                values_in, solid = border_row(i, t)
                tile = mended(tile, i, jnp.where(solid, wall, values_in))
            y_new[y, t] = tile
        at = 0 if c_y == 1 else ROWS - 8
        send(y_new.at[y], out_hbm.at[i, :, at : at + 8])

    middle = {0: chip[...]}
    middle[-1], middle[1] = swap_if(near_in[16:24, :], far_in[16:24, :])
    middle[-2], middle[2] = swap_if(near_2[...], far_in[24:32, :])
    arrived = []
    for ref, start in ((outer_in, EDGE_ROWS + 16), (inner_in, 0)):
        group = [ref[start + 8 * k : start + 8 * k + 8, :] for k in range(5)]
        columns = {0: group[0]}
        columns[-1], columns[1] = swap_if(group[3], group[1])
        columns[-2], columns[2] = swap_if(group[4], group[2])
        arrived.append(columns)
    tiles = {}
    low = lane < HALF
    for b in range(-2, 3):
        before, after = swap_if(arrived[0][b], arrived[1][b])
        turned_before, turned_own, turned_after = (
            pltpu.roll(part, HALF, 1) for part in (before, middle[b], after)
        )
        tiles[0, b] = jnp.where(second, jnp.where(low, turned_before, turned_own), before)
        tiles[1, b] = jnp.where(second, jnp.where(low, turned_own, turned_after), middle[b])
        tiles[2, b] = jnp.where(second, turned_after, after)

    def device_lanes(a, b, at):
        shift = (COLS - (at + HALF * (a % 2))) % COLS
        part = tiles[(a + 2) // 2, b]
        return pltpu.roll(part, shift, 1) if shift else part

    own_lanes = lane < SLOTS
    picked = [jnp.zeros((8, COLS), jnp.float32) for _ in range(SLOTS)]
    for a in (-1, 0, 1):
        for b in (-1, 0, 1):
            force = jnp.zeros((8, COLS), jnp.float32)
            for e in (-1, 0, 1):
                for g in (-1, 0, 1):
                    block = (1 - e) * 3 + 1 - g
                    force = force + device_lanes(a + e, b + g, block * SLOTS)
            if a == 0 and b == 0:
                own_force = force
            record = device_lanes(a, b, STATE_LANE)
            target = device_lanes(a, b, DEST_LANE)[0:1, :]
            mass = record[6:7, :] * (3.0 / (4.0 * math.pi * RADIUS * RADIUS * RADIUS))
            spin = mass * record[7:8, :] * (1.0 / (RADIUS * RADIUS))
            gain = jnp.where(sub < 3, force * mass, jnp.where(sub < 6, force * spin, 0.0))
            updated = record + gain
            for j in range(SLOTS):
                wanted = meta[0:1, :] + float(j)
                picked[j] = picked[j] + jnp.where(own_lanes & (target == wanted), updated, 0.0)
    result = jnp.zeros((8, COLS), jnp.float32)
    for j in range(SLOTS):
        result = jnp.where(lane == j, jnp.sum(picked[j], axis=1, keepdims=True), result)
    turn[0:8, :] = result
    turn[8:16, :] = own_force
    turned = turn[...].T
    state_next[...] = turned[0:SLOTS, 0:8]
    forces[...] = turned[0:SLOTS, 8:14]
    for copy in copies:
        copy.wait()


VMEM = pl.BlockSpec(memory_space=pltpu.VMEM)
HBM = pl.BlockSpec(memory_space=pltpu.HBM)


def f32(*shape):
    return jax.ShapeDtypeStruct(shape, jnp.float32)


def in_hbm(array):
    return pltpu.with_memory_space_constraint(array, pltpu.HBM)


def swapped(block, distance):
    count = lax.axis_size("gy")
    route = [(p, (p + (distance if p % 2 == 0 else -distance)) % count) for p in range(count)]
    return lax.ppermute(block, "gy", route)


def spread(block, distance):
    count_y, count_z = lax.axis_size("gy"), lax.axis_size("gz")
    route = []
    for p in range(count_y):
        step = distance if p % 2 == 0 else -distance
        route += [(p * count_z + q, p * count_z + (q + step) % count_z) for q in range(count_z)]
    return lax.ppermute(block, ("gy", "gz"), route)


def on_device(populations, solid_mask, centers, tile_lists, sphere_state, destination, relax_rates):
    held, walls, keep, give, info, inner, outer, border, meta = pl.pallas_call(
        collide_kernel,
        out_shape=(
            f32(19, GROUPS, 8, COLS),
            f32(GROUPS, 8, COLS),
            f32(8, COLS),
            f32(8, COLS),
            f32(8, COLS),
            f32(EDGE_ROWS, COLS),
            f32(EDGE_ROWS, COLS),
            f32(16, COLS),
            f32(8, COLS),
        ),
        in_specs=[HBM] * 7,
        out_specs=(VMEM,) * 9,
        scratch_shapes=[
            pltpu.VMEM((19, GROUPS, 8, COLS), jnp.float32),
            pltpu.VMEM((GROUPS, 8, COLS), jnp.int32),
            pltpu.SMEM((SLOTS, 8), jnp.float32),
            pltpu.SMEM((3, SLOTS), jnp.int32),
            pltpu.SMEM((4, 16), jnp.int32),
            pltpu.SMEM((SLOTS,), jnp.int32),
            pltpu.SMEM((19,), jnp.float32),
            pltpu.VMEM((19, GROUPS, 8, COLS), jnp.float32),
            pltpu.VMEM((N_COEF, 8, COLS), jnp.float32),
            pltpu.VMEM((COLS, COLS), jnp.float32),
            pltpu.VMEM((20, 8, COLS), jnp.float32),
            pltpu.SemaphoreType.DMA((10,)),
        ],
        compiler_params=pltpu.CompilerParams(vmem_limit_bytes=32 * 1024 * 1024),
        name="collide",
    )(
        in_hbm(populations.reshape(19, GROUPS, 8, COLS)),
        in_hbm(solid_mask.reshape(GROUPS, 8, COLS)),
        in_hbm(sphere_state.T),
        in_hbm(centers),
        in_hbm(tile_lists.T),
        in_hbm(destination),
        in_hbm(relax_rates),
    )
    partner = swapped(jnp.concatenate([give, info, inner]), 1)
    chip = info + partner[8:16]
    near_2 = spread(chip, 2)
    near = spread(jnp.concatenate([keep, partner[0:8], chip]), 1)
    far = swapped(jnp.concatenate([near, near_2]), 1)
    spheres = [chip, near[16:24], near_2, far[16:32]]
    from_outer = swapped(jnp.concatenate([outer, near[0:8], far[8:16]] + spheres), -1)
    from_inner = swapped(jnp.concatenate(spheres), 3)
    walls = walls.reshape(PLANES, ROWS, COLS)
    streamed, z_part, y_part = pl.pallas_call(
        stream_kernel,
        out_shape=(
            f32(19, PLANES, ROWS, COLS),
            f32(10, PLANES, ROWS, COLS),
            f32(6, PLANES, 8, COLS),
        ),
        in_specs=[VMEM] * 2,
        out_specs=(HBM, VMEM, VMEM),
        scratch_shapes=[
            pltpu.VMEM((19, PLANES, ROWS + 16, COLS), jnp.float32),
            pltpu.VMEM((11, PLANES, ROWS, COLS), jnp.float32),
            pltpu.SemaphoreType.DMA((2,)),
        ],
        compiler_params=pltpu.CompilerParams(vmem_limit_bytes=32 * 1024 * 1024),
        cost_estimate=pl.CostEstimate(flops=4_000_000, bytes_accessed=4_000_000, transcendentals=0),
        name="stream",
    )(held.reshape(19, PLANES, ROWS, COLS), walls)
    populations_next, forces, state_next = pl.pallas_call(
        update_kernel,
        out_shape=(f32(19, PLANES, ROWS, COLS), f32(SLOTS, 6), f32(SLOTS, 8)),
        in_specs=[HBM] + [VMEM] * 12,
        out_specs=(HBM, VMEM, VMEM),
        scratch_shapes=[
            pltpu.VMEM((COLS, COLS), jnp.float32),
            pltpu.VMEM((10, PLANES, ROWS, COLS), jnp.float32),
            pltpu.VMEM((6, PLANES, 8, COLS), jnp.float32),
            pltpu.SemaphoreType.DMA((9,)),
        ],
        input_output_aliases={0: 0},
        compiler_params=pltpu.CompilerParams(vmem_limit_bytes=32 * 1024 * 1024),
        name="update",
    )(
        in_hbm(streamed),
        z_part,
        y_part,
        walls,
        border,
        meta,
        chip,
        partner[16:40],
        near,
        near_2,
        far,
        from_outer,
        from_inner,
    )
    return populations_next, forces.T, state_next.T


def solution(mesh):
    return jax.shard_map(
        on_device,
        mesh=mesh,
        in_specs=(
            P(None, None, "gy", "gz"),
            P(None, "gy", "gz"),
            P(None, ("gy", "gz")),
            P(("gy", "gz"), None),
            P(None, ("gy", "gz")),
            P(("gy", "gz")),
            P(),
        ),
        out_specs=(P(None, None, "gy", "gz"), P(None, ("gy", "gz")), P(None, ("gy", "gz"))),
        check_vma=False,
    )
```

```python
import math

import jax
import jax.numpy as jnp
import numpy as np
from jax import lax
from jax.experimental import pallas as pl
from jax.experimental.pallas import tpu as pltpu
from jax.sharding import PartitionSpec as P

TILE = 16
RADIUS = 6
PLANES = 4
ROWS = 32
COLS = 128
SLOTS = 4
GROUPS = PLANES * ROWS // 8

VELOCITIES = (
    (0, 0, 0),
    (1, 0, 0),
    (-1, 0, 0),
    (0, 1, 0),
    (0, -1, 0),
    (0, 0, 1),
    (0, 0, -1),
    (1, 1, 0),
    (-1, -1, 0),
    (1, -1, 0),
    (-1, 1, 0),
    (1, 0, 1),
    (-1, 0, -1),
    (1, 0, -1),
    (-1, 0, 1),
    (0, 1, 1),
    (0, -1, -1),
    (0, 1, -1),
    (0, -1, 1),
)
OPPOSITE = (0, 2, 1, 4, 3, 6, 5, 8, 7, 10, 9, 12, 11, 14, 13, 16, 15, 18, 17)
EXPONENTS = (
    (0, 0, 0),
    (1, 0, 0),
    (0, 1, 0),
    (0, 0, 1),
    (2, 0, 0),
    (0, 2, 0),
    (0, 0, 2),
    (1, 1, 0),
    (1, 0, 1),
    (0, 1, 1),
    (1, 2, 0),
    (1, 0, 2),
    (2, 1, 0),
    (0, 1, 2),
    (2, 0, 1),
    (0, 2, 1),
    (2, 2, 0),
    (2, 0, 2),
    (0, 2, 2),
)
DIRECTIONS = ((-1, -1), (-1, 0), (-1, 1), (0, -1), (0, 1), (1, -1), (1, 0), (1, 1))

Z_UP = (5, 11, 14, 15, 18)
Z_DOWN = (6, 12, 13, 16, 17)
Y_UP = (3, 7, 10, 15, 17)
Y_DOWN = (4, 8, 9, 16, 18)
CLASS_MEMBER = (0, 1, 3, 5, 7, 11, 15)
EVEN_MOMENTS = (0, 4, 5, 6, 16, 17, 18)
ODD_MOMENTS = ((1, 10, 11), (2, 12, 13), (3, 14, 15))
ODD_CLASSES = ((1, 4, 5), (2, 4, 6), (3, 5, 6))
CROSS_MOMENTS = (7, 8, 9)
STATE_LANE = 40
DEST_LANE = 48
HALF = 64
EDGE_ROWS = 24


def moment_basis():
    velocity = np.array(VELOCITIES, dtype=np.float64)
    moment_rows = []
    for a, b, e in EXPONENTS:
        vector = velocity[:, 0] ** a * velocity[:, 1] ** b * velocity[:, 2] ** e
        for earlier in moment_rows:
            vector = vector - np.dot(earlier, vector) * earlier
        moment_rows.append(vector / np.sqrt(np.dot(vector, vector)))
    return np.array(moment_rows)


BASIS = moment_basis()


def store_coefficients(rates, coef):
    splat = [jnp.full((8, COLS), rates[k], jnp.float32) for k in range(19)]
    at = 0
    for a in range(7):
        for b in range(a, 7):
            total = None
            for k in EVEN_MOMENTS:
                c = float(BASIS[k, CLASS_MEMBER[a]] * BASIS[k, CLASS_MEMBER[b]])
                if abs(c) > 1e-12:
                    total = c * splat[k] if total is None else total + c * splat[k]
            coef[at] = total
            at += 1
    for axis in range(3):
        for a in range(3):
            for b in range(a, 3):
                total = None
                for k in ODD_MOMENTS[axis]:
                    c = float(
                        BASIS[k, CLASS_MEMBER[ODD_CLASSES[axis][a]]]
                        * BASIS[k, CLASS_MEMBER[ODD_CLASSES[axis][b]]]
                    )
                    if abs(c) > 1e-12:
                        total = c * splat[k] if total is None else total + c * splat[k]
                coef[at] = total
                at += 1
    for axis in range(3):
        c = float(BASIS[CROSS_MOMENTS[axis], CLASS_MEMBER[4 + axis]] ** 2)
        coef[at] = c * splat[CROSS_MOMENTS[axis]]
        at += 1


N_COEF = 28 + 18 + 3


def collide(f, coef):
    even_at = {}
    at = 0
    for a in range(7):
        for b in range(a, 7):
            even_at[a, b] = even_at[b, a] = at
            at += 1
    odd_at = []
    for _ in range(3):
        table = {}
        for a in range(3):
            for b in range(a, 3):
                table[a, b] = table[b, a] = at
                at += 1
        odd_at.append(table)
    cross_at = at

    def split(i):
        ab, amb = f[i] + f[i + 1], f[i] - f[i + 1]
        cd, cmd = f[i + 2] + f[i + 3], f[i + 2] - f[i + 3]
        return ab + cd, ab - cd, amb + cmd, amb - cmd

    s_xy, q_xy, xy_x, xy_y = split(7)
    s_xz, q_xz, xz_x, xz_z = split(11)
    s_yz, q_yz, yz_y, yz_z = split(15)
    s_x, s_y, s_z = f[1] + f[2], f[3] + f[4], f[5] + f[6]
    d_x, d_y, d_z = f[1] - f[2], f[3] - f[4], f[5] - f[6]
    rho = ((f[0] + s_x) + (s_y + s_z)) + ((s_xy + s_xz) + s_yz)
    j_x = d_x + (xy_x + xz_x)
    j_y = d_y + (xy_y + yz_y)
    j_z = d_z + (xz_z + yz_z)
    inverse = 1.0 / rho
    u_x, u_y, u_z = j_x * inverse, j_y * inverse, j_z * inverse
    e_x, e_y, e_z = j_x * u_x, j_y * u_y, j_z * u_z
    base = (rho - 1.5 * ((e_x + e_y) + e_z)) * (1.0 / 9.0)
    h_x, h_y, h_z = 0.5 * e_x, 0.5 * e_y, 0.5 * e_z
    even = (
        f[0] - 3.0 * base,
        s_x - (base + h_x),
        s_y - (base + h_y),
        s_z - (base + h_z),
        s_xy - (base + (h_x + h_y)),
        s_xz - (base + (h_x + h_z)),
        s_yz - (base + (h_y + h_z)),
    )
    third = 1.0 / 3.0
    t_x, t_y, t_z = third * j_x, third * j_y, third * j_z
    odd = (
        (d_x - t_x, xy_x - t_x, xz_x - t_x),
        (d_y - t_y, xy_y - t_y, yz_y - t_y),
        (d_z - t_z, xz_z - t_z, yz_z - t_z),
    )
    cross = (
        (q_xy - j_x * u_y) * coef[cross_at],
        (q_xz - j_x * u_z) * coef[cross_at + 1],
        (q_yz - j_y * u_z) * coef[cross_at + 2],
    )

    def apply(vector, table, n):
        out = []
        for a in range(n):
            terms = [coef[table[a, b]] * vector[b] for b in range(n)]
            while len(terms) > 1:
                terms = [
                    terms[i] + terms[i + 1] if i + 1 < len(terms) else terms[i]
                    for i in range(0, len(terms), 2)
                ]
            out.append(terms[0])
        return out

    ev = apply(even, even_at, 7)
    ox, oy, oz = (apply(odd[axis], odd_at[axis], 3) for axis in range(3))
    new = [f[0] - ev[0]]
    for axis, o in enumerate((ox, oy, oz)):
        i = 1 + 2 * axis
        new += [f[i] - (ev[1 + axis] + o[0]), f[i + 1] - (ev[1 + axis] - o[0])]
    for axis, (a, b) in enumerate(((ox[1], oy[1]), (ox[2], oz[1]), (oy[2], oz[2]))):
        i = 7 + 4 * axis
        plus, minus = ev[4 + axis] + cross[axis], ev[4 + axis] - cross[axis]
        both, differ = a + b, a - b
        new += [
            f[i] - (plus + both),
            f[i + 1] - (plus - both),
            f[i + 2] - (minus + differ),
            f[i + 3] - (minus - differ),
        ]
    return new


def sphere_partial(coll, partial, at, center_x, center_y, center_z, row_f, lane_f):
    first = jnp.maximum(lax.shift_right_arithmetic(center_y - (RADIUS + 1), 3), 0)
    last = jnp.minimum(lax.shift_right_arithmetic(center_y + (RADIUS + 1), 3), ROWS // 8 - 1)
    x_f = center_x.astype(jnp.float32)
    r_z = lane_f - center_z.astype(jnp.float32)
    z_sq = r_z * r_z
    zero = jnp.zeros((8, COLS), jnp.float32)

    def row_tile(tile, carry):
        f_x, f_y, f_z, t_x, t_y, t_z = carry
        r_y = row_f + (tile * 8 - center_y).astype(jnp.float32)
        yz_sq = r_y * r_y + z_sq
        p_x, p_y, p_z, x_py, x_pz = zero, zero, zero, zero, zero
        y_plus_z, y_minus_z = r_y + r_z, r_y - r_z
        for t in range(PLANES):
            r_x = t - x_f
            dist = yz_sq + r_x * r_x
            outside = dist > float(RADIUS * RADIUS)
            half = jnp.where(outside, (RADIUS * RADIUS - 1.0) * 0.5 - 0.5 * dist, -1e9)
            half_2 = half - 0.5
            limits = {1: (half, -half), 2: (half_2, -half_2)}

            def linked(i, along, kind):
                limit, negative = limits[kind]
                up, down = VELOCITIES[i][0], VELOCITIES[i + 1][0]
                total = None
                if 0 <= t + up < PLANES:
                    total = jnp.where(along <= limit, coll[i, t * 4 + tile], 0.0)
                if 0 <= t + down < PLANES:
                    back = jnp.where(along >= negative, coll[i + 1, t * 4 + tile], 0.0)
                    total = -back if total is None else total - back
                return total

            l_x = linked(1, r_x, 1)
            l_y = linked(3, r_y, 1)
            l_z = linked(5, r_z, 1)
            l_xy = linked(7, r_y + r_x, 2)
            l_xmy = linked(9, r_x - r_y, 2)
            l_xz = linked(11, r_z + r_x, 2)
            l_xmz = linked(13, r_x - r_z, 2)
            l_yz = linked(15, y_plus_z, 2)
            l_ymz = linked(17, y_minus_z, 2)
            m_x = l_x + ((l_xy + l_xmy) + (l_xz + l_xmz))
            m_y = l_y + ((l_xy - l_xmy) + (l_yz + l_ymz))
            m_z = l_z + ((l_xz - l_xmz) + (l_yz - l_ymz))
            p_x, p_y, p_z = p_x + m_x, p_y + m_y, p_z + m_z
            x_py, x_pz = x_py + r_x * m_y, x_pz + r_x * m_z
        return (
            f_x + p_x,
            f_y + p_y,
            f_z + p_z,
            t_x + (r_y * p_z - r_z * p_y),
            t_y + (r_z * p_x - x_pz),
            t_z + (x_py - r_y * p_x),
        )

    sums = lax.fori_loop(first, last + 1, row_tile, (zero,) * 6)
    for j in range(6):
        partial[at, j] = sums[j]


def summed(partial, at, row_f):
    packed = jnp.zeros((8, COLS), jnp.float32)
    for j in range(6):
        packed = jnp.where(row_f == float(j), jnp.sum(partial[at, j], axis=0, keepdims=True), packed)
    return 2.0 * jnp.sum(packed, axis=1, keepdims=True)


def collide_kernel(
    pops_in,
    mask_in,
    state_in,
    centers_in,
    lists_in,
    destination_in,
    rates_in,
    held,
    walls,
    keep,
    give,
    info,
    inner,
    outer,
    border,
    meta,
    pops,
    mask,
    state,
    centers,
    lists,
    destination,
    rates,
    coll,
    coef,
    turn,
    partial,
    sems,
):
    small = [
        pltpu.make_async_copy(source, target, sems.at[4 + k])
        for k, (source, target) in enumerate(
            (
                (rates_in, rates),
                (mask_in, mask),
                (centers_in, centers),
                (lists_in, lists),
                (destination_in, destination),
                (state_in, state),
            )
        )
    ]
    large = [
        pltpu.make_async_copy(
            pops_in.at[:, pl.ds(t * 4, 4)], pops.at[:, pl.ds(t * 4, 4)], sems.at[t]
        )
        for t in range(PLANES)
    ]
    small[0].start()
    small[1].start()
    for copy in large:
        copy.start()
    for copy in small[2:]:
        copy.start()
    lane = lax.broadcasted_iota(jnp.int32, (8, COLS), 1)
    lane_f = lane.astype(jnp.float32)
    row_f = lax.broadcasted_iota(jnp.int32, (8, COLS), 0).astype(jnp.float32)
    small[0].wait()
    store_coefficients(rates, coef)
    small[1].wait()

    def group(g, _):
        f = [pops[i, g] for i in range(19)]
        solid = mask[g] > 0
        flag = solid.astype(jnp.float32)
        walls[g] = flag
        new = collide(f, coef)
        for i in range(19):
            coll[i, g] = new[i]
            held[i, g] = jnp.where(solid, f[i], new[i])
        return 0

    for t in range(PLANES):
        large[t].wait()
        lax.fori_loop(t * 4, t * 4 + 4, group, 0)
    for copy in small[2:]:
        copy.wait()

    device_y = lax.shift_right_logical(centers[1, 0], 5)
    device_z = lax.shift_right_logical(centers[2, 0], 7)
    core = device_y & 1
    first = core == 0
    meta[0:1, :] = jnp.full((1, COLS), (device_y * 16 + device_z) * SLOTS, jnp.int32).astype(
        jnp.float32
    )
    meta[1:2, :] = jnp.full((1, COLS), core, jnp.int32).astype(jnp.float32)
    meta[2:8, :] = jnp.zeros((6, COLS), jnp.float32)

    for g in range(GROUPS):
        edge = jnp.zeros((8, COLS), jnp.float32)
        for k in range(6):
            values = coll[Z_UP[k], g] if k < 5 else walls[g]
            edge = jnp.where(lane == k, pltpu.roll(values, k + 1, 1), edge)
        for k in range(6):
            values = coll[Z_DOWN[k], g] if k < 5 else walls[g]
            edge = jnp.where(lane == 8 + k, pltpu.roll(values, 8 + k, 1), edge)
        turn[g * 8 : g * 8 + 8, :] = edge
    turned = turn[...].T
    up_z, down_z = turned[0:8, :], turned[8:16, :]
    border[...] = turned[0:16, :]
    keep[...] = jnp.where(first, up_z, down_z)
    give[...] = jnp.where(first, down_z, up_z)
    for t in range(PLANES):
        for d in range(5):
            up = coll[Y_UP[d], t * 4 + 3, 7:8, :]
            down = coll[Y_DOWN[d], t * 4, 0:1, :]
            inner[d * 4 + t : d * 4 + t + 1, :] = jnp.where(first, up, down)
            outer[d * 4 + t : d * 4 + t + 1, :] = jnp.where(first, down, up)
        up = walls[t * 4 + 3, 7:8, :]
        down = walls[t * 4, 0:1, :]
        inner[20 + t : 21 + t, :] = jnp.where(first, up, down)
        outer[20 + t : 21 + t, :] = jnp.where(first, down, up)

    def own(s, _):
        sphere_partial(
            coll,
            partial,
            s,
            centers[0, s],
            centers[1, s] & (ROWS - 1),
            centers[2, s] & (COLS - 1),
            row_f,
            lane_f,
        )
        return 0

    partial[SLOTS:] = jnp.zeros((16, 6, 8, COLS), jnp.float32)
    lax.fori_loop(0, SLOTS, own, 0)

    def listed(r, _):
        @pl.when(lists[0, r] >= 0)
        def _():
            sphere_partial(
                coll,
                partial,
                SLOTS + r,
                lists[3, r],
                lists[1, r] + TILE // 2,
                lists[2, r] + TILE // 2,
                row_f,
                lane_f,
            )

        return 0

    lax.fori_loop(0, 16, listed, 0)

    base = core * HALF
    tile = jnp.zeros((8, COLS), jnp.float32)
    for s in range(SLOTS):
        total = summed(partial, s, row_f)
        tile = jnp.where(lane == base + 4 * SLOTS + s, total, tile)
        column = jnp.zeros((8, COLS), jnp.float32)
        for r in range(8):
            column = jnp.where(row_f == float(r), state[s, r], column)
        tile = jnp.where(lane == base + STATE_LANE + s, column, tile)
        tile = jnp.where(lane == base + DEST_LANE + s, destination[s].astype(jnp.float32), tile)
    for r in range(16):
        offset = DIRECTIONS[r // 2]
        block = (offset[0] + 1) * 3 + offset[1] + 1
        total = summed(partial, SLOTS + r, row_f)
        slot = lists[0, r]
        at = jnp.where(slot >= 0, base + block * SLOTS + slot, -1)
        tile = jnp.where(lane == at, total, tile)
    info[...] = tile


Y_ALL = (3, 4, 7, 8, 9, 10, 15, 16, 17, 18)


def select_by(meta):
    second = jnp.broadcast_to(meta[1:2, :], (8, COLS)) > 0.5

    def swap_if(a, b):
        return jnp.where(second, b, a), jnp.where(second, a, b)

    return second, swap_if


def walled(values):
    return jnp.where(values[5:6, :] > 0.5, jnp.inf, values)


def stream_kernel(
    held, walls, border, meta, near_in, far_in, out_hbm, y_part, ext, turn, out, sems
):
    wall = jnp.inf
    _, swap_if = select_by(meta)
    lane = lax.broadcasted_iota(jnp.int32, (8, COLS), 1)
    sub = lax.broadcasted_iota(jnp.int32, (8, COLS), 0)
    row = lane & (ROWS - 1)
    plane = lax.shift_right_logical(lane, 5)

    def side(here, order):
        total = here
        for k, i in enumerate(order):
            c_x, c_y, _ = VELOCITIES[i]
            moved = here
            if c_y == 1:
                moved = jnp.where(row == 0, wall, pltpu.roll(here, 1, 1))
            if c_y == -1:
                moved = jnp.where(row == ROWS - 1, wall, pltpu.roll(here, COLS - 1, 1))
            if c_x == 1:
                moved = jnp.where(plane == 0, wall, pltpu.roll(here, 32, 1))
            if c_x == -1:
                moved = jnp.where(plane == PLANES - 1, wall, pltpu.roll(here, COLS - 32, 1))
            total = jnp.where(sub == k, moved, total)
        return total

    west, east = swap_if(walled(near_in[0:8, :]), walled(far_in[8:16, :]))
    turn[...] = jnp.zeros((COLS, COLS), jnp.float32)
    turn[0:8, :] = side(west, Z_UP)
    turn[8:16, :] = side(east, Z_DOWN)
    turned = turn[...].T
    turn[...] = turned
    column = lax.broadcasted_iota(jnp.int32, (ROWS, COLS), 1)
    for t in range(PLANES):
        solid = walls[t] > 0.5
        for i in range(19):
            ext[i, t, 8 : 8 + ROWS, :] = jnp.where(solid, wall, held[i, t])
            c_y = VELOCITIES[i][1]
            if c_y == 1:
                ext[i, t, 7:8, :] = jnp.full((1, COLS), wall, jnp.float32)
            if c_y == -1:
                ext[i, t, 8 + ROWS : 9 + ROWS, :] = jnp.full((1, COLS), wall, jnp.float32)
    copies = []
    for t in range(PLANES):
        solid = walls[t] > 0.5
        for i in range(19):
            c_x, c_y, c_z = VELOCITIES[i]
            source = t - c_x
            if 0 <= source < PLANES:
                pulled = ext[i, source, 8 - c_y : 8 - c_y + ROWS, :]
                if c_z != 0:
                    k = Z_UP.index(i) if c_z == 1 else 8 + Z_DOWN.index(i)
                    pulled = jnp.where(
                        column == (0 if c_z == 1 else COLS - 1),
                        turn[t * ROWS : (t + 1) * ROWS, k : k + 1],
                        pltpu.roll(pulled, 1 if c_z == 1 else COLS - 1, 1),
                    )
                fluid = jnp.where(pulled == wall, held[OPPOSITE[i], t], pulled)
            else:
                fluid = held[OPPOSITE[i], t]
            result = jnp.where(solid, held[i, t], fluid)
            out[i, t] = result
            if i in Y_ALL:
                y_part[Y_ALL.index(i), t] = result[0:8] if c_y == 1 else result[ROWS - 8 : ROWS]
        copies.append(pltpu.make_async_copy(out.at[:, t], out_hbm.at[:, t], sems.at[t]))
        copies[t].start()
    for copy in copies:
        copy.wait()


def update_kernel(
    streamed,
    y_part,
    walls,
    meta,
    chip,
    partner_edge,
    near_in,
    near_2,
    far_in,
    outer_in,
    inner_in,
    out_hbm,
    forces_hbm,
    state_hbm,
    turn,
    y_new,
    forces,
    state_next,
    sems,
):
    del streamed
    lane = lax.broadcasted_iota(jnp.int32, (8, COLS), 1)
    sub = lax.broadcasted_iota(jnp.int32, (8, COLS), 0)
    wall = jnp.inf
    second, swap_if = select_by(meta)
    west_partner, east_partner = swap_if(walled(near_in[8:16, :]), walled(far_in[0:8, :]))
    west_outer, east_outer = swap_if(
        walled(outer_in[EDGE_ROWS + 8 : EDGE_ROWS + 16, :]), walled(outer_in[EDGE_ROWS : EDGE_ROWS + 8, :])
    )
    west_south, west_north = swap_if(west_outer, west_partner)
    east_south, east_north = swap_if(east_outer, east_partner)
    pairs = [
        swap_if(outer_in[k : k + 8, :], partner_edge[k : k + 8, :]) for k in range(0, EDGE_ROWS, 8)
    ]
    south = [p[0] for p in pairs]
    north = [p[1] for p in pairs]

    def edge_row(edge, r):
        return edge[r // 8][r % 8 : r % 8 + 1, :]

    first_lane = lax.broadcasted_iota(jnp.int32, (1, COLS), 1)
    copies = []

    def send(source, target):
        copies.append(pltpu.make_async_copy(source, target, sems.at[len(copies)]))
        copies[-1].start()

    for y, i in enumerate(Y_ALL):
        c_x, c_y, c_z = VELOCITIES[i]
        edge, order = (south, Y_UP) if c_y == 1 else (north, Y_DOWN)
        for t in range(PLANES):
            source = t - c_x
            if not 0 <= source < PLANES:
                y_new[y, t] = y_part[y, t]
                continue
            values = edge_row(edge, order.index(i) * 4 + source)
            values = jnp.where(edge_row(edge, 20 + source) > 0.5, wall, values)
            if c_z != 0:
                if c_z == 1:
                    corner, k = (west_south if c_y == 1 else west_north), Z_UP.index(i)
                else:
                    corner, k = (east_south if c_y == 1 else east_north), Z_DOWN.index(i)
                at = t * ROWS + (ROWS - 1 if c_y == 1 else 0)
                to = 0 if c_z == 1 else COLS - 1
                values = jnp.where(
                    first_lane == to,
                    pltpu.roll(corner, (to - at) % COLS, 1)[k : k + 1, :],
                    pltpu.roll(values, 1 if c_z == 1 else COLS - 1, 1),
                )
            cells = walls[t, 0:1, :] if c_y == 1 else walls[t, ROWS - 1 : ROWS, :]
            values = jnp.where(cells > 0.5, wall, values)
            changed = (sub == (0 if c_y == 1 else 7)) & (values != wall)
            y_new[y, t] = jnp.where(changed, values, y_part[y, t])
        at = 0 if c_y == 1 else ROWS - 8
        send(y_new.at[y], out_hbm.at[i, :, at : at + 8])

    middle = {0: chip[...]}
    middle[-1], middle[1] = swap_if(near_in[16:24, :], far_in[16:24, :])
    middle[-2], middle[2] = swap_if(near_2[...], far_in[24:32, :])
    arrived = []
    for ref, start in ((outer_in, EDGE_ROWS + 16), (inner_in, 0)):
        group = [ref[start + 8 * k : start + 8 * k + 8, :] for k in range(5)]
        columns = {0: group[0]}
        columns[-1], columns[1] = swap_if(group[3], group[1])
        columns[-2], columns[2] = swap_if(group[4], group[2])
        arrived.append(columns)
    tiles = {}
    low = lane < HALF
    for b in range(-2, 3):
        before, after = swap_if(arrived[0][b], arrived[1][b])
        turned_before, turned_own, turned_after = (
            pltpu.roll(part, HALF, 1) for part in (before, middle[b], after)
        )
        tiles[0, b] = jnp.where(second, jnp.where(low, turned_before, turned_own), before)
        tiles[1, b] = jnp.where(second, jnp.where(low, turned_own, turned_after), middle[b])
        tiles[2, b] = jnp.where(second, turned_after, after)

    def device_lanes(a, b, at):
        shift = (COLS - (at + HALF * (a % 2))) % COLS
        part = tiles[(a + 2) // 2, b]
        return pltpu.roll(part, shift, 1) if shift else part

    own_lanes = lane < SLOTS
    picked = [jnp.zeros((8, COLS), jnp.float32) for _ in range(SLOTS)]
    for a in (-1, 0, 1):
        for b in (-1, 0, 1):
            force = jnp.zeros((8, COLS), jnp.float32)
            for e in (-1, 0, 1):
                for g in (-1, 0, 1):
                    block = (1 - e) * 3 + 1 - g
                    force = force + device_lanes(a + e, b + g, block * SLOTS)
            if a == 0 and b == 0:
                own_force = force
            record = device_lanes(a, b, STATE_LANE)
            target = device_lanes(a, b, DEST_LANE)[0:1, :]
            mass = record[6:7, :] * (3.0 / (4.0 * math.pi * RADIUS * RADIUS * RADIUS))
            spin = mass * record[7:8, :] * (1.0 / (RADIUS * RADIUS))
            gain = jnp.where(sub < 3, force * mass, jnp.where(sub < 6, force * spin, 0.0))
            updated = record + gain
            for j in range(SLOTS):
                wanted = meta[0:1, :] + float(j)
                picked[j] = picked[j] + jnp.where(own_lanes & (target == wanted), updated, 0.0)
    result = jnp.zeros((8, COLS), jnp.float32)
    for j in range(SLOTS):
        result = jnp.where(lane == j, jnp.sum(picked[j], axis=1, keepdims=True), result)
    turn[0:8, :] = result
    turn[8:16, :] = own_force
    turned = turn[...].T
    state_next[...] = turned[0:SLOTS, 0:8]
    forces[...] = turned[0:SLOTS, 8:14]
    send(state_next, state_hbm)
    send(forces, forces_hbm)
    for copy in copies:
        copy.wait()


VMEM = pl.BlockSpec(memory_space=pltpu.VMEM)
HBM = pl.BlockSpec(memory_space=pltpu.HBM)


def f32(*shape):
    return jax.ShapeDtypeStruct(shape, jnp.float32)


def in_hbm(array):
    return pltpu.with_memory_space_constraint(array, pltpu.HBM)


def swapped(block, distance):
    count = lax.axis_size("gy")
    route = [(p, (p + (distance if p % 2 == 0 else -distance)) % count) for p in range(count)]
    return lax.ppermute(block, "gy", route)


def spread(block, distance):
    count_y, count_z = lax.axis_size("gy"), lax.axis_size("gz")
    route = []
    for p in range(count_y):
        step = distance if p % 2 == 0 else -distance
        route += [(p * count_z + q, p * count_z + (q + step) % count_z) for q in range(count_z)]
    return lax.ppermute(block, ("gy", "gz"), route)


def on_device(populations, solid_mask, centers, tile_lists, sphere_state, destination, relax_rates):
    held, walls, keep, give, info, inner, outer, border, meta = pl.pallas_call(
        collide_kernel,
        out_shape=(
            f32(19, GROUPS, 8, COLS),
            f32(GROUPS, 8, COLS),
            f32(8, COLS),
            f32(8, COLS),
            f32(8, COLS),
            f32(EDGE_ROWS, COLS),
            f32(EDGE_ROWS, COLS),
            f32(16, COLS),
            f32(8, COLS),
        ),
        in_specs=[HBM] * 7,
        out_specs=(VMEM,) * 9,
        scratch_shapes=[
            pltpu.VMEM((19, GROUPS, 8, COLS), jnp.float32),
            pltpu.VMEM((GROUPS, 8, COLS), jnp.int32),
            pltpu.SMEM((SLOTS, 8), jnp.float32),
            pltpu.SMEM((3, SLOTS), jnp.int32),
            pltpu.SMEM((4, 16), jnp.int32),
            pltpu.SMEM((SLOTS,), jnp.int32),
            pltpu.SMEM((19,), jnp.float32),
            pltpu.VMEM((19, GROUPS, 8, COLS), jnp.float32),
            pltpu.VMEM((N_COEF, 8, COLS), jnp.float32),
            pltpu.VMEM((COLS, COLS), jnp.float32),
            pltpu.VMEM((20, 6, 8, COLS), jnp.float32),
            pltpu.SemaphoreType.DMA((10,)),
        ],
        compiler_params=pltpu.CompilerParams(vmem_limit_bytes=32 * 1024 * 1024),
        name="collide",
    )(
        in_hbm(populations.reshape(19, GROUPS, 8, COLS)),
        in_hbm(solid_mask.reshape(GROUPS, 8, COLS)),
        in_hbm(sphere_state.T),
        in_hbm(centers),
        in_hbm(tile_lists.T),
        in_hbm(destination),
        in_hbm(relax_rates),
    )
    partner = swapped(jnp.concatenate([give, info, inner]), 1)
    chip = info + partner[8:16]
    near_2 = spread(chip, 2)
    near = spread(jnp.concatenate([keep, partner[0:8], chip]), 1)
    far = swapped(jnp.concatenate([near, near_2]), 1)
    spheres = [chip, near[16:24], near_2, far[16:32]]
    from_outer = swapped(jnp.concatenate([outer, near[0:8], far[8:16]] + spheres), -1)
    from_inner = swapped(jnp.concatenate(spheres), 3)
    walls = walls.reshape(PLANES, ROWS, COLS)
    streamed, y_part = pl.pallas_call(
        stream_kernel,
        out_shape=(f32(19, PLANES, ROWS, COLS), f32(10, PLANES, 8, COLS)),
        in_specs=[VMEM] * 6,
        out_specs=(HBM, VMEM),
        scratch_shapes=[
            pltpu.VMEM((19, PLANES, ROWS + 16, COLS), jnp.float32),
            pltpu.VMEM((COLS, COLS), jnp.float32),
            pltpu.VMEM((19, PLANES, ROWS, COLS), jnp.float32),
            pltpu.SemaphoreType.DMA((PLANES,)),
        ],
        compiler_params=pltpu.CompilerParams(vmem_limit_bytes=32 * 1024 * 1024),
        cost_estimate=pl.CostEstimate(flops=4_000_000, bytes_accessed=4_000_000, transcendentals=0),
        name="stream",
    )(held.reshape(19, PLANES, ROWS, COLS), walls, border, meta, near, far)
    populations_next, forces, state_next = pl.pallas_call(
        update_kernel,
        out_shape=(f32(19, PLANES, ROWS, COLS), f32(SLOTS, 6), f32(SLOTS, 8)),
        in_specs=[HBM] + [VMEM] * 10,
        out_specs=(HBM, HBM, HBM),
        scratch_shapes=[
            pltpu.VMEM((COLS, COLS), jnp.float32),
            pltpu.VMEM((10, PLANES, 8, COLS), jnp.float32),
            pltpu.VMEM((SLOTS, 6), jnp.float32),
            pltpu.VMEM((SLOTS, 8), jnp.float32),
            pltpu.SemaphoreType.DMA((12,)),
        ],
        input_output_aliases={0: 0},
        compiler_params=pltpu.CompilerParams(vmem_limit_bytes=32 * 1024 * 1024),
        name="update",
    )(
        in_hbm(streamed),
        y_part,
        walls,
        meta,
        chip,
        partner[16:40],
        near,
        near_2,
        far,
        from_outer,
        from_inner,
    )
    return populations_next, forces.T, state_next.T


def solution(mesh):
    return jax.shard_map(
        on_device,
        mesh=mesh,
        in_specs=(
            P(None, None, "gy", "gz"),
            P(None, "gy", "gz"),
            P(None, ("gy", "gz")),
            P(("gy", "gz"), None),
            P(None, ("gy", "gz")),
            P(("gy", "gz")),
            P(),
        ),
        out_specs=(P(None, None, "gy", "gz"), P(None, ("gy", "gz")), P(None, ("gy", "gz"))),
        check_vma=False,
    )
```

```python
import math

import jax
import jax.numpy as jnp
import numpy as np
from jax import lax
from jax.experimental import pallas as pl
from jax.experimental.pallas import tpu as pltpu
from jax.sharding import PartitionSpec as P

TILE = 16
RADIUS = 6
PLANES = 4
ROWS = 32
COLS = 128
SLOTS = 4
GROUPS = PLANES * ROWS // 8

VELOCITIES = (
    (0, 0, 0),
    (1, 0, 0),
    (-1, 0, 0),
    (0, 1, 0),
    (0, -1, 0),
    (0, 0, 1),
    (0, 0, -1),
    (1, 1, 0),
    (-1, -1, 0),
    (1, -1, 0),
    (-1, 1, 0),
    (1, 0, 1),
    (-1, 0, -1),
    (1, 0, -1),
    (-1, 0, 1),
    (0, 1, 1),
    (0, -1, -1),
    (0, 1, -1),
    (0, -1, 1),
)
OPPOSITE = (0, 2, 1, 4, 3, 6, 5, 8, 7, 10, 9, 12, 11, 14, 13, 16, 15, 18, 17)
EXPONENTS = (
    (0, 0, 0),
    (1, 0, 0),
    (0, 1, 0),
    (0, 0, 1),
    (2, 0, 0),
    (0, 2, 0),
    (0, 0, 2),
    (1, 1, 0),
    (1, 0, 1),
    (0, 1, 1),
    (1, 2, 0),
    (1, 0, 2),
    (2, 1, 0),
    (0, 1, 2),
    (2, 0, 1),
    (0, 2, 1),
    (2, 2, 0),
    (2, 0, 2),
    (0, 2, 2),
)
DIRECTIONS = ((-1, -1), (-1, 0), (-1, 1), (0, -1), (0, 1), (1, -1), (1, 0), (1, 1))

Z_UP = (5, 11, 14, 15, 18)
Z_DOWN = (6, 12, 13, 16, 17)
Y_UP = (3, 7, 10, 15, 17)
Y_DOWN = (4, 8, 9, 16, 18)
CLASS_MEMBER = (0, 1, 3, 5, 7, 11, 15)
EVEN_MOMENTS = (0, 4, 5, 6, 16, 17, 18)
ODD_MOMENTS = ((1, 10, 11), (2, 12, 13), (3, 14, 15))
ODD_CLASSES = ((1, 4, 5), (2, 4, 6), (3, 5, 6))
CROSS_MOMENTS = (7, 8, 9)
STATE_LANE = 40
DEST_LANE = 48
HALF = 64
EDGE_ROWS = 24


def moment_basis():
    velocity = np.array(VELOCITIES, dtype=np.float64)
    moment_rows = []
    for a, b, e in EXPONENTS:
        vector = velocity[:, 0] ** a * velocity[:, 1] ** b * velocity[:, 2] ** e
        for earlier in moment_rows:
            vector = vector - np.dot(earlier, vector) * earlier
        moment_rows.append(vector / np.sqrt(np.dot(vector, vector)))
    return np.array(moment_rows)


BASIS = moment_basis()


def store_coefficients(rates, coef):
    splat = [jnp.full((8, COLS), rates[k], jnp.float32) for k in range(19)]
    at = 0
    for a in range(7):
        for b in range(a, 7):
            total = None
            for k in EVEN_MOMENTS:
                c = float(BASIS[k, CLASS_MEMBER[a]] * BASIS[k, CLASS_MEMBER[b]])
                if abs(c) > 1e-12:
                    total = c * splat[k] if total is None else total + c * splat[k]
            coef[at] = total
            at += 1
    for axis in range(3):
        for a in range(3):
            for b in range(a, 3):
                total = None
                for k in ODD_MOMENTS[axis]:
                    c = float(
                        BASIS[k, CLASS_MEMBER[ODD_CLASSES[axis][a]]]
                        * BASIS[k, CLASS_MEMBER[ODD_CLASSES[axis][b]]]
                    )
                    if abs(c) > 1e-12:
                        total = c * splat[k] if total is None else total + c * splat[k]
                coef[at] = total
                at += 1
    for axis in range(3):
        c = float(BASIS[CROSS_MOMENTS[axis], CLASS_MEMBER[4 + axis]] ** 2)
        coef[at] = c * splat[CROSS_MOMENTS[axis]]
        at += 1


N_COEF = 28 + 18 + 3


def collide(f, coef):
    even_at = {}
    at = 0
    for a in range(7):
        for b in range(a, 7):
            even_at[a, b] = even_at[b, a] = at
            at += 1
    odd_at = []
    for _ in range(3):
        table = {}
        for a in range(3):
            for b in range(a, 3):
                table[a, b] = table[b, a] = at
                at += 1
        odd_at.append(table)
    cross_at = at

    def split(i):
        ab, amb = f[i] + f[i + 1], f[i] - f[i + 1]
        cd, cmd = f[i + 2] + f[i + 3], f[i + 2] - f[i + 3]
        return ab + cd, ab - cd, amb + cmd, amb - cmd

    s_xy, q_xy, xy_x, xy_y = split(7)
    s_xz, q_xz, xz_x, xz_z = split(11)
    s_yz, q_yz, yz_y, yz_z = split(15)
    s_x, s_y, s_z = f[1] + f[2], f[3] + f[4], f[5] + f[6]
    d_x, d_y, d_z = f[1] - f[2], f[3] - f[4], f[5] - f[6]
    rho = ((f[0] + s_x) + (s_y + s_z)) + ((s_xy + s_xz) + s_yz)
    j_x = d_x + (xy_x + xz_x)
    j_y = d_y + (xy_y + yz_y)
    j_z = d_z + (xz_z + yz_z)
    inverse = 1.0 / rho
    u_x, u_y, u_z = j_x * inverse, j_y * inverse, j_z * inverse
    e_x, e_y, e_z = j_x * u_x, j_y * u_y, j_z * u_z
    base = (rho - 1.5 * ((e_x + e_y) + e_z)) * (1.0 / 9.0)
    h_x, h_y, h_z = 0.5 * e_x, 0.5 * e_y, 0.5 * e_z
    even = (
        f[0] - 3.0 * base,
        s_x - (base + h_x),
        s_y - (base + h_y),
        s_z - (base + h_z),
        s_xy - (base + (h_x + h_y)),
        s_xz - (base + (h_x + h_z)),
        s_yz - (base + (h_y + h_z)),
    )
    third = 1.0 / 3.0
    t_x, t_y, t_z = third * j_x, third * j_y, third * j_z
    odd = (
        (d_x - t_x, xy_x - t_x, xz_x - t_x),
        (d_y - t_y, xy_y - t_y, yz_y - t_y),
        (d_z - t_z, xz_z - t_z, yz_z - t_z),
    )
    cross = (
        (q_xy - j_x * u_y) * coef[cross_at],
        (q_xz - j_x * u_z) * coef[cross_at + 1],
        (q_yz - j_y * u_z) * coef[cross_at + 2],
    )

    def apply(vector, table, n):
        out = []
        for a in range(n):
            terms = [coef[table[a, b]] * vector[b] for b in range(n)]
            while len(terms) > 1:
                terms = [
                    terms[i] + terms[i + 1] if i + 1 < len(terms) else terms[i]
                    for i in range(0, len(terms), 2)
                ]
            out.append(terms[0])
        return out

    ev = apply(even, even_at, 7)
    ox, oy, oz = (apply(odd[axis], odd_at[axis], 3) for axis in range(3))
    new = [f[0] - ev[0]]
    for axis, o in enumerate((ox, oy, oz)):
        i = 1 + 2 * axis
        new += [f[i] - (ev[1 + axis] + o[0]), f[i + 1] - (ev[1 + axis] - o[0])]
    for axis, (a, b) in enumerate(((ox[1], oy[1]), (ox[2], oz[1]), (oy[2], oz[2]))):
        i = 7 + 4 * axis
        plus, minus = ev[4 + axis] + cross[axis], ev[4 + axis] - cross[axis]
        both, differ = a + b, a - b
        new += [
            f[i] - (plus + both),
            f[i + 1] - (plus - both),
            f[i + 2] - (minus + differ),
            f[i + 3] - (minus - differ),
        ]
    return new


def sphere_partial(coll, partial, at, center_x, center_y, center_z, row_f, lane_f):
    first = jnp.maximum(lax.shift_right_arithmetic(center_y - (RADIUS + 1), 3), 0)
    last = jnp.minimum(lax.shift_right_arithmetic(center_y + (RADIUS + 1), 3), ROWS // 8 - 1)
    x_f = center_x.astype(jnp.float32)
    r_z = lane_f - center_z.astype(jnp.float32)
    z_sq = r_z * r_z
    zero = jnp.zeros((8, COLS), jnp.float32)

    def row_tile(tile, carry):
        f_x, f_y, f_z, t_x, t_y, t_z = carry
        r_y = row_f + (tile * 8 - center_y).astype(jnp.float32)
        yz_sq = r_y * r_y + z_sq
        p_x, p_y, p_z, x_py, x_pz = zero, zero, zero, zero, zero
        y_plus_z, y_minus_z = r_y + r_z, r_y - r_z
        for t in range(PLANES):
            r_x = t - x_f
            dist = yz_sq + r_x * r_x
            outside = dist > float(RADIUS * RADIUS)
            half = jnp.where(outside, (RADIUS * RADIUS - 1.0) * 0.5 - 0.5 * dist, -1e9)
            half_2 = half - 0.5
            limits = {1: (half, -half), 2: (half_2, -half_2)}

            def linked(i, along, kind):
                limit, negative = limits[kind]
                up, down = VELOCITIES[i][0], VELOCITIES[i + 1][0]
                total = None
                if 0 <= t + up < PLANES:
                    total = jnp.where(along <= limit, coll[i, t * 4 + tile], 0.0)
                if 0 <= t + down < PLANES:
                    back = jnp.where(along >= negative, coll[i + 1, t * 4 + tile], 0.0)
                    total = -back if total is None else total - back
                return total

            l_x = linked(1, r_x, 1)
            l_y = linked(3, r_y, 1)
            l_z = linked(5, r_z, 1)
            l_xy = linked(7, r_y + r_x, 2)
            l_xmy = linked(9, r_x - r_y, 2)
            l_xz = linked(11, r_z + r_x, 2)
            l_xmz = linked(13, r_x - r_z, 2)
            l_yz = linked(15, y_plus_z, 2)
            l_ymz = linked(17, y_minus_z, 2)
            m_x = l_x + ((l_xy + l_xmy) + (l_xz + l_xmz))
            m_y = l_y + ((l_xy - l_xmy) + (l_yz + l_ymz))
            m_z = l_z + ((l_xz - l_xmz) + (l_yz - l_ymz))
            p_x, p_y, p_z = p_x + m_x, p_y + m_y, p_z + m_z
            x_py, x_pz = x_py + r_x * m_y, x_pz + r_x * m_z
        return (
            f_x + p_x,
            f_y + p_y,
            f_z + p_z,
            t_x + (r_y * p_z - r_z * p_y),
            t_y + (r_z * p_x - x_pz),
            t_z + (x_py - r_y * p_x),
        )

    sums = lax.fori_loop(first, last + 1, row_tile, (zero,) * 6)
    packed = zero
    for j in range(6):
        packed = jnp.where(row_f == float(j), jnp.sum(sums[j], axis=0, keepdims=True), packed)
    partial[at] = packed


def collide_kernel(
    pops_in,
    mask_in,
    state_in,
    centers_in,
    lists_in,
    destination_in,
    rates_in,
    held,
    walls,
    keep,
    give,
    info,
    inner,
    outer,
    border,
    meta,
    pops,
    mask,
    state,
    centers,
    lists,
    destination,
    rates,
    coll,
    coef,
    turn,
    partial,
    sems,
):
    small = [
        pltpu.make_async_copy(source, target, sems.at[4 + k])
        for k, (source, target) in enumerate(
            (
                (rates_in, rates),
                (mask_in, mask),
                (centers_in, centers),
                (lists_in, lists),
                (destination_in, destination),
                (state_in, state),
            )
        )
    ]
    large = [
        pltpu.make_async_copy(
            pops_in.at[:, pl.ds(t * 4, 4)], pops.at[:, pl.ds(t * 4, 4)], sems.at[t]
        )
        for t in range(PLANES)
    ]
    small[0].start()
    small[1].start()
    for copy in large:
        copy.start()
    for copy in small[2:]:
        copy.start()
    lane = lax.broadcasted_iota(jnp.int32, (8, COLS), 1)
    lane_f = lane.astype(jnp.float32)
    row_f = lax.broadcasted_iota(jnp.int32, (8, COLS), 0).astype(jnp.float32)
    small[0].wait()
    store_coefficients(rates, coef)
    small[1].wait()

    def group(g, _):
        f = [pops[i, g] for i in range(19)]
        solid = mask[g] > 0
        flag = solid.astype(jnp.float32)
        walls[g] = flag
        new = collide(f, coef)
        for i in range(19):
            coll[i, g] = new[i]
            held[i, g] = jnp.where(solid, f[i], new[i])
        return 0

    for t in range(PLANES):
        large[t].wait()
        lax.fori_loop(t * 4, t * 4 + 4, group, 0, unroll=4)
    for copy in small[2:]:
        copy.wait()

    device_y = lax.shift_right_logical(centers[1, 0], 5)
    device_z = lax.shift_right_logical(centers[2, 0], 7)
    core = device_y & 1
    first = core == 0
    meta[0:1, :] = jnp.full((1, COLS), (device_y * 16 + device_z) * SLOTS, jnp.int32).astype(
        jnp.float32
    )
    meta[1:2, :] = jnp.full((1, COLS), core, jnp.int32).astype(jnp.float32)
    meta[2:8, :] = jnp.zeros((6, COLS), jnp.float32)

    for g in range(GROUPS):
        edge = jnp.zeros((8, COLS), jnp.float32)
        for k in range(6):
            values = walls[g]
            if k < 5:
                values = jnp.where(lane == 0, coll[Z_DOWN[k], g], coll[Z_UP[k], g])
            pair = lax.shift_right_logical(lane, 1) == k
            edge = jnp.where(pair, pltpu.roll(values, 2 * k + 1, 1), edge)
        turn[g * 8 : g * 8 + 8, :] = edge
    turn[...] = turn[...].T
    up_z = turn[pl.ds(0, 8, stride=2), :]
    down_z = turn[pl.ds(1, 8, stride=2), :]
    border[0:8, :] = up_z
    border[8:16, :] = down_z
    keep[...] = jnp.where(first, up_z, down_z)
    give[...] = jnp.where(first, down_z, up_z)
    for t in range(PLANES):
        for d in range(5):
            up = coll[Y_UP[d], t * 4 + 3, 7:8, :]
            down = coll[Y_DOWN[d], t * 4, 0:1, :]
            inner[d * 4 + t : d * 4 + t + 1, :] = jnp.where(first, up, down)
            outer[d * 4 + t : d * 4 + t + 1, :] = jnp.where(first, down, up)
        up = walls[t * 4 + 3, 7:8, :]
        down = walls[t * 4, 0:1, :]
        inner[20 + t : 21 + t, :] = jnp.where(first, up, down)
        outer[20 + t : 21 + t, :] = jnp.where(first, down, up)

    def own(s, _):
        sphere_partial(
            coll,
            partial,
            s,
            centers[0, s],
            centers[1, s] & (ROWS - 1),
            centers[2, s] & (COLS - 1),
            row_f,
            lane_f,
        )
        return 0

    partial[SLOTS:] = jnp.zeros((16, 8, COLS), jnp.float32)
    lax.fori_loop(0, SLOTS, own, 0)

    def listed(r, _):
        @pl.when(lists[0, r] >= 0)
        def _():
            sphere_partial(
                coll,
                partial,
                SLOTS + r,
                lists[3, r],
                lists[1, r] + TILE // 2,
                lists[2, r] + TILE // 2,
                row_f,
                lane_f,
            )

        return 0

    lax.fori_loop(0, 16, listed, 0)

    base = core * HALF
    tile = jnp.zeros((8, COLS), jnp.float32)
    for s in range(SLOTS):
        total = 2.0 * jnp.sum(partial[s], axis=1, keepdims=True)
        tile = jnp.where(lane == base + 4 * SLOTS + s, total, tile)
        column = jnp.zeros((8, COLS), jnp.float32)
        for r in range(8):
            column = jnp.where(row_f == float(r), state[s, r], column)
        tile = jnp.where(lane == base + STATE_LANE + s, column, tile)
        tile = jnp.where(lane == base + DEST_LANE + s, destination[s].astype(jnp.float32), tile)
    for r in range(16):
        offset = DIRECTIONS[r // 2]
        block = (offset[0] + 1) * 3 + offset[1] + 1
        total = 2.0 * jnp.sum(partial[SLOTS + r], axis=1, keepdims=True)
        slot = lists[0, r]
        at = jnp.where(slot >= 0, base + block * SLOTS + slot, -1)
        tile = jnp.where(lane == at, total, tile)
    info[...] = tile


Y_ALL = (3, 4, 7, 8, 9, 10, 15, 16, 17, 18)


def select_by(meta):
    second = jnp.broadcast_to(meta[1:2, :], (8, COLS)) > 0.5

    def swap_if(a, b):
        return jnp.where(second, b, a), jnp.where(second, a, b)

    return second, swap_if


def walled(values):
    return jnp.where(values[5:6, :] > 0.5, jnp.inf, values)


def stream_kernel(
    held, walls, border, meta, near_in, far_in, out_hbm, y_part, ext, turn, out, sems
):
    wall = jnp.inf
    _, swap_if = select_by(meta)
    lane = lax.broadcasted_iota(jnp.int32, (8, COLS), 1)
    sub = lax.broadcasted_iota(jnp.int32, (8, COLS), 0)
    row = lane & (ROWS - 1)
    plane = lax.shift_right_logical(lane, 5)

    def side(here, order):
        total = here
        for k, i in enumerate(order):
            c_x, c_y, _ = VELOCITIES[i]
            moved = here
            if c_y == 1:
                moved = jnp.where(row == 0, wall, pltpu.roll(here, 1, 1))
            if c_y == -1:
                moved = jnp.where(row == ROWS - 1, wall, pltpu.roll(here, COLS - 1, 1))
            if c_x == 1:
                moved = jnp.where(plane == 0, wall, pltpu.roll(here, 32, 1))
            if c_x == -1:
                moved = jnp.where(plane == PLANES - 1, wall, pltpu.roll(here, COLS - 32, 1))
            total = jnp.where(sub == k, moved, total)
        return total

    west, east = swap_if(walled(near_in[0:8, :]), walled(far_in[8:16, :]))
    turn[...] = jnp.zeros((COLS, COLS), jnp.float32)
    turn[0:8, :] = side(west, Z_UP)
    turn[8:16, :] = side(east, Z_DOWN)
    turned = turn[...].T
    turn[...] = turned
    column = lax.broadcasted_iota(jnp.int32, (ROWS, COLS), 1)
    for t in range(PLANES):
        solid = walls[t] > 0.5
        for i in range(19):
            ext[i, t, 8 : 8 + ROWS, :] = jnp.where(solid, wall, held[i, t])
            c_y = VELOCITIES[i][1]
            if c_y == 1:
                ext[i, t, 7:8, :] = jnp.full((1, COLS), wall, jnp.float32)
            if c_y == -1:
                ext[i, t, 8 + ROWS : 9 + ROWS, :] = jnp.full((1, COLS), wall, jnp.float32)
    copies = []
    for t in range(PLANES):
        solid = walls[t] > 0.5
        for i in range(19):
            c_x, c_y, c_z = VELOCITIES[i]
            source = t - c_x
            if 0 <= source < PLANES:
                pulled = ext[i, source, 8 - c_y : 8 - c_y + ROWS, :]
                if c_z != 0:
                    k = Z_UP.index(i) if c_z == 1 else 8 + Z_DOWN.index(i)
                    pulled = jnp.where(
                        column == (0 if c_z == 1 else COLS - 1),
                        turn[t * ROWS : (t + 1) * ROWS, k : k + 1],
                        pltpu.roll(pulled, 1 if c_z == 1 else COLS - 1, 1),
                    )
                fluid = jnp.where(pulled == wall, held[OPPOSITE[i], t], pulled)
            else:
                fluid = held[OPPOSITE[i], t]
            result = jnp.where(solid, held[i, t], fluid)
            out[i, t] = result
            if i in Y_ALL:
                y_part[Y_ALL.index(i), t] = result[0:8] if c_y == 1 else result[ROWS - 8 : ROWS]
        copies.append(pltpu.make_async_copy(out.at[:, t], out_hbm.at[:, t], sems.at[t]))
        copies[t].start()
    for copy in copies:
        copy.wait()


def update_kernel(
    streamed,
    y_part,
    walls,
    meta,
    chip,
    partner_edge,
    near_in,
    near_2,
    far_in,
    outer_in,
    inner_in,
    out_hbm,
    forces_hbm,
    state_hbm,
    turn,
    y_new,
    forces,
    state_next,
    sems,
):
    del streamed
    lane = lax.broadcasted_iota(jnp.int32, (8, COLS), 1)
    sub = lax.broadcasted_iota(jnp.int32, (8, COLS), 0)
    wall = jnp.inf
    second, swap_if = select_by(meta)
    west_partner, east_partner = swap_if(walled(near_in[8:16, :]), walled(far_in[0:8, :]))
    west_outer, east_outer = swap_if(
        walled(outer_in[EDGE_ROWS + 8 : EDGE_ROWS + 16, :]), walled(outer_in[EDGE_ROWS : EDGE_ROWS + 8, :])
    )
    west_south, west_north = swap_if(west_outer, west_partner)
    east_south, east_north = swap_if(east_outer, east_partner)
    pairs = [
        swap_if(outer_in[k : k + 8, :], partner_edge[k : k + 8, :]) for k in range(0, EDGE_ROWS, 8)
    ]
    south = [p[0] for p in pairs]
    north = [p[1] for p in pairs]

    def edge_row(edge, r):
        return edge[r // 8][r % 8 : r % 8 + 1, :]

    first_lane = lax.broadcasted_iota(jnp.int32, (1, COLS), 1)
    copies = []

    def send(source, target):
        copies.append(pltpu.make_async_copy(source, target, sems.at[len(copies)]))
        copies[-1].start()

    for y, i in enumerate(Y_ALL):
        c_x, c_y, c_z = VELOCITIES[i]
        edge, order = (south, Y_UP) if c_y == 1 else (north, Y_DOWN)
        for t in range(PLANES):
            source = t - c_x
            if not 0 <= source < PLANES:
                y_new[y, t] = y_part[y, t]
                continue
            values = edge_row(edge, order.index(i) * 4 + source)
            values = jnp.where(edge_row(edge, 20 + source) > 0.5, wall, values)
            if c_z != 0:
                if c_z == 1:
                    corner, k = (west_south if c_y == 1 else west_north), Z_UP.index(i)
                else:
                    corner, k = (east_south if c_y == 1 else east_north), Z_DOWN.index(i)
                at = t * ROWS + (ROWS - 1 if c_y == 1 else 0)
                to = 0 if c_z == 1 else COLS - 1
                values = jnp.where(
                    first_lane == to,
                    pltpu.roll(corner, (to - at) % COLS, 1)[k : k + 1, :],
                    pltpu.roll(values, 1 if c_z == 1 else COLS - 1, 1),
                )
            cells = walls[t, 0:1, :] if c_y == 1 else walls[t, ROWS - 1 : ROWS, :]
            values = jnp.where(cells > 0.5, wall, values)
            changed = (sub == (0 if c_y == 1 else 7)) & (values != wall)
            y_new[y, t] = jnp.where(changed, values, y_part[y, t])
        at = 0 if c_y == 1 else ROWS - 8
        send(y_new.at[y], out_hbm.at[i, :, at : at + 8])

    middle = {0: chip[...]}
    middle[-1], middle[1] = swap_if(near_in[16:24, :], far_in[16:24, :])
    middle[-2], middle[2] = swap_if(near_2[...], far_in[24:32, :])
    arrived = []
    for ref, start in ((outer_in, EDGE_ROWS + 16), (inner_in, 0)):
        group = [ref[start + 8 * k : start + 8 * k + 8, :] for k in range(5)]
        columns = {0: group[0]}
        columns[-1], columns[1] = swap_if(group[3], group[1])
        columns[-2], columns[2] = swap_if(group[4], group[2])
        arrived.append(columns)
    tiles = {}
    low = lane < HALF
    for b in range(-2, 3):
        before, after = swap_if(arrived[0][b], arrived[1][b])
        turned_before, turned_own, turned_after = (
            pltpu.roll(part, HALF, 1) for part in (before, middle[b], after)
        )
        tiles[0, b] = jnp.where(second, jnp.where(low, turned_before, turned_own), before)
        tiles[1, b] = jnp.where(second, jnp.where(low, turned_own, turned_after), middle[b])
        tiles[2, b] = jnp.where(second, turned_after, after)

    number = lax.shift_right_logical(lane, 2)
    number_a = sum((number >= 3 * k).astype(jnp.int32) for k in (1, 2, 3)) - 1
    number_b = number - 3 * (number_a + 1) - 1
    listed = lane < 9 * SLOTS
    near_a = {a: listed & (number_a >= a - 1) & (number_a <= a + 1) for a in range(-2, 3)}
    near_b = {b: (number_b >= b - 1) & (number_b <= b + 1) for b in range(-2, 3)}

    def device_lanes(a, b, shift):
        shift = (shift - HALF * (a % 2)) % COLS
        part = tiles[(a + 2) // 2, b]
        return pltpu.roll(part, shift, 1) if shift else part

    force = jnp.zeros((8, COLS), jnp.float32)
    for a in range(-2, 3):
        for b in range(-2, 3):
            part = device_lanes(a, b, SLOTS * (3 * a + b))
            force = force + jnp.where(near_a[a] & near_b[b], part, 0.0)
    record = jnp.zeros((8, COLS), jnp.float32)
    target = jnp.full((8, COLS), -1.0, jnp.float32)
    for a in (-1, 0, 1):
        for b in (-1, 0, 1):
            n = 3 * (a + 1) + b + 1
            record = jnp.where(number == n, device_lanes(a, b, SLOTS * n - STATE_LANE), record)
            target = jnp.where(number == n, device_lanes(a, b, SLOTS * n - DEST_LANE), target)
    mass = record[6:7, :] * (3.0 / (4.0 * math.pi * RADIUS * RADIUS * RADIUS))
    spin = mass * record[7:8, :] * (1.0 / (RADIUS * RADIUS))
    gain = jnp.where(sub < 3, force * mass, jnp.where(sub < 6, force * spin, 0.0))
    updated = record + gain
    picked = [
        jnp.where(listed & (target[0:1, :] == meta[0:1, :] + float(j)), updated, 0.0)
        for j in range(SLOTS)
    ]
    result = jnp.zeros((8, COLS), jnp.float32)
    for j in range(SLOTS):
        result = jnp.where(lane == j, jnp.sum(picked[j], axis=1, keepdims=True), result)
    turn[0:8, :] = result
    turn[8:16, :] = force
    turned = turn[...].T
    state_next[...] = turned[0:SLOTS, 0:8]
    forces[...] = turned[4 * SLOTS : 5 * SLOTS, 8:14]
    send(state_next, state_hbm)
    send(forces, forces_hbm)
    for copy in copies:
        copy.wait()


VMEM = pl.BlockSpec(memory_space=pltpu.VMEM)
HBM = pl.BlockSpec(memory_space=pltpu.HBM)


def f32(*shape):
    return jax.ShapeDtypeStruct(shape, jnp.float32)


def in_hbm(array):
    return pltpu.with_memory_space_constraint(array, pltpu.HBM)


def swapped(block, distance):
    count = lax.axis_size("gy")
    route = [(p, (p + (distance if p % 2 == 0 else -distance)) % count) for p in range(count)]
    return lax.ppermute(block, "gy", route)


def spread(block, distance):
    count_y, count_z = lax.axis_size("gy"), lax.axis_size("gz")
    route = []
    for p in range(count_y):
        step = distance if p % 2 == 0 else -distance
        route += [(p * count_z + q, p * count_z + (q + step) % count_z) for q in range(count_z)]
    return lax.ppermute(block, ("gy", "gz"), route)


def on_device(populations, solid_mask, centers, tile_lists, sphere_state, destination, relax_rates):
    held, walls, keep, give, info, inner, outer, border, meta = pl.pallas_call(
        collide_kernel,
        out_shape=(
            f32(19, GROUPS, 8, COLS),
            f32(GROUPS, 8, COLS),
            f32(8, COLS),
            f32(8, COLS),
            f32(8, COLS),
            f32(EDGE_ROWS, COLS),
            f32(EDGE_ROWS, COLS),
            f32(16, COLS),
            f32(8, COLS),
        ),
        in_specs=[HBM] * 7,
        out_specs=(VMEM,) * 9,
        scratch_shapes=[
            pltpu.VMEM((19, GROUPS, 8, COLS), jnp.float32),
            pltpu.VMEM((GROUPS, 8, COLS), jnp.int32),
            pltpu.SMEM((SLOTS, 8), jnp.float32),
            pltpu.SMEM((3, SLOTS), jnp.int32),
            pltpu.SMEM((4, 16), jnp.int32),
            pltpu.SMEM((SLOTS,), jnp.int32),
            pltpu.SMEM((19,), jnp.float32),
            pltpu.VMEM((19, GROUPS, 8, COLS), jnp.float32),
            pltpu.VMEM((N_COEF, 8, COLS), jnp.float32),
            pltpu.VMEM((COLS, COLS), jnp.float32),
            pltpu.VMEM((20, 8, COLS), jnp.float32),
            pltpu.SemaphoreType.DMA((10,)),
        ],
        compiler_params=pltpu.CompilerParams(vmem_limit_bytes=32 * 1024 * 1024),
        name="collide",
    )(
        in_hbm(populations.reshape(19, GROUPS, 8, COLS)),
        in_hbm(solid_mask.reshape(GROUPS, 8, COLS)),
        in_hbm(sphere_state.T),
        in_hbm(centers),
        in_hbm(tile_lists.T),
        in_hbm(destination),
        in_hbm(relax_rates),
    )
    partner = swapped(jnp.concatenate([give, info, inner]), 1)
    chip = info + partner[8:16]
    near_2 = spread(chip, 2)
    near = spread(jnp.concatenate([keep, partner[0:8], chip]), 1)
    far = swapped(jnp.concatenate([near, near_2]), 1)
    spheres = [chip, near[16:24], near_2, far[16:32]]
    from_outer = swapped(jnp.concatenate([outer, near[0:8], far[8:16]] + spheres), -1)
    from_inner = swapped(jnp.concatenate(spheres), 3)
    walls = walls.reshape(PLANES, ROWS, COLS)
    streamed, y_part = pl.pallas_call(
        stream_kernel,
        out_shape=(f32(19, PLANES, ROWS, COLS), f32(10, PLANES, 8, COLS)),
        in_specs=[VMEM] * 6,
        out_specs=(HBM, VMEM),
        scratch_shapes=[
            pltpu.VMEM((19, PLANES, ROWS + 16, COLS), jnp.float32),
            pltpu.VMEM((COLS, COLS), jnp.float32),
            pltpu.VMEM((19, PLANES, ROWS, COLS), jnp.float32),
            pltpu.SemaphoreType.DMA((PLANES,)),
        ],
        compiler_params=pltpu.CompilerParams(vmem_limit_bytes=32 * 1024 * 1024),
        cost_estimate=pl.CostEstimate(flops=4_000_000, bytes_accessed=4_000_000, transcendentals=0),
        name="stream",
    )(held.reshape(19, PLANES, ROWS, COLS), walls, border, meta, near, far)
    populations_next, forces, state_next = pl.pallas_call(
        update_kernel,
        out_shape=(f32(19, PLANES, ROWS, COLS), f32(SLOTS, 6), f32(SLOTS, 8)),
        in_specs=[HBM] + [VMEM] * 10,
        out_specs=(HBM, HBM, HBM),
        scratch_shapes=[
            pltpu.VMEM((COLS, COLS), jnp.float32),
            pltpu.VMEM((10, PLANES, 8, COLS), jnp.float32),
            pltpu.VMEM((SLOTS, 6), jnp.float32),
            pltpu.VMEM((SLOTS, 8), jnp.float32),
            pltpu.SemaphoreType.DMA((12,)),
        ],
        input_output_aliases={0: 0},
        compiler_params=pltpu.CompilerParams(vmem_limit_bytes=32 * 1024 * 1024),
        name="update",
    )(
        in_hbm(streamed),
        y_part,
        walls,
        meta,
        chip,
        partner[16:40],
        near,
        near_2,
        far,
        from_outer,
        from_inner,
    )
    return populations_next, forces.T, state_next.T


def solution(mesh):
    return jax.shard_map(
        on_device,
        mesh=mesh,
        in_specs=(
            P(None, None, "gy", "gz"),
            P(None, "gy", "gz"),
            P(None, ("gy", "gz")),
            P(("gy", "gz"), None),
            P(None, ("gy", "gz")),
            P(("gy", "gz")),
            P(),
        ),
        out_specs=(P(None, None, "gy", "gz"), P(None, ("gy", "gz")), P(None, ("gy", "gz"))),
        check_vma=False,
    )
```

```python
import math

import jax
import jax.numpy as jnp
import numpy as np
from jax import lax
from jax.experimental import pallas as pl
from jax.experimental.pallas import tpu as pltpu
from jax.sharding import PartitionSpec as P

TILE = 16
RADIUS = 6
PLANES = 4
ROWS = 32
COLS = 128
SLOTS = 4
GROUPS = PLANES * ROWS // 8

VELOCITIES = (
    (0, 0, 0),
    (1, 0, 0),
    (-1, 0, 0),
    (0, 1, 0),
    (0, -1, 0),
    (0, 0, 1),
    (0, 0, -1),
    (1, 1, 0),
    (-1, -1, 0),
    (1, -1, 0),
    (-1, 1, 0),
    (1, 0, 1),
    (-1, 0, -1),
    (1, 0, -1),
    (-1, 0, 1),
    (0, 1, 1),
    (0, -1, -1),
    (0, 1, -1),
    (0, -1, 1),
)
OPPOSITE = (0, 2, 1, 4, 3, 6, 5, 8, 7, 10, 9, 12, 11, 14, 13, 16, 15, 18, 17)
EXPONENTS = (
    (0, 0, 0),
    (1, 0, 0),
    (0, 1, 0),
    (0, 0, 1),
    (2, 0, 0),
    (0, 2, 0),
    (0, 0, 2),
    (1, 1, 0),
    (1, 0, 1),
    (0, 1, 1),
    (1, 2, 0),
    (1, 0, 2),
    (2, 1, 0),
    (0, 1, 2),
    (2, 0, 1),
    (0, 2, 1),
    (2, 2, 0),
    (2, 0, 2),
    (0, 2, 2),
)
DIRECTIONS = ((-1, -1), (-1, 0), (-1, 1), (0, -1), (0, 1), (1, -1), (1, 0), (1, 1))

Z_UP = (5, 11, 14, 15, 18)
Z_DOWN = (6, 12, 13, 16, 17)
Y_UP = (3, 7, 10, 15, 17)
Y_DOWN = (4, 8, 9, 16, 18)
CLASS_MEMBER = (0, 1, 3, 5, 7, 11, 15)
EVEN_MOMENTS = (0, 4, 5, 6, 16, 17, 18)
ODD_MOMENTS = ((1, 10, 11), (2, 12, 13), (3, 14, 15))
ODD_CLASSES = ((1, 4, 5), (2, 4, 6), (3, 5, 6))
CROSS_MOMENTS = (7, 8, 9)
STATE_LANE = 40
DEST_LANE = 48
HALF = 64
EDGE_ROWS = 24


def moment_basis():
    velocity = np.array(VELOCITIES, dtype=np.float64)
    moment_rows = []
    for a, b, e in EXPONENTS:
        vector = velocity[:, 0] ** a * velocity[:, 1] ** b * velocity[:, 2] ** e
        for earlier in moment_rows:
            vector = vector - np.dot(earlier, vector) * earlier
        moment_rows.append(vector / np.sqrt(np.dot(vector, vector)))
    return np.array(moment_rows)


BASIS = moment_basis()


def store_coefficients(rates, coef):
    splat = [jnp.full((8, COLS), rates[k], jnp.float32) for k in range(19)]
    at = 0
    for a in range(7):
        for b in range(a, 7):
            total = None
            for k in EVEN_MOMENTS:
                c = float(BASIS[k, CLASS_MEMBER[a]] * BASIS[k, CLASS_MEMBER[b]])
                if abs(c) > 1e-12:
                    total = c * splat[k] if total is None else total + c * splat[k]
            coef[at] = total
            at += 1
    for axis in range(3):
        for a in range(3):
            for b in range(a, 3):
                total = None
                for k in ODD_MOMENTS[axis]:
                    c = float(
                        BASIS[k, CLASS_MEMBER[ODD_CLASSES[axis][a]]]
                        * BASIS[k, CLASS_MEMBER[ODD_CLASSES[axis][b]]]
                    )
                    if abs(c) > 1e-12:
                        total = c * splat[k] if total is None else total + c * splat[k]
                coef[at] = total
                at += 1
    for axis in range(3):
        c = float(BASIS[CROSS_MOMENTS[axis], CLASS_MEMBER[4 + axis]] ** 2)
        coef[at] = c * splat[CROSS_MOMENTS[axis]]
        at += 1


N_COEF = 28 + 18 + 3


def collide(f, coef):
    even_at = {}
    at = 0
    for a in range(7):
        for b in range(a, 7):
            even_at[a, b] = even_at[b, a] = at
            at += 1
    odd_at = []
    for _ in range(3):
        table = {}
        for a in range(3):
            for b in range(a, 3):
                table[a, b] = table[b, a] = at
                at += 1
        odd_at.append(table)
    cross_at = at

    def split(i):
        ab, amb = f[i] + f[i + 1], f[i] - f[i + 1]
        cd, cmd = f[i + 2] + f[i + 3], f[i + 2] - f[i + 3]
        return ab + cd, ab - cd, amb + cmd, amb - cmd

    s_xy, q_xy, xy_x, xy_y = split(7)
    s_xz, q_xz, xz_x, xz_z = split(11)
    s_yz, q_yz, yz_y, yz_z = split(15)
    s_x, s_y, s_z = f[1] + f[2], f[3] + f[4], f[5] + f[6]
    d_x, d_y, d_z = f[1] - f[2], f[3] - f[4], f[5] - f[6]
    rho = ((f[0] + s_x) + (s_y + s_z)) + ((s_xy + s_xz) + s_yz)
    j_x = d_x + (xy_x + xz_x)
    j_y = d_y + (xy_y + yz_y)
    j_z = d_z + (xz_z + yz_z)
    inverse = 1.0 / rho
    u_x, u_y, u_z = j_x * inverse, j_y * inverse, j_z * inverse
    e_x, e_y, e_z = j_x * u_x, j_y * u_y, j_z * u_z
    base = (rho - 1.5 * ((e_x + e_y) + e_z)) * (1.0 / 9.0)
    h_x, h_y, h_z = 0.5 * e_x, 0.5 * e_y, 0.5 * e_z
    even = (
        f[0] - 3.0 * base,
        s_x - (base + h_x),
        s_y - (base + h_y),
        s_z - (base + h_z),
        s_xy - (base + (h_x + h_y)),
        s_xz - (base + (h_x + h_z)),
        s_yz - (base + (h_y + h_z)),
    )
    third = 1.0 / 3.0
    t_x, t_y, t_z = third * j_x, third * j_y, third * j_z
    odd = (
        (d_x - t_x, xy_x - t_x, xz_x - t_x),
        (d_y - t_y, xy_y - t_y, yz_y - t_y),
        (d_z - t_z, xz_z - t_z, yz_z - t_z),
    )
    cross = (
        (q_xy - j_x * u_y) * coef[cross_at],
        (q_xz - j_x * u_z) * coef[cross_at + 1],
        (q_yz - j_y * u_z) * coef[cross_at + 2],
    )

    def apply(vector, table, n):
        out = []
        for a in range(n):
            terms = [coef[table[a, b]] * vector[b] for b in range(n)]
            while len(terms) > 1:
                terms = [
                    terms[i] + terms[i + 1] if i + 1 < len(terms) else terms[i]
                    for i in range(0, len(terms), 2)
                ]
            out.append(terms[0])
        return out

    ev = apply(even, even_at, 7)
    ox, oy, oz = (apply(odd[axis], odd_at[axis], 3) for axis in range(3))
    new = [f[0] - ev[0]]
    for axis, o in enumerate((ox, oy, oz)):
        i = 1 + 2 * axis
        new += [f[i] - (ev[1 + axis] + o[0]), f[i + 1] - (ev[1 + axis] - o[0])]
    for axis, (a, b) in enumerate(((ox[1], oy[1]), (ox[2], oz[1]), (oy[2], oz[2]))):
        i = 7 + 4 * axis
        plus, minus = ev[4 + axis] + cross[axis], ev[4 + axis] - cross[axis]
        both, differ = a + b, a - b
        new += [
            f[i] - (plus + both),
            f[i + 1] - (plus - both),
            f[i + 2] - (minus + differ),
            f[i + 3] - (minus - differ),
        ]
    return new


def sphere_partial(coll, partial, at, center_x, center_y, center_z, row_f, lane_f):
    first = jnp.maximum(lax.shift_right_arithmetic(center_y - (RADIUS + 1), 3), 0)
    last = jnp.minimum(lax.shift_right_arithmetic(center_y + (RADIUS + 1), 3), ROWS // 8 - 1)
    x_f = center_x.astype(jnp.float32)
    r_z = lane_f - center_z.astype(jnp.float32)
    z_sq = r_z * r_z
    zero = jnp.zeros((8, COLS), jnp.float32)

    def row_tile(tile, carry):
        f_x, f_y, f_z, t_x, t_y, t_z = carry
        r_y = row_f + (tile * 8 - center_y).astype(jnp.float32)
        yz_sq = r_y * r_y + z_sq
        p_x, p_y, p_z, x_py, x_pz = zero, zero, zero, zero, zero
        y_plus_z, y_minus_z = r_y + r_z, r_y - r_z
        for t in range(PLANES):
            r_x = t - x_f
            dist = yz_sq + r_x * r_x
            outside = dist > float(RADIUS * RADIUS)
            half = jnp.where(outside, (RADIUS * RADIUS - 1.0) * 0.5 - 0.5 * dist, -1e9)
            half_2 = half - 0.5
            limits = {1: (half, -half), 2: (half_2, -half_2)}

            def linked(i, along, kind):
                limit, negative = limits[kind]
                up, down = VELOCITIES[i][0], VELOCITIES[i + 1][0]
                total = None
                if 0 <= t + up < PLANES:
                    total = jnp.where(along <= limit, coll[i, t * 4 + tile], 0.0)
                if 0 <= t + down < PLANES:
                    back = jnp.where(along >= negative, coll[i + 1, t * 4 + tile], 0.0)
                    total = -back if total is None else total - back
                return total

            l_x = linked(1, r_x, 1)
            l_y = linked(3, r_y, 1)
            l_z = linked(5, r_z, 1)
            l_xy = linked(7, r_y + r_x, 2)
            l_xmy = linked(9, r_x - r_y, 2)
            l_xz = linked(11, r_z + r_x, 2)
            l_xmz = linked(13, r_x - r_z, 2)
            l_yz = linked(15, y_plus_z, 2)
            l_ymz = linked(17, y_minus_z, 2)
            m_x = l_x + ((l_xy + l_xmy) + (l_xz + l_xmz))
            m_y = l_y + ((l_xy - l_xmy) + (l_yz + l_ymz))
            m_z = l_z + ((l_xz - l_xmz) + (l_yz - l_ymz))
            p_x, p_y, p_z = p_x + m_x, p_y + m_y, p_z + m_z
            x_py, x_pz = x_py + r_x * m_y, x_pz + r_x * m_z
        return (
            f_x + p_x,
            f_y + p_y,
            f_z + p_z,
            t_x + (r_y * p_z - r_z * p_y),
            t_y + (r_z * p_x - x_pz),
            t_z + (x_py - r_y * p_x),
        )

    sums = lax.fori_loop(first, last + 1, row_tile, (zero,) * 6)
    packed = zero
    for j in range(6):
        packed = jnp.where(row_f == float(j), jnp.sum(sums[j], axis=0, keepdims=True), packed)
    partial[at] = packed


def collide_kernel(
    pops_in,
    mask_in,
    state_in,
    centers_in,
    lists_in,
    destination_in,
    rates_in,
    held,
    walls,
    keep,
    give,
    info,
    inner,
    outer,
    border,
    meta,
    pops,
    mask,
    state,
    centers,
    lists,
    destination,
    rates,
    coll,
    coef,
    turn,
    partial,
    sems,
):
    small = [
        pltpu.make_async_copy(source, target, sems.at[4 + k])
        for k, (source, target) in enumerate(
            (
                (rates_in, rates),
                (mask_in, mask),
                (centers_in, centers),
                (lists_in, lists),
                (destination_in, destination),
                (state_in, state),
            )
        )
    ]
    large = [
        pltpu.make_async_copy(
            pops_in.at[:, pl.ds(t * 4, 4)], pops.at[:, pl.ds(t * 4, 4)], sems.at[t]
        )
        for t in range(PLANES)
    ]
    small[0].start()
    small[1].start()
    for copy in large:
        copy.start()
    for copy in small[2:]:
        copy.start()
    lane = lax.broadcasted_iota(jnp.int32, (8, COLS), 1)
    lane_f = lane.astype(jnp.float32)
    row_f = lax.broadcasted_iota(jnp.int32, (8, COLS), 0).astype(jnp.float32)
    small[0].wait()
    store_coefficients(rates, coef)
    small[1].wait()

    def group(g, _):
        f = [pops[i, g] for i in range(19)]
        solid = mask[g] > 0
        flag = solid.astype(jnp.float32)
        walls[g] = flag
        new = collide(f, coef)
        for i in range(19):
            coll[i, g] = new[i]
            held[i, g] = jnp.where(solid, f[i], new[i])
        return 0

    for t in range(PLANES):
        large[t].wait()
        lax.fori_loop(t * 4, t * 4 + 4, group, 0, unroll=4)
    for copy in small[2:]:
        copy.wait()

    device_y = lax.shift_right_logical(centers[1, 0], 5)
    device_z = lax.shift_right_logical(centers[2, 0], 7)
    core = device_y & 1
    first = core == 0
    meta[0:1, :] = jnp.full((1, COLS), (device_y * 16 + device_z) * SLOTS, jnp.int32).astype(
        jnp.float32
    )
    meta[1:2, :] = jnp.full((1, COLS), core, jnp.int32).astype(jnp.float32)
    meta[2:8, :] = jnp.zeros((6, COLS), jnp.float32)

    for g in range(GROUPS):
        edge = jnp.zeros((8, COLS), jnp.float32)
        for k in range(6):
            values = walls[g]
            if k < 5:
                values = jnp.where(lane == 0, coll[Z_DOWN[k], g], coll[Z_UP[k], g])
            pair = lax.shift_right_logical(lane, 1) == k
            edge = jnp.where(pair, pltpu.roll(values, 2 * k + 1, 1), edge)
        turn[g * 8 : g * 8 + 8, :] = edge
    turn[...] = turn[...].T
    up_z = turn[pl.ds(0, 8, stride=2), :]
    down_z = turn[pl.ds(1, 8, stride=2), :]
    border[0:8, :] = up_z
    border[8:16, :] = down_z
    keep[...] = jnp.where(first, up_z, down_z)
    give[...] = jnp.where(first, down_z, up_z)
    for t in range(PLANES):
        for d in range(5):
            up = coll[Y_UP[d], t * 4 + 3, 7:8, :]
            down = coll[Y_DOWN[d], t * 4, 0:1, :]
            inner[d * 4 + t : d * 4 + t + 1, :] = jnp.where(first, up, down)
            outer[d * 4 + t : d * 4 + t + 1, :] = jnp.where(first, down, up)
        up = walls[t * 4 + 3, 7:8, :]
        down = walls[t * 4, 0:1, :]
        inner[20 + t : 21 + t, :] = jnp.where(first, up, down)
        outer[20 + t : 21 + t, :] = jnp.where(first, down, up)

    def own(s, _):
        sphere_partial(
            coll,
            partial,
            s,
            centers[0, s],
            centers[1, s] & (ROWS - 1),
            centers[2, s] & (COLS - 1),
            row_f,
            lane_f,
        )
        return 0

    partial[SLOTS:] = jnp.zeros((16, 8, COLS), jnp.float32)
    lax.fori_loop(0, SLOTS, own, 0)

    def listed(r, _):
        @pl.when(lists[0, r] >= 0)
        def _():
            sphere_partial(
                coll,
                partial,
                SLOTS + r,
                lists[3, r],
                lists[1, r] + TILE // 2,
                lists[2, r] + TILE // 2,
                row_f,
                lane_f,
            )

        return 0

    lax.fori_loop(0, 16, listed, 0)

    base = core * HALF
    tile = jnp.zeros((8, COLS), jnp.float32)
    for s in range(SLOTS):
        total = 2.0 * jnp.sum(partial[s], axis=1, keepdims=True)
        tile = jnp.where(lane == base + 4 * SLOTS + s, total, tile)
        column = jnp.zeros((8, COLS), jnp.float32)
        for r in range(8):
            column = jnp.where(row_f == float(r), state[s, r], column)
        tile = jnp.where(lane == base + STATE_LANE + s, column, tile)
        tile = jnp.where(lane == base + DEST_LANE + s, destination[s].astype(jnp.float32), tile)
    for r in range(16):
        offset = DIRECTIONS[r // 2]
        block = (offset[0] + 1) * 3 + offset[1] + 1
        total = 2.0 * jnp.sum(partial[SLOTS + r], axis=1, keepdims=True)
        slot = lists[0, r]
        at = jnp.where(slot >= 0, base + block * SLOTS + slot, -1)
        tile = jnp.where(lane == at, total, tile)
    info[...] = tile


Y_ALL = (3, 4, 7, 8, 9, 10, 15, 16, 17, 18)


def select_by(meta):
    second = jnp.broadcast_to(meta[1:2, :], (8, COLS)) > 0.5

    def swap_if(a, b):
        return jnp.where(second, b, a), jnp.where(second, a, b)

    return second, swap_if


def walled(values):
    return jnp.where(values[5:6, :] > 0.5, jnp.inf, values)


def stream_kernel(
    held, walls, border, meta, near_in, far_in, out_hbm, y_part, ext, turn, out, sems
):
    wall = jnp.inf
    _, swap_if = select_by(meta)
    lane = lax.broadcasted_iota(jnp.int32, (8, COLS), 1)
    sub = lax.broadcasted_iota(jnp.int32, (8, COLS), 0)
    row = lane & (ROWS - 1)
    plane = lax.shift_right_logical(lane, 5)

    def side(here, order):
        total = here
        for k, i in enumerate(order):
            c_x, c_y, _ = VELOCITIES[i]
            moved = here
            if c_y == 1:
                moved = jnp.where(row == 0, wall, pltpu.roll(here, 1, 1))
            if c_y == -1:
                moved = jnp.where(row == ROWS - 1, wall, pltpu.roll(here, COLS - 1, 1))
            if c_x == 1:
                moved = jnp.where(plane == 0, wall, pltpu.roll(here, 32, 1))
            if c_x == -1:
                moved = jnp.where(plane == PLANES - 1, wall, pltpu.roll(here, COLS - 32, 1))
            total = jnp.where(sub == k, moved, total)
        return total

    west, east = swap_if(walled(near_in[0:8, :]), walled(far_in[8:16, :]))
    turn[...] = jnp.zeros((COLS, COLS), jnp.float32)
    turn[0:8, :] = side(west, Z_UP)
    turn[8:16, :] = side(east, Z_DOWN)
    turned = turn[...].T
    turn[...] = turned
    column = lax.broadcasted_iota(jnp.int32, (ROWS, COLS), 1)
    for t in range(PLANES):
        solid = walls[t] > 0.5
        for i in range(19):
            ext[i, t, 8 : 8 + ROWS, :] = jnp.where(solid, wall, held[i, t])
            c_y = VELOCITIES[i][1]
            if c_y == 1:
                ext[i, t, 7:8, :] = jnp.full((1, COLS), wall, jnp.float32)
            if c_y == -1:
                ext[i, t, 8 + ROWS : 9 + ROWS, :] = jnp.full((1, COLS), wall, jnp.float32)
    copies = []
    for t in range(PLANES):
        solid = walls[t] > 0.5
        for i in range(19):
            c_x, c_y, c_z = VELOCITIES[i]
            source = t - c_x
            if 0 <= source < PLANES:
                pulled = ext[i, source, 8 - c_y : 8 - c_y + ROWS, :]
                if c_z != 0:
                    k = Z_UP.index(i) if c_z == 1 else 8 + Z_DOWN.index(i)
                    pulled = jnp.where(
                        column == (0 if c_z == 1 else COLS - 1),
                        turn[t * ROWS : (t + 1) * ROWS, k : k + 1],
                        pltpu.roll(pulled, 1 if c_z == 1 else COLS - 1, 1),
                    )
                fluid = jnp.where(pulled == wall, held[OPPOSITE[i], t], pulled)
            else:
                fluid = held[OPPOSITE[i], t]
            result = jnp.where(solid, held[i, t], fluid)
            out[i, t] = result
            if i in Y_ALL:
                y_part[Y_ALL.index(i), t] = result[0:8] if c_y == 1 else result[ROWS - 8 : ROWS]
        copies.append(pltpu.make_async_copy(out.at[:, t], out_hbm.at[:, t], sems.at[t]))
        copies[t].start()
    for copy in copies:
        copy.wait()


def update_kernel(
    streamed,
    y_part,
    walls,
    meta,
    chip,
    partner_edge,
    near_in,
    near_2,
    far_in,
    outer_in,
    inner_in,
    out_hbm,
    forces_hbm,
    state_hbm,
    turn,
    y_new,
    forces,
    state_next,
    sems,
):
    del streamed
    lane = lax.broadcasted_iota(jnp.int32, (8, COLS), 1)
    sub = lax.broadcasted_iota(jnp.int32, (8, COLS), 0)
    wall = jnp.inf
    second, swap_if = select_by(meta)
    west_partner, east_partner = swap_if(walled(near_in[8:16, :]), walled(far_in[0:8, :]))
    west_outer, east_outer = swap_if(
        walled(outer_in[EDGE_ROWS + 8 : EDGE_ROWS + 16, :]), walled(outer_in[EDGE_ROWS : EDGE_ROWS + 8, :])
    )
    west_south, west_north = swap_if(west_outer, west_partner)
    east_south, east_north = swap_if(east_outer, east_partner)
    pairs = [
        swap_if(outer_in[k : k + 8, :], partner_edge[k : k + 8, :]) for k in range(0, EDGE_ROWS, 8)
    ]
    south = [p[0] for p in pairs]
    north = [p[1] for p in pairs]

    def edge_row(edge, r):
        return edge[r // 8][r % 8 : r % 8 + 1, :]

    first_lane = lax.broadcasted_iota(jnp.int32, (1, COLS), 1)
    copies = []

    def send(source, target):
        copies.append(pltpu.make_async_copy(source, target, sems.at[len(copies)]))
        copies[-1].start()

    for y, i in enumerate(Y_ALL):
        c_x, c_y, c_z = VELOCITIES[i]
        edge, order = (south, Y_UP) if c_y == 1 else (north, Y_DOWN)
        for t in range(PLANES):
            source = t - c_x
            if not 0 <= source < PLANES:
                y_new[y, t] = y_part[y, t]
                continue
            values = edge_row(edge, order.index(i) * 4 + source)
            values = jnp.where(edge_row(edge, 20 + source) > 0.5, wall, values)
            if c_z != 0:
                if c_z == 1:
                    corner, k = (west_south if c_y == 1 else west_north), Z_UP.index(i)
                else:
                    corner, k = (east_south if c_y == 1 else east_north), Z_DOWN.index(i)
                at = t * ROWS + (ROWS - 1 if c_y == 1 else 0)
                to = 0 if c_z == 1 else COLS - 1
                values = jnp.where(
                    first_lane == to,
                    pltpu.roll(corner, (to - at) % COLS, 1)[k : k + 1, :],
                    pltpu.roll(values, 1 if c_z == 1 else COLS - 1, 1),
                )
            cells = walls[t, 0:1, :] if c_y == 1 else walls[t, ROWS - 1 : ROWS, :]
            values = jnp.where(cells > 0.5, wall, values)
            changed = (sub == (0 if c_y == 1 else 7)) & (values != wall)
            y_new[y, t] = jnp.where(changed, values, y_part[y, t])
        at = 0 if c_y == 1 else ROWS - 8
        send(y_new.at[y], out_hbm.at[i, :, at : at + 8])

    middle = {0: chip[...]}
    middle[-1], middle[1] = swap_if(near_in[16:24, :], far_in[16:24, :])
    middle[-2], middle[2] = swap_if(near_2[...], far_in[24:32, :])
    arrived = []
    for ref, start in ((outer_in, EDGE_ROWS + 16), (inner_in, 0)):
        group = [ref[start + 8 * k : start + 8 * k + 8, :] for k in range(5)]
        columns = {0: group[0]}
        columns[-1], columns[1] = swap_if(group[3], group[1])
        columns[-2], columns[2] = swap_if(group[4], group[2])
        arrived.append(columns)
    tiles = {}
    low = lane < HALF
    for b in range(-2, 3):
        before, after = swap_if(arrived[0][b], arrived[1][b])
        turned_before, turned_own, turned_after = (
            pltpu.roll(part, HALF, 1) for part in (before, middle[b], after)
        )
        tiles[0, b] = jnp.where(second, jnp.where(low, turned_before, turned_own), before)
        tiles[1, b] = jnp.where(second, jnp.where(low, turned_own, turned_after), middle[b])
        tiles[2, b] = jnp.where(second, turned_after, after)

    number = lax.shift_right_logical(lane, 2)
    number_a = sum((number >= 3 * k).astype(jnp.int32) for k in (1, 2, 3)) - 1
    number_b = number - 3 * (number_a + 1) - 1
    listed = lane < 9 * SLOTS
    near_a = {a: listed & (number_a >= a - 1) & (number_a <= a + 1) for a in range(-2, 3)}
    near_b = {b: (number_b >= b - 1) & (number_b <= b + 1) for b in range(-2, 3)}

    def device_lanes(a, b, shift):
        shift = (shift - HALF * (a % 2)) % COLS
        part = tiles[(a + 2) // 2, b]
        return pltpu.roll(part, shift, 1) if shift else part

    force = jnp.zeros((8, COLS), jnp.float32)
    for a in range(-2, 3):
        for b in range(-2, 3):
            part = device_lanes(a, b, SLOTS * (3 * a + b))
            force = force + jnp.where(near_a[a] & near_b[b], part, 0.0)
    record = jnp.zeros((8, COLS), jnp.float32)
    target = jnp.full((8, COLS), -1.0, jnp.float32)
    for a in (-1, 0, 1):
        for b in (-1, 0, 1):
            n = 3 * (a + 1) + b + 1
            record = jnp.where(number == n, device_lanes(a, b, SLOTS * n - STATE_LANE), record)
            target = jnp.where(number == n, device_lanes(a, b, SLOTS * n - DEST_LANE), target)
    mass = record[6:7, :] * (3.0 / (4.0 * math.pi * RADIUS * RADIUS * RADIUS))
    spin = mass * record[7:8, :] * (1.0 / (RADIUS * RADIUS))
    gain = jnp.where(sub < 3, force * mass, jnp.where(sub < 6, force * spin, 0.0))
    updated = record + gain
    picked = [
        jnp.where(listed & (target[0:1, :] == meta[0:1, :] + float(j)), updated, 0.0)
        for j in range(SLOTS)
    ]
    result = jnp.zeros((8, COLS), jnp.float32)
    for j in range(SLOTS):
        result = jnp.where(lane == j, jnp.sum(picked[j], axis=1, keepdims=True), result)
    turn[0:8, :] = result
    turn[8:16, :] = force
    turned = turn[...].T
    state_next[...] = turned[0:SLOTS, 0:8]
    forces[...] = turned[4 * SLOTS : 5 * SLOTS, 8:14]
    send(state_next, state_hbm)
    send(forces, forces_hbm)
    for copy in copies:
        copy.wait()


VMEM = pl.BlockSpec(memory_space=pltpu.VMEM)
HBM = pl.BlockSpec(memory_space=pltpu.HBM)


def f32(*shape):
    return jax.ShapeDtypeStruct(shape, jnp.float32)


def in_hbm(array):
    return pltpu.with_memory_space_constraint(array, pltpu.HBM)


def swapped(block, distance):
    count = lax.axis_size("gy")
    route = [(p, (p + (distance if p % 2 == 0 else -distance)) % count) for p in range(count)]
    return lax.ppermute(block, "gy", route)


def spread(block, distance):
    count_y, count_z = lax.axis_size("gy"), lax.axis_size("gz")
    route = []
    for p in range(count_y):
        step = distance if p % 2 == 0 else -distance
        route += [(p * count_z + q, p * count_z + (q + step) % count_z) for q in range(count_z)]
    return lax.ppermute(block, ("gy", "gz"), route)


def on_device(populations, solid_mask, centers, tile_lists, sphere_state, destination, relax_rates):
    held, walls, keep, give, info, inner, outer, border, meta = pl.pallas_call(
        collide_kernel,
        out_shape=(
            f32(19, GROUPS, 8, COLS),
            f32(GROUPS, 8, COLS),
            f32(8, COLS),
            f32(8, COLS),
            f32(8, COLS),
            f32(EDGE_ROWS, COLS),
            f32(EDGE_ROWS, COLS),
            f32(16, COLS),
            f32(8, COLS),
        ),
        in_specs=[HBM] * 7,
        out_specs=(VMEM,) * 9,
        scratch_shapes=[
            pltpu.VMEM((19, GROUPS, 8, COLS), jnp.float32),
            pltpu.VMEM((GROUPS, 8, COLS), jnp.int32),
            pltpu.SMEM((SLOTS, 8), jnp.float32),
            pltpu.SMEM((3, SLOTS), jnp.int32),
            pltpu.SMEM((4, 16), jnp.int32),
            pltpu.SMEM((SLOTS,), jnp.int32),
            pltpu.SMEM((19,), jnp.float32),
            pltpu.VMEM((19, GROUPS, 8, COLS), jnp.float32),
            pltpu.VMEM((N_COEF, 8, COLS), jnp.float32),
            pltpu.VMEM((COLS, COLS), jnp.float32),
            pltpu.VMEM((20, 8, COLS), jnp.float32),
            pltpu.SemaphoreType.DMA((10,)),
        ],
        compiler_params=pltpu.CompilerParams(vmem_limit_bytes=32 * 1024 * 1024),
        name="collide",
    )(
        in_hbm(populations.reshape(19, GROUPS, 8, COLS)),
        in_hbm(solid_mask.reshape(GROUPS, 8, COLS)),
        in_hbm(sphere_state.T),
        in_hbm(centers),
        in_hbm(tile_lists.T),
        in_hbm(destination),
        in_hbm(relax_rates),
    )
    partner = swapped(jnp.concatenate([give, info, inner]), 1)
    chip = info + partner[8:16]
    load = jnp.concatenate([keep, partner[0:8], chip])
    near = spread(load, 1)
    near_2 = spread(load, 2)[16:24]
    far = swapped(jnp.concatenate([near, near_2]), 1)
    spheres = [chip, near[16:24], near_2, far[16:32]]
    from_outer = swapped(jnp.concatenate([outer, near[0:8], far[8:16]] + spheres), -1)
    from_inner = swapped(jnp.concatenate(spheres), 3)
    walls = walls.reshape(PLANES, ROWS, COLS)
    streamed, y_part = pl.pallas_call(
        stream_kernel,
        out_shape=(f32(19, PLANES, ROWS, COLS), f32(10, PLANES, 8, COLS)),
        in_specs=[VMEM] * 6,
        out_specs=(HBM, VMEM),
        scratch_shapes=[
            pltpu.VMEM((19, PLANES, ROWS + 16, COLS), jnp.float32),
            pltpu.VMEM((COLS, COLS), jnp.float32),
            pltpu.VMEM((19, PLANES, ROWS, COLS), jnp.float32),
            pltpu.SemaphoreType.DMA((PLANES,)),
        ],
        compiler_params=pltpu.CompilerParams(vmem_limit_bytes=32 * 1024 * 1024),
        cost_estimate=pl.CostEstimate(flops=4_000_000, bytes_accessed=4_000_000, transcendentals=0),
        name="stream",
    )(held.reshape(19, PLANES, ROWS, COLS), walls, border, meta, near, far)
    populations_next, forces, state_next = pl.pallas_call(
        update_kernel,
        out_shape=(f32(19, PLANES, ROWS, COLS), f32(SLOTS, 6), f32(SLOTS, 8)),
        in_specs=[HBM] + [VMEM] * 10,
        out_specs=(HBM, HBM, HBM),
        scratch_shapes=[
            pltpu.VMEM((COLS, COLS), jnp.float32),
            pltpu.VMEM((10, PLANES, 8, COLS), jnp.float32),
            pltpu.VMEM((SLOTS, 6), jnp.float32),
            pltpu.VMEM((SLOTS, 8), jnp.float32),
            pltpu.SemaphoreType.DMA((12,)),
        ],
        input_output_aliases={0: 0},
        compiler_params=pltpu.CompilerParams(vmem_limit_bytes=32 * 1024 * 1024),
        name="update",
    )(
        in_hbm(streamed),
        y_part,
        walls,
        meta,
        chip,
        partner[16:40],
        near,
        near_2,
        far,
        from_outer,
        from_inner,
    )
    return populations_next, forces.T, state_next.T


def solution(mesh):
    return jax.shard_map(
        on_device,
        mesh=mesh,
        in_specs=(
            P(None, None, "gy", "gz"),
            P(None, "gy", "gz"),
            P(None, ("gy", "gz")),
            P(("gy", "gz"), None),
            P(None, ("gy", "gz")),
            P(("gy", "gz")),
            P(),
        ),
        out_specs=(P(None, None, "gy", "gz"), P(None, ("gy", "gz")), P(None, ("gy", "gz"))),
        check_vma=False,
    )
```

```python
import math

import jax
import jax.numpy as jnp
import numpy as np
from jax import lax
from jax.experimental import pallas as pl
from jax.experimental.pallas import tpu as pltpu
from jax.sharding import PartitionSpec as P

TILE = 16
RADIUS = 6
PLANES = 4
ROWS = 32
COLS = 128
SLOTS = 4
GROUPS = PLANES * ROWS // 8

VELOCITIES = (
    (0, 0, 0),
    (1, 0, 0),
    (-1, 0, 0),
    (0, 1, 0),
    (0, -1, 0),
    (0, 0, 1),
    (0, 0, -1),
    (1, 1, 0),
    (-1, -1, 0),
    (1, -1, 0),
    (-1, 1, 0),
    (1, 0, 1),
    (-1, 0, -1),
    (1, 0, -1),
    (-1, 0, 1),
    (0, 1, 1),
    (0, -1, -1),
    (0, 1, -1),
    (0, -1, 1),
)
OPPOSITE = (0, 2, 1, 4, 3, 6, 5, 8, 7, 10, 9, 12, 11, 14, 13, 16, 15, 18, 17)
EXPONENTS = (
    (0, 0, 0),
    (1, 0, 0),
    (0, 1, 0),
    (0, 0, 1),
    (2, 0, 0),
    (0, 2, 0),
    (0, 0, 2),
    (1, 1, 0),
    (1, 0, 1),
    (0, 1, 1),
    (1, 2, 0),
    (1, 0, 2),
    (2, 1, 0),
    (0, 1, 2),
    (2, 0, 1),
    (0, 2, 1),
    (2, 2, 0),
    (2, 0, 2),
    (0, 2, 2),
)
DIRECTIONS = ((-1, -1), (-1, 0), (-1, 1), (0, -1), (0, 1), (1, -1), (1, 0), (1, 1))

Z_UP = (5, 11, 14, 15, 18)
Z_DOWN = (6, 12, 13, 16, 17)
Y_UP = (3, 7, 10, 15, 17)
Y_DOWN = (4, 8, 9, 16, 18)
CLASS_MEMBER = (0, 1, 3, 5, 7, 11, 15)
EVEN_MOMENTS = (0, 4, 5, 6, 16, 17, 18)
ODD_MOMENTS = ((1, 10, 11), (2, 12, 13), (3, 14, 15))
ODD_CLASSES = ((1, 4, 5), (2, 4, 6), (3, 5, 6))
CROSS_MOMENTS = (7, 8, 9)
STATE_LANE = 40
DEST_LANE = 48
HALF = 64
EDGE_ROWS = 24


def moment_basis():
    velocity = np.array(VELOCITIES, dtype=np.float64)
    moment_rows = []
    for a, b, e in EXPONENTS:
        vector = velocity[:, 0] ** a * velocity[:, 1] ** b * velocity[:, 2] ** e
        for earlier in moment_rows:
            vector = vector - np.dot(earlier, vector) * earlier
        moment_rows.append(vector / np.sqrt(np.dot(vector, vector)))
    return np.array(moment_rows)


BASIS = moment_basis()


def store_coefficients(rates, coef):
    splat = [jnp.full((8, COLS), rates[k], jnp.float32) for k in range(19)]
    at = 0
    for a in range(7):
        for b in range(a, 7):
            total = None
            for k in EVEN_MOMENTS:
                c = float(BASIS[k, CLASS_MEMBER[a]] * BASIS[k, CLASS_MEMBER[b]])
                if abs(c) > 1e-12:
                    total = c * splat[k] if total is None else total + c * splat[k]
            coef[at] = total
            at += 1
    for axis in range(3):
        for a in range(3):
            for b in range(a, 3):
                total = None
                for k in ODD_MOMENTS[axis]:
                    c = float(
                        BASIS[k, CLASS_MEMBER[ODD_CLASSES[axis][a]]]
                        * BASIS[k, CLASS_MEMBER[ODD_CLASSES[axis][b]]]
                    )
                    if abs(c) > 1e-12:
                        total = c * splat[k] if total is None else total + c * splat[k]
                coef[at] = total
                at += 1
    for axis in range(3):
        c = float(BASIS[CROSS_MOMENTS[axis], CLASS_MEMBER[4 + axis]] ** 2)
        coef[at] = c * splat[CROSS_MOMENTS[axis]]
        at += 1


N_COEF = 28 + 18 + 3


def collide(f, coef):
    even_at = {}
    at = 0
    for a in range(7):
        for b in range(a, 7):
            even_at[a, b] = even_at[b, a] = at
            at += 1
    odd_at = []
    for _ in range(3):
        table = {}
        for a in range(3):
            for b in range(a, 3):
                table[a, b] = table[b, a] = at
                at += 1
        odd_at.append(table)
    cross_at = at

    def split(i):
        ab, amb = f[i] + f[i + 1], f[i] - f[i + 1]
        cd, cmd = f[i + 2] + f[i + 3], f[i + 2] - f[i + 3]
        return ab + cd, ab - cd, amb + cmd, amb - cmd

    s_xy, q_xy, xy_x, xy_y = split(7)
    s_xz, q_xz, xz_x, xz_z = split(11)
    s_yz, q_yz, yz_y, yz_z = split(15)
    s_x, s_y, s_z = f[1] + f[2], f[3] + f[4], f[5] + f[6]
    d_x, d_y, d_z = f[1] - f[2], f[3] - f[4], f[5] - f[6]
    rho = ((f[0] + s_x) + (s_y + s_z)) + ((s_xy + s_xz) + s_yz)
    j_x = d_x + (xy_x + xz_x)
    j_y = d_y + (xy_y + yz_y)
    j_z = d_z + (xz_z + yz_z)
    inverse = 1.0 / rho
    u_x, u_y, u_z = j_x * inverse, j_y * inverse, j_z * inverse
    e_x, e_y, e_z = j_x * u_x, j_y * u_y, j_z * u_z
    base = (rho - 1.5 * ((e_x + e_y) + e_z)) * (1.0 / 9.0)
    h_x, h_y, h_z = 0.5 * e_x, 0.5 * e_y, 0.5 * e_z
    even = (
        f[0] - 3.0 * base,
        s_x - (base + h_x),
        s_y - (base + h_y),
        s_z - (base + h_z),
        s_xy - (base + (h_x + h_y)),
        s_xz - (base + (h_x + h_z)),
        s_yz - (base + (h_y + h_z)),
    )
    third = 1.0 / 3.0
    t_x, t_y, t_z = third * j_x, third * j_y, third * j_z
    odd = (
        (d_x - t_x, xy_x - t_x, xz_x - t_x),
        (d_y - t_y, xy_y - t_y, yz_y - t_y),
        (d_z - t_z, xz_z - t_z, yz_z - t_z),
    )
    cross = (
        (q_xy - j_x * u_y) * coef[cross_at],
        (q_xz - j_x * u_z) * coef[cross_at + 1],
        (q_yz - j_y * u_z) * coef[cross_at + 2],
    )

    def apply(vector, table, n):
        out = []
        for a in range(n):
            terms = [coef[table[a, b]] * vector[b] for b in range(n)]
            while len(terms) > 1:
                terms = [
                    terms[i] + terms[i + 1] if i + 1 < len(terms) else terms[i]
                    for i in range(0, len(terms), 2)
                ]
            out.append(terms[0])
        return out

    ev = apply(even, even_at, 7)
    ox, oy, oz = (apply(odd[axis], odd_at[axis], 3) for axis in range(3))
    new = [f[0] - ev[0]]
    for axis, o in enumerate((ox, oy, oz)):
        i = 1 + 2 * axis
        new += [f[i] - (ev[1 + axis] + o[0]), f[i + 1] - (ev[1 + axis] - o[0])]
    for axis, (a, b) in enumerate(((ox[1], oy[1]), (ox[2], oz[1]), (oy[2], oz[2]))):
        i = 7 + 4 * axis
        plus, minus = ev[4 + axis] + cross[axis], ev[4 + axis] - cross[axis]
        both, differ = a + b, a - b
        new += [
            f[i] - (plus + both),
            f[i + 1] - (plus - both),
            f[i + 2] - (minus + differ),
            f[i + 3] - (minus - differ),
        ]
    return new


def sphere_partial(coll, partial, at, center_x, center_y, center_z, row_f, lane_f):
    first = jnp.maximum(lax.shift_right_arithmetic(center_y - (RADIUS + 1), 3), 0)
    last = jnp.minimum(lax.shift_right_arithmetic(center_y + (RADIUS + 1), 3), ROWS // 8 - 1)
    x_f = center_x.astype(jnp.float32)
    r_z = lane_f - center_z.astype(jnp.float32)
    z_sq = r_z * r_z
    zero = jnp.zeros((8, COLS), jnp.float32)

    def row_tile(tile, carry):
        f_x, f_y, f_z, t_x, t_y, t_z = carry
        r_y = row_f + (tile * 8 - center_y).astype(jnp.float32)
        yz_sq = r_y * r_y + z_sq
        p_x, p_y, p_z, x_py, x_pz = zero, zero, zero, zero, zero
        y_plus_z, y_minus_z = r_y + r_z, r_y - r_z
        for t in range(PLANES):
            r_x = t - x_f
            dist = yz_sq + r_x * r_x
            outside = dist > float(RADIUS * RADIUS)
            half = jnp.where(outside, (RADIUS * RADIUS - 1.0) * 0.5 - 0.5 * dist, -1e9)
            half_2 = half - 0.5
            limits = {1: (half, -half), 2: (half_2, -half_2)}

            def linked(i, along, kind):
                limit, negative = limits[kind]
                up, down = VELOCITIES[i][0], VELOCITIES[i + 1][0]
                total = None
                if 0 <= t + up < PLANES:
                    total = jnp.where(along <= limit, coll[i, t * 4 + tile], 0.0)
                if 0 <= t + down < PLANES:
                    back = jnp.where(along >= negative, coll[i + 1, t * 4 + tile], 0.0)
                    total = -back if total is None else total - back
                return total

            l_x = linked(1, r_x, 1)
            l_y = linked(3, r_y, 1)
            l_z = linked(5, r_z, 1)
            l_xy = linked(7, r_y + r_x, 2)
            l_xmy = linked(9, r_x - r_y, 2)
            l_xz = linked(11, r_z + r_x, 2)
            l_xmz = linked(13, r_x - r_z, 2)
            l_yz = linked(15, y_plus_z, 2)
            l_ymz = linked(17, y_minus_z, 2)
            m_x = l_x + ((l_xy + l_xmy) + (l_xz + l_xmz))
            m_y = l_y + ((l_xy - l_xmy) + (l_yz + l_ymz))
            m_z = l_z + ((l_xz - l_xmz) + (l_yz - l_ymz))
            p_x, p_y, p_z = p_x + m_x, p_y + m_y, p_z + m_z
            x_py, x_pz = x_py + r_x * m_y, x_pz + r_x * m_z
        return (
            f_x + p_x,
            f_y + p_y,
            f_z + p_z,
            t_x + (r_y * p_z - r_z * p_y),
            t_y + (r_z * p_x - x_pz),
            t_z + (x_py - r_y * p_x),
        )

    sums = lax.fori_loop(first, last + 1, row_tile, (zero,) * 6)
    packed = zero
    for j in range(6):
        packed = jnp.where(row_f == float(j), jnp.sum(sums[j], axis=0, keepdims=True), packed)
    partial[at] = packed


def collide_kernel(
    pops_in,
    mask_in,
    state_in,
    centers_in,
    lists_in,
    destination_in,
    rates_in,
    held,
    walls,
    keep,
    give,
    info,
    inner,
    outer,
    border,
    meta,
    pops,
    mask,
    state,
    centers,
    lists,
    destination,
    rates,
    coll,
    coef,
    turn,
    partial,
    sems,
):
    small = [
        pltpu.make_async_copy(source, target, sems.at[4 + k])
        for k, (source, target) in enumerate(
            (
                (rates_in, rates),
                (mask_in, mask),
                (centers_in, centers),
                (lists_in, lists),
                (destination_in, destination),
                (state_in, state),
            )
        )
    ]
    large = [
        pltpu.make_async_copy(
            pops_in.at[:, pl.ds(t * 4, 4)], pops.at[:, pl.ds(t * 4, 4)], sems.at[t]
        )
        for t in range(PLANES)
    ]
    small[0].start()
    small[1].start()
    for copy in large:
        copy.start()
    for copy in small[2:]:
        copy.start()
    lane = lax.broadcasted_iota(jnp.int32, (8, COLS), 1)
    lane_f = lane.astype(jnp.float32)
    row_f = lax.broadcasted_iota(jnp.int32, (8, COLS), 0).astype(jnp.float32)
    small[0].wait()
    store_coefficients(rates, coef)
    small[1].wait()

    def group(g, _):
        f = [pops[i, g] for i in range(19)]
        solid = mask[g] > 0
        flag = solid.astype(jnp.float32)
        walls[g] = flag
        new = collide(f, coef)
        for i in range(19):
            coll[i, g] = new[i]
            held[i, g] = jnp.where(solid, f[i], new[i])
        return 0

    for t in range(PLANES):
        large[t].wait()
        lax.fori_loop(t * 4, t * 4 + 4, group, 0, unroll=4)
    for copy in small[2:]:
        copy.wait()

    device_y = lax.shift_right_logical(centers[1, 0], 5)
    device_z = lax.shift_right_logical(centers[2, 0], 7)
    core = device_y & 1
    first = core == 0
    meta[0:1, :] = jnp.full((1, COLS), (device_y * 16 + device_z) * SLOTS, jnp.int32).astype(
        jnp.float32
    )
    meta[1:2, :] = jnp.full((1, COLS), core, jnp.int32).astype(jnp.float32)
    meta[2:8, :] = jnp.zeros((6, COLS), jnp.float32)

    for g in range(GROUPS):
        edge = jnp.zeros((8, COLS), jnp.float32)
        for k in range(6):
            values = walls[g]
            if k < 5:
                values = jnp.where(lane == 0, coll[Z_DOWN[k], g], coll[Z_UP[k], g])
            pair = lax.shift_right_logical(lane, 1) == k
            edge = jnp.where(pair, pltpu.roll(values, 2 * k + 1, 1), edge)
        turn[g * 8 : g * 8 + 8, :] = edge
    turn[...] = turn[...].T
    up_z = turn[pl.ds(0, 8, stride=2), :]
    down_z = turn[pl.ds(1, 8, stride=2), :]
    border[0:8, :] = up_z
    border[8:16, :] = down_z
    keep[...] = jnp.where(first, up_z, down_z)
    give[...] = jnp.where(first, down_z, up_z)
    for t in range(PLANES):
        for d in range(5):
            up = coll[Y_UP[d], t * 4 + 3, 7:8, :]
            down = coll[Y_DOWN[d], t * 4, 0:1, :]
            inner[d * 4 + t : d * 4 + t + 1, :] = jnp.where(first, up, down)
            outer[d * 4 + t : d * 4 + t + 1, :] = jnp.where(first, down, up)
        up = walls[t * 4 + 3, 7:8, :]
        down = walls[t * 4, 0:1, :]
        inner[20 + t : 21 + t, :] = jnp.where(first, up, down)
        outer[20 + t : 21 + t, :] = jnp.where(first, down, up)

    def own(s, _):
        sphere_partial(
            coll,
            partial,
            s,
            centers[0, s],
            centers[1, s] & (ROWS - 1),
            centers[2, s] & (COLS - 1),
            row_f,
            lane_f,
        )
        return 0

    partial[SLOTS:] = jnp.zeros((16, 8, COLS), jnp.float32)
    lax.fori_loop(0, SLOTS, own, 0, unroll=True)

    def listed(r, _):
        @pl.when(lists[0, r] >= 0)
        def _():
            sphere_partial(
                coll,
                partial,
                SLOTS + r,
                lists[3, r],
                lists[1, r] + TILE // 2,
                lists[2, r] + TILE // 2,
                row_f,
                lane_f,
            )

        return 0

    lax.fori_loop(0, 16, listed, 0)

    base = core * HALF
    tile = jnp.zeros((8, COLS), jnp.float32)
    for s in range(SLOTS):
        total = 2.0 * jnp.sum(partial[s], axis=1, keepdims=True)
        tile = jnp.where(lane == base + 4 * SLOTS + s, total, tile)
        column = jnp.zeros((8, COLS), jnp.float32)
        for r in range(8):
            column = jnp.where(row_f == float(r), state[s, r], column)
        tile = jnp.where(lane == base + STATE_LANE + s, column, tile)
        tile = jnp.where(lane == base + DEST_LANE + s, destination[s].astype(jnp.float32), tile)
    for r in range(16):
        offset = DIRECTIONS[r // 2]
        block = (offset[0] + 1) * 3 + offset[1] + 1
        total = 2.0 * jnp.sum(partial[SLOTS + r], axis=1, keepdims=True)
        slot = lists[0, r]
        at = jnp.where(slot >= 0, base + block * SLOTS + slot, -1)
        tile = jnp.where(lane == at, total, tile)
    info[...] = tile


Y_ALL = (3, 4, 7, 8, 9, 10, 15, 16, 17, 18)


def select_by(meta):
    second = jnp.broadcast_to(meta[1:2, :], (8, COLS)) > 0.5

    def swap_if(a, b):
        return jnp.where(second, b, a), jnp.where(second, a, b)

    return second, swap_if


def walled(values):
    return jnp.where(values[5:6, :] > 0.5, jnp.inf, values)


def stream_kernel(
    held, walls, border, meta, near_in, far_in, out_hbm, y_part, ext, turn, out, sems
):
    wall = jnp.inf
    _, swap_if = select_by(meta)
    lane = lax.broadcasted_iota(jnp.int32, (8, COLS), 1)
    sub = lax.broadcasted_iota(jnp.int32, (8, COLS), 0)
    row = lane & (ROWS - 1)
    plane = lax.shift_right_logical(lane, 5)

    def side(here, order):
        total = here
        for k, i in enumerate(order):
            c_x, c_y, _ = VELOCITIES[i]
            moved = here
            if c_y == 1:
                moved = jnp.where(row == 0, wall, pltpu.roll(here, 1, 1))
            if c_y == -1:
                moved = jnp.where(row == ROWS - 1, wall, pltpu.roll(here, COLS - 1, 1))
            if c_x == 1:
                moved = jnp.where(plane == 0, wall, pltpu.roll(here, 32, 1))
            if c_x == -1:
                moved = jnp.where(plane == PLANES - 1, wall, pltpu.roll(here, COLS - 32, 1))
            total = jnp.where(sub == k, moved, total)
        return total

    west, east = swap_if(walled(near_in[0:8, :]), walled(far_in[8:16, :]))
    turn[...] = jnp.zeros((COLS, COLS), jnp.float32)
    turn[0:8, :] = side(west, Z_UP)
    turn[8:16, :] = side(east, Z_DOWN)
    turned = turn[...].T
    turn[...] = turned
    column = lax.broadcasted_iota(jnp.int32, (ROWS, COLS), 1)
    for t in range(PLANES):
        solid = walls[t] > 0.5
        for i in range(19):
            ext[i, t, 8 : 8 + ROWS, :] = jnp.where(solid, wall, held[i, t])
            c_y = VELOCITIES[i][1]
            if c_y == 1:
                ext[i, t, 7:8, :] = jnp.full((1, COLS), wall, jnp.float32)
            if c_y == -1:
                ext[i, t, 8 + ROWS : 9 + ROWS, :] = jnp.full((1, COLS), wall, jnp.float32)
    copies = []
    for t in range(PLANES):
        solid = walls[t] > 0.5
        for i in range(19):
            c_x, c_y, c_z = VELOCITIES[i]
            source = t - c_x
            if 0 <= source < PLANES:
                pulled = ext[i, source, 8 - c_y : 8 - c_y + ROWS, :]
                if c_z != 0:
                    k = Z_UP.index(i) if c_z == 1 else 8 + Z_DOWN.index(i)
                    pulled = jnp.where(
                        column == (0 if c_z == 1 else COLS - 1),
                        turn[t * ROWS : (t + 1) * ROWS, k : k + 1],
                        pltpu.roll(pulled, 1 if c_z == 1 else COLS - 1, 1),
                    )
                fluid = jnp.where(pulled == wall, held[OPPOSITE[i], t], pulled)
            else:
                fluid = held[OPPOSITE[i], t]
            result = jnp.where(solid, held[i, t], fluid)
            out[i, t] = result
            if i in Y_ALL:
                y_part[Y_ALL.index(i), t] = result[0:8] if c_y == 1 else result[ROWS - 8 : ROWS]
        copies.append(pltpu.make_async_copy(out.at[:, t], out_hbm.at[:, t], sems.at[t]))
        copies[t].start()
    for copy in copies:
        copy.wait()


def update_kernel(
    streamed,
    y_part,
    walls,
    meta,
    chip,
    partner_edge,
    near_in,
    near_2,
    far_in,
    outer_in,
    inner_in,
    out_hbm,
    forces_hbm,
    state_hbm,
    turn,
    y_new,
    forces,
    state_next,
    sems,
):
    del streamed
    lane = lax.broadcasted_iota(jnp.int32, (8, COLS), 1)
    sub = lax.broadcasted_iota(jnp.int32, (8, COLS), 0)
    wall = jnp.inf
    second, swap_if = select_by(meta)
    west_partner, east_partner = swap_if(walled(near_in[8:16, :]), walled(far_in[0:8, :]))
    west_outer, east_outer = swap_if(
        walled(outer_in[EDGE_ROWS + 8 : EDGE_ROWS + 16, :]), walled(outer_in[EDGE_ROWS : EDGE_ROWS + 8, :])
    )
    west_south, west_north = swap_if(west_outer, west_partner)
    east_south, east_north = swap_if(east_outer, east_partner)
    pairs = [
        swap_if(outer_in[k : k + 8, :], partner_edge[k : k + 8, :]) for k in range(0, EDGE_ROWS, 8)
    ]
    south = [p[0] for p in pairs]
    north = [p[1] for p in pairs]

    def edge_row(edge, r):
        return edge[r // 8][r % 8 : r % 8 + 1, :]

    first_lane = lax.broadcasted_iota(jnp.int32, (1, COLS), 1)
    copies = []

    def send(source, target):
        copies.append(pltpu.make_async_copy(source, target, sems.at[len(copies)]))
        copies[-1].start()

    for y, i in enumerate(Y_ALL):
        c_x, c_y, c_z = VELOCITIES[i]
        edge, order = (south, Y_UP) if c_y == 1 else (north, Y_DOWN)
        for t in range(PLANES):
            source = t - c_x
            if not 0 <= source < PLANES:
                y_new[y, t] = y_part[y, t]
                continue
            values = edge_row(edge, order.index(i) * 4 + source)
            values = jnp.where(edge_row(edge, 20 + source) > 0.5, wall, values)
            if c_z != 0:
                if c_z == 1:
                    corner, k = (west_south if c_y == 1 else west_north), Z_UP.index(i)
                else:
                    corner, k = (east_south if c_y == 1 else east_north), Z_DOWN.index(i)
                at = t * ROWS + (ROWS - 1 if c_y == 1 else 0)
                to = 0 if c_z == 1 else COLS - 1
                values = jnp.where(
                    first_lane == to,
                    pltpu.roll(corner, (to - at) % COLS, 1)[k : k + 1, :],
                    pltpu.roll(values, 1 if c_z == 1 else COLS - 1, 1),
                )
            cells = walls[t, 0:1, :] if c_y == 1 else walls[t, ROWS - 1 : ROWS, :]
            values = jnp.where(cells > 0.5, wall, values)
            changed = (sub == (0 if c_y == 1 else 7)) & (values != wall)
            y_new[y, t] = jnp.where(changed, values, y_part[y, t])
        at = 0 if c_y == 1 else ROWS - 8
        send(y_new.at[y], out_hbm.at[i, :, at : at + 8])

    middle = {0: chip[...]}
    middle[-1], middle[1] = swap_if(near_in[16:24, :], far_in[16:24, :])
    middle[-2], middle[2] = swap_if(near_2[...], far_in[24:32, :])
    arrived = []
    for ref, start in ((outer_in, EDGE_ROWS + 16), (inner_in, 0)):
        group = [ref[start + 8 * k : start + 8 * k + 8, :] for k in range(5)]
        columns = {0: group[0]}
        columns[-1], columns[1] = swap_if(group[3], group[1])
        columns[-2], columns[2] = swap_if(group[4], group[2])
        arrived.append(columns)
    tiles = {}
    low = lane < HALF
    for b in range(-2, 3):
        before, after = swap_if(arrived[0][b], arrived[1][b])
        turned_before, turned_own, turned_after = (
            pltpu.roll(part, HALF, 1) for part in (before, middle[b], after)
        )
        tiles[0, b] = jnp.where(second, jnp.where(low, turned_before, turned_own), before)
        tiles[1, b] = jnp.where(second, jnp.where(low, turned_own, turned_after), middle[b])
        tiles[2, b] = jnp.where(second, turned_after, after)

    number = lax.shift_right_logical(lane, 2)
    number_a = sum((number >= 3 * k).astype(jnp.int32) for k in (1, 2, 3)) - 1
    number_b = number - 3 * (number_a + 1) - 1
    listed = lane < 9 * SLOTS
    near_a = {a: listed & (number_a >= a - 1) & (number_a <= a + 1) for a in range(-2, 3)}
    near_b = {b: (number_b >= b - 1) & (number_b <= b + 1) for b in range(-2, 3)}

    def device_lanes(a, b, shift):
        shift = (shift - HALF * (a % 2)) % COLS
        part = tiles[(a + 2) // 2, b]
        return pltpu.roll(part, shift, 1) if shift else part

    force = jnp.zeros((8, COLS), jnp.float32)
    for a in range(-2, 3):
        for b in range(-2, 3):
            part = device_lanes(a, b, SLOTS * (3 * a + b))
            force = force + jnp.where(near_a[a] & near_b[b], part, 0.0)
    record = jnp.zeros((8, COLS), jnp.float32)
    target = jnp.full((8, COLS), -1.0, jnp.float32)
    for a in (-1, 0, 1):
        for b in (-1, 0, 1):
            n = 3 * (a + 1) + b + 1
            record = jnp.where(number == n, device_lanes(a, b, SLOTS * n - STATE_LANE), record)
            target = jnp.where(number == n, device_lanes(a, b, SLOTS * n - DEST_LANE), target)
    mass = record[6:7, :] * (3.0 / (4.0 * math.pi * RADIUS * RADIUS * RADIUS))
    spin = mass * record[7:8, :] * (1.0 / (RADIUS * RADIUS))
    gain = jnp.where(sub < 3, force * mass, jnp.where(sub < 6, force * spin, 0.0))
    updated = record + gain
    picked = [
        jnp.where(listed & (target[0:1, :] == meta[0:1, :] + float(j)), updated, 0.0)
        for j in range(SLOTS)
    ]
    result = jnp.zeros((8, COLS), jnp.float32)
    for j in range(SLOTS):
        result = jnp.where(lane == j, jnp.sum(picked[j], axis=1, keepdims=True), result)
    turn[0:8, :] = result
    turn[8:16, :] = force
    turned = turn[...].T
    state_next[...] = turned[0:SLOTS, 0:8]
    forces[...] = turned[4 * SLOTS : 5 * SLOTS, 8:14]
    send(state_next, state_hbm)
    send(forces, forces_hbm)
    for copy in copies:
        copy.wait()


VMEM = pl.BlockSpec(memory_space=pltpu.VMEM)
HBM = pl.BlockSpec(memory_space=pltpu.HBM)


def f32(*shape):
    return jax.ShapeDtypeStruct(shape, jnp.float32)


def in_hbm(array):
    return pltpu.with_memory_space_constraint(array, pltpu.HBM)


def swapped(block, distance):
    count = lax.axis_size("gy")
    route = [(p, (p + (distance if p % 2 == 0 else -distance)) % count) for p in range(count)]
    return lax.ppermute(block, "gy", route)


def spread(block, distance):
    count_y, count_z = lax.axis_size("gy"), lax.axis_size("gz")
    route = []
    for p in range(count_y):
        step = distance if p % 2 == 0 else -distance
        route += [(p * count_z + q, p * count_z + (q + step) % count_z) for q in range(count_z)]
    return lax.ppermute(block, ("gy", "gz"), route)


def on_device(populations, solid_mask, centers, tile_lists, sphere_state, destination, relax_rates):
    held, walls, keep, give, info, inner, outer, border, meta = pl.pallas_call(
        collide_kernel,
        out_shape=(
            f32(19, GROUPS, 8, COLS),
            f32(GROUPS, 8, COLS),
            f32(8, COLS),
            f32(8, COLS),
            f32(8, COLS),
            f32(EDGE_ROWS, COLS),
            f32(EDGE_ROWS, COLS),
            f32(16, COLS),
            f32(8, COLS),
        ),
        in_specs=[HBM] * 7,
        out_specs=(VMEM,) * 9,
        scratch_shapes=[
            pltpu.VMEM((19, GROUPS, 8, COLS), jnp.float32),
            pltpu.VMEM((GROUPS, 8, COLS), jnp.int32),
            pltpu.SMEM((SLOTS, 8), jnp.float32),
            pltpu.SMEM((3, SLOTS), jnp.int32),
            pltpu.SMEM((4, 16), jnp.int32),
            pltpu.SMEM((SLOTS,), jnp.int32),
            pltpu.SMEM((19,), jnp.float32),
            pltpu.VMEM((19, GROUPS, 8, COLS), jnp.float32),
            pltpu.VMEM((N_COEF, 8, COLS), jnp.float32),
            pltpu.VMEM((COLS, COLS), jnp.float32),
            pltpu.VMEM((20, 8, COLS), jnp.float32),
            pltpu.SemaphoreType.DMA((10,)),
        ],
        compiler_params=pltpu.CompilerParams(vmem_limit_bytes=32 * 1024 * 1024),
        name="collide",
    )(
        in_hbm(populations.reshape(19, GROUPS, 8, COLS)),
        in_hbm(solid_mask.reshape(GROUPS, 8, COLS)),
        in_hbm(sphere_state.T),
        in_hbm(centers),
        in_hbm(tile_lists.T),
        in_hbm(destination),
        in_hbm(relax_rates),
    )
    partner = swapped(jnp.concatenate([give, info, inner]), 1)
    chip = info + partner[8:16]
    load = jnp.concatenate([keep, partner[0:8], chip])
    near = spread(load, 1)
    near_2 = spread(load[8:24], 2)[8:16]
    far = swapped(jnp.concatenate([near, near_2]), 1)
    spheres = [chip, near[16:24], near_2, far[16:32]]
    from_outer = swapped(jnp.concatenate([outer, near[0:8], far[8:16]] + spheres), -1)
    from_inner = swapped(jnp.concatenate(spheres), 3)
    walls = walls.reshape(PLANES, ROWS, COLS)
    streamed, y_part = pl.pallas_call(
        stream_kernel,
        out_shape=(f32(19, PLANES, ROWS, COLS), f32(10, PLANES, 8, COLS)),
        in_specs=[VMEM] * 6,
        out_specs=(HBM, VMEM),
        scratch_shapes=[
            pltpu.VMEM((19, PLANES, ROWS + 16, COLS), jnp.float32),
            pltpu.VMEM((COLS, COLS), jnp.float32),
            pltpu.VMEM((19, PLANES, ROWS, COLS), jnp.float32),
            pltpu.SemaphoreType.DMA((PLANES,)),
        ],
        compiler_params=pltpu.CompilerParams(vmem_limit_bytes=32 * 1024 * 1024),
        cost_estimate=pl.CostEstimate(flops=4_000_000, bytes_accessed=4_000_000, transcendentals=0),
        name="stream",
    )(held.reshape(19, PLANES, ROWS, COLS), walls, border, meta, near, far)
    populations_next, forces, state_next = pl.pallas_call(
        update_kernel,
        out_shape=(f32(19, PLANES, ROWS, COLS), f32(SLOTS, 6), f32(SLOTS, 8)),
        in_specs=[HBM] + [VMEM] * 10,
        out_specs=(HBM, HBM, HBM),
        scratch_shapes=[
            pltpu.VMEM((COLS, COLS), jnp.float32),
            pltpu.VMEM((10, PLANES, 8, COLS), jnp.float32),
            pltpu.VMEM((SLOTS, 6), jnp.float32),
            pltpu.VMEM((SLOTS, 8), jnp.float32),
            pltpu.SemaphoreType.DMA((12,)),
        ],
        input_output_aliases={0: 0},
        compiler_params=pltpu.CompilerParams(vmem_limit_bytes=32 * 1024 * 1024),
        name="update",
    )(
        in_hbm(streamed),
        y_part,
        walls,
        meta,
        chip,
        partner[16:40],
        near,
        near_2,
        far,
        from_outer,
        from_inner,
    )
    return populations_next, forces.T, state_next.T


def solution(mesh):
    return jax.shard_map(
        on_device,
        mesh=mesh,
        in_specs=(
            P(None, None, "gy", "gz"),
            P(None, "gy", "gz"),
            P(None, ("gy", "gz")),
            P(("gy", "gz"), None),
            P(None, ("gy", "gz")),
            P(("gy", "gz")),
            P(),
        ),
        out_specs=(P(None, None, "gy", "gz"), P(None, ("gy", "gz")), P(None, ("gy", "gz"))),
        check_vma=False,
    )
```
